128 devices in a mesh: ctx: 8 (over z, x_lo), fsdp: 16 (over x_hi, y, core).
Axes of the slice: x: 4 (x_hi: 2, x_lo: 2; x = x_hi * 2 + x_lo), y: 4, z: 4, core: 2. Of those that a mesh axis runs over, the one named last changes fastest.
Arguments:
- tokens: bfloat16 [16, 2048, 576], P('fsdp', 'ctx'), may hold values from -6 to 6
- positions: int32 [16, 2048], P('fsdp'), may hold values from 0 to 2047, as said below
- vectors: bfloat16 [2, 1152], P(None, 'fsdp'), may hold values from 0.5 to 1.5
- w_query: bfloat16 [2, 576, 576], P(None, 'fsdp', 'ctx'), may hold values from -0.25 to 0.25
- w_key: bfloat16 [2, 576, 192], P(None, 'fsdp', 'ctx'), may hold values from -0.25 to 0.25
- w_value: bfloat16 [2, 576, 192], P(None, 'fsdp', 'ctx'), may hold values from -0.25 to 0.25
- w_out: bfloat16 [2, 576, 576], P(None, 'fsdp', 'ctx'), may hold values from -4 to 4
- w_gate: bfloat16 [2, 576, 1536], P(None, 'fsdp', 'ctx'), may hold values from -0.25 to 0.25
- w_up: bfloat16 [2, 576, 1536], P(None, 'fsdp', 'ctx'), may hold values from -0.25 to 0.25
- w_down: bfloat16 [2, 1536, 576], P(None, 'fsdp', 'ctx'), may hold values from -0.3125 to 0.3125
- cotangent: bfloat16 [16, 2048, 576], P('fsdp', 'ctx'), may hold values from -6 to 6
Outputs:
- output: bfloat16 [16, 2048, 576], P('fsdp', 'ctx')
- grad_tokens: float32 [16, 2048, 576], P('fsdp', 'ctx')
- grad_vectors: float32 [2, 1152], P(None, 'fsdp')
- grad_w_query: float32 [2, 576, 576], P(None, 'fsdp', 'ctx')
- grad_w_key: float32 [2, 576, 192], P(None, 'fsdp', 'ctx')
- grad_w_value: float32 [2, 576, 192], P(None, 'fsdp', 'ctx')
- grad_w_out: float32 [2, 576, 576], P(None, 'fsdp', 'ctx')
- grad_w_gate: float32 [2, 576, 1536], P(None, 'fsdp', 'ctx')
- grad_w_up: float32 [2, 576, 1536], P(None, 'fsdp', 'ctx')
- grad_w_down: float32 [2, 1536, 576], P(None, 'fsdp', 'ctx')
The draws below stay inside these ranges and needn't reach their ends.
Inputs may be any that keep to these rules, and one draw needn't show every extreme that they name: In each sequence every position 0 to 2047 appears once. The 256 rows of one index of ctx are two runs of 128 consecutive positions, starting at b * 128 and at 2048 - (b + 1) * 128, with b different on each index.
All inputs are finite; a program needn't handle non-finite values.
Results may differ from the reference program's by a relative error of at most 0.03.
Values may be sent and summed in bfloat16 or wider, within the bound.
No kernel may reach another device: no remote copies, remote signals or barrier semaphores. Data moves between devices by JAX's collectives and lax.ppermute only.
A program may use at most 192 MiB of HBM per device.

```python
import jax
import jax.numpy as jnp
from jax import lax

D = 576
HEADS = 9
KV_HEADS = 3
HEAD_DIM = 64
FF = 1536
LAYERS = 2
SEQ_LEN = 2048
ROWS = 256
BLOCK = 128
SEQS = 16
KVD = 192
NV = 1152


def draw_positions(key, part):
    key = jax.random.fold_in(key, 11)
    pair_count = SEQ_LEN // ROWS
    seq_keys = jax.random.split(key, SEQS)
    pairs = jax.vmap(lambda one_key: jax.random.permutation(one_key, pair_count))(seq_keys)
    inner = jnp.arange(BLOCK, dtype=jnp.int32)
    front = pairs[:, :, None] * BLOCK + inner[None, None, :]
    back = (2 * pair_count - 1 - pairs[:, :, None]) * BLOCK + inner[None, None, :]
    return jnp.concatenate([front, back], -1).reshape(SEQS, SEQ_LEN).astype(jnp.int32)


def draw_vectors(key, part):
    key = jax.random.fold_in(key, 23)
    gains = jax.random.uniform(key, (LAYERS, NV), jnp.float32, 0.6, 1.4)
    return gains.astype(jnp.bfloat16)


def with_spikes(result, own_key, source, target, shards_of, factor):
    owner, partner = [(jnp.arange(result.shape[axis_at]) // (result.shape[axis_at] // shards_of)).reshape([-1 if axis == axis_at else 1 for axis in range(result.ndim)]) for axis_at in (source, target)]
    chosen = jax.random.permutation(own_key, shards_of)[partner]
    strong = (owner == chosen) | (owner == (partner + shards_of // 2) % shards_of)
    return jnp.where(strong, factor * result, result)


def block_levels(key, dims, cuts, low, high):
    def one(position, blocks):
        steps = jax.random.uniform(jax.random.fold_in(jax.random.fold_in(key, 6), position), (blocks,), jnp.float32, low / len(cuts), high / len(cuts))
        return jnp.repeat(jnp.exp(steps), dims[position] // blocks).reshape((-1,) + (1,) * (len(dims) - position - 1))

    factor_of = one(*cuts[0])
    for cut in cuts[1:]:
        factor_of = factor_of * one(*cut)
    return factor_of


def bell_draw(own_key, dims, scale, most, cuts=(), held_as=jnp.bfloat16):
    entries = scale * jax.random.normal(own_key, dims, jnp.float32)
    if cuts:
        entries = entries * block_levels(own_key, dims, cuts, -0.22, 0.18)
    return jnp.clip(entries, -most, most).astype(held_as)


def noise_with(rng, dims, scale, reach, cuts, heavy, held_as=jnp.bfloat16):
    array = scale * jax.random.normal(rng, dims, jnp.float32)
    if cuts:
        array = array * block_levels(rng, dims, cuts, -0.22, 0.18)
    return jnp.clip(with_spikes(array, jax.random.fold_in(rng, 3), *heavy), -reach, reach).astype(held_as)


def setup_inputs(seed: int = 0) -> dict:
    key_list = jax.random.split(jax.random.key(seed), 12)
    tokens = noise_with(key_list[0], (SEQS, SEQ_LEN, D), 1.0, 6.0, ((0, 16), (1, 8)), (0, 2, 16, 2.0))
    positions = draw_positions(jax.random.fold_in(key_list[11], 71), 0)
    vectors = draw_vectors(jax.random.fold_in(key_list[11], 71), 0)
    w_query = bell_draw(key_list[3], (LAYERS, D, D), D ** -0.5, 0.25, ((1, 16), (2, 8)))
    w_key = bell_draw(key_list[4], (LAYERS, D, KVD), D ** -0.5, 0.25, ((1, 16), (2, 8)))
    w_value = bell_draw(key_list[5], (LAYERS, D, KVD), D ** -0.5, 0.25, ((1, 16), (2, 8)))
    w_out = bell_draw(key_list[6], (LAYERS, D, D), (max(1, 8 * D // SEQ_LEN)) ** -0.5, 4.0, ((1, 16), (2, 8)))
    w_gate = bell_draw(key_list[7], (LAYERS, D, FF), D ** -0.5, 0.25, ((1, 16), (2, 8)))
    w_up = bell_draw(key_list[8], (LAYERS, D, FF), D ** -0.5, 0.25, ((1, 16), (2, 8)))
    w_down = bell_draw(key_list[9], (LAYERS, FF, D), (FF // 4) ** -0.5, 0.3125, ((1, 16), (2, 8)))
    cotangent = bell_draw(key_list[10], (SEQS, SEQ_LEN, D), 1.0, 6.0, ((0, 16), (1, 8)))
    return {"tokens": tokens, "positions": positions, "vectors": vectors, "w_query": w_query, "w_key": w_key, "w_value": w_value, "w_out": w_out, "w_gate": w_gate, "w_up": w_up, "w_down": w_down, "cotangent": cotangent}


rope_base = 10000.0
norm_eps = 1e-05
masked_score = -1e+30
highest = lax.Precision.HIGHEST

@jax.custom_vjp
def low(v):
    return lax.optimization_barrier(v.astype(jnp.bfloat16)).astype(jnp.float32)

@jax.custom_vjp
def low_back(v):
    return v

def low_keep(v):
    return (low(v), None)

def low_pass(kept, grad):
    return (grad,)

def back_keep(v):
    return (v, None)

def back_low(kept, grad):
    return (low(grad),)
low.defvjp(low_keep, low_pass)
low_back.defvjp(back_keep, back_low)

def matmul(left, right):
    return jnp.dot(left, right, precision=highest)

def rms_norm(stream, gain):
    return stream * lax.rsqrt(lax.optimization_barrier(jnp.mean(stream * stream, -1, keepdims=True)) + norm_eps) * gain

def angles(places):
    half_dim = HEAD_DIM // 2
    inverse = rope_base ** (-2.0 * jnp.arange(half_dim).astype(jnp.float32) / HEAD_DIM)
    turned = places.astype(jnp.float32)[:, None] * inverse[None, :]
    return (jnp.cos(turned)[:, None, :], jnp.sin(turned)[:, None, :])

def rotate(values, cosine, sine_part):
    half_dim = values.shape[-1] // 2
    first_half = values[..., :half_dim]
    second = values[..., half_dim:]
    return jnp.concatenate([first_half * cosine - second * sine_part, second * cosine + first_half * sine_part], -1)

def sequence_layer(stream, places, params):
    vector_row, query_weight, key_weight, value_weight, out_weight, gate_weight, up_weight, down_weight = params
    attn_gain = vector_row[:D]
    mlp_gain = vector_row[D:]
    length = stream.shape[0]
    group_size = HEADS // KV_HEADS
    score_scale = HEAD_DIM ** (-0.5)
    cosine, sine_part = angles(places)
    normed = low(rms_norm(stream, attn_gain))
    query_rot = low(rotate(low_back(matmul(normed, query_weight)).reshape(length, HEADS, HEAD_DIM), cosine, sine_part))
    key_rot = low(rotate(low_back(matmul(normed, key_weight)).reshape(length, KV_HEADS, HEAD_DIM), cosine, sine_part))
    values = low(low_back(matmul(normed, value_weight))).reshape(length, KV_HEADS, HEAD_DIM)
    grouped = query_rot.reshape(length, KV_HEADS, group_size, HEAD_DIM)
    scores = low_back(jnp.einsum('rkgd,lkd->kgrl', grouped, key_rot, precision=highest) * score_scale)
    visible = places[None, :] <= places[:, None]
    scores = jnp.where(visible, scores, masked_score)
    row_max = lax.optimization_barrier(jnp.max(scores, -1, keepdims=True))
    raised = jnp.exp(scores - row_max)
    attn_probs = low(raised / lax.optimization_barrier(jnp.sum(raised, -1, keepdims=True)))
    attended = low(low_back(jnp.einsum('kgrl,lkd->rkgd', attn_probs, values, precision=highest).reshape(length, D)))
    middle = stream + low_back(matmul(attended, out_weight))
    normed_mlp = low(rms_norm(middle, mlp_gain))
    gate_value = low_back(matmul(normed_mlp, gate_weight))
    up_value = low_back(matmul(normed_mlp, up_weight))
    hidden = low(jax.nn.silu(gate_value) * up_value)
    return middle + low_back(matmul(hidden, down_weight))

def reference(tokens, positions, vectors, w_query, w_key, w_value, w_out, w_gate, w_up, w_down, cotangent):
    step_layer = jax.checkpoint(sequence_layer)

    def forward(stream, vector_all, query_all, key_all, value_all, out_all, gate_all, up_all, down_all):
        for layer_index in range(LAYERS):
            params = (vector_all[layer_index], query_all[layer_index], key_all[layer_index], value_all[layer_index], out_all[layer_index], gate_all[layer_index], up_all[layer_index], down_all[layer_index])
            stream = lax.map(lambda pair_item: step_layer(pair_item[0], pair_item[1], params), (stream, positions))
        return stream
    output, pullback = jax.vjp(forward, tokens.astype(jnp.float32), vectors.astype(jnp.float32), w_query.astype(jnp.float32), w_key.astype(jnp.float32), w_value.astype(jnp.float32), w_out.astype(jnp.float32), w_gate.astype(jnp.float32), w_up.astype(jnp.float32), w_down.astype(jnp.float32))
    gradients = pullback(cotangent.astype(jnp.float32))
    return (output.astype(jnp.bfloat16), gradients[0], gradients[1], gradients[2], gradients[3], gradients[4], gradients[5], gradients[6], gradients[7], gradients[8])
```

```python
import functools

import jax
import jax.numpy as jnp
import numpy as np
from jax import lax
from jax.experimental import pallas as pl
from jax.experimental.pallas import tpu as pltpu
from jax.sharding import Mesh
from jax.sharding import PartitionSpec as P

D = 576
HEADS = 9
KV_HEADS = 3
HEAD_DIM = 64
GROUP = HEADS // KV_HEADS
FF = 1536
ROWS = 256
BLOCK = 128
KEYS = 2048
KVD = KV_HEADS * HEAD_DIM
HALF_FF = FF // 2

rope_base = 10000.0
norm_eps = 1e-05
masked_score = -1e30
score_scale = HEAD_DIM ** (-0.5)

F32 = jnp.float32
BF16 = jnp.bfloat16

AXES = ("z", "xl", "xh", "y", "core")
SIZES = (4, 2, 2, 4, 2)
CTX = ("z", "xl")
FSDP = ("xh", "y", "core")
INNER = ("y", "core")
OUTER = ("z", "xl", "xh")

PACK = 896
PK_Q, PK_K, PK_V, PK_O, PK_GAIN = 0, 72, 96, 120, 192
PK_G, PK_U, PK_D = 256, 448, 640

A_STEP = 1024
A_WIDTH = 3 * A_STEP
B_STEP = 2 * FF
B_DOWN = 3 * B_STEP
B_OUT = B_DOWN + 8 * 512
B_DOWN_TAIL = B_OUT + 3 * 512
B_OUT_TAIL = B_DOWN_TAIL + 8 * 64
B_WIDTH = B_OUT_TAIL + 256

VMEM_LIMIT = 56 * 1024 * 1024


def feature_order():
    n = np.arange(D)
    owner, i = n // 36, n % 36
    xh, yc = owner // 8, owner % 8
    local = xh * 36 + i
    return (local // 24) * 192 + yc * 24 + local % 24


def hidden_order():
    n = np.arange(HALF_FF)
    yc, i = n // 96, n % 96
    return (i // 24) * 192 + yc * 24 + i % 24


def one_hot(places):
    size = len(places)
    out = np.zeros((size, size), np.float32)
    out[np.arange(size), places] = 1.0
    return out


def gain_matrix():
    n = np.arange(D)
    yc, local = n // 72, n % 72
    gathered = (local // 24) * 192 + yc * 24 + local % 24
    out = np.zeros((D, D), np.float32)
    out[gathered, feature_order()] = 1.0
    return out


def dot(left, right):
    return lax.dot_general(left, right, (((1,), (0,)), ((), ())), preferred_element_type=F32)


def dot_rows(left, right):
    return lax.dot_general(left, right, (((0,), (0,)), ((), ())), preferred_element_type=F32)


def dot_back(left, right):
    return lax.dot_general(left, right, (((1,), (1,)), ((), ())), preferred_element_type=F32)


def call(kernel, out_shape, n_in, smem=(), scratch=(), flops=0, bytes_accessed=0):
    in_specs = [
        pl.BlockSpec(memory_space=pltpu.SMEM) if i in smem else pl.BlockSpec(memory_space=pltpu.VMEM)
        for i in range(n_in)
    ]
    many = isinstance(out_shape, (list, tuple))
    out_spec = pl.BlockSpec(memory_space=pltpu.VMEM)
    return pl.pallas_call(
        kernel,
        out_shape=out_shape,
        in_specs=in_specs,
        out_specs=[out_spec] * len(out_shape) if many else out_spec,
        scratch_shapes=list(scratch),
        compiler_params=pltpu.CompilerParams(vmem_limit_bytes=VMEM_LIMIT),
        cost_estimate=pl.CostEstimate(
            flops=flops, bytes_accessed=bytes_accessed, transcendentals=0
        ),
    )


def sds(shape, dtype):
    return jax.ShapeDtypeStruct(shape, dtype)


def eye(size):
    rows = lax.broadcasted_iota(jnp.int32, (size, size), 0)
    cols = lax.broadcasted_iota(jnp.int32, (size, size), 1)
    return jnp.where(rows == cols, 1.0, 0.0).astype(F32)


def pack_kernel(vec, wq, wk, wv, wo, wg, wu, wd, out0, out1):
    diagonal = eye(36)
    for layer, out in ((0, out0), (1, out1)):
        gains = vec[layer : layer + 1, :].astype(F32)
        first = jnp.sum(diagonal * gains[:, :36], 1, keepdims=True)
        second = jnp.sum(diagonal * gains[:, 36:72], 1, keepdims=True)
        down = wd[layer].astype(F32)
        out[...] = jnp.concatenate(
            [
                wq[layer].astype(F32),
                wk[layer].astype(F32),
                wv[layer].astype(F32),
                wo[layer].astype(F32),
                first,
                second,
                jnp.zeros((36, 62), F32),
                wg[layer].astype(F32),
                wu[layer].astype(F32),
                down[:36],
                down[36:72],
                jnp.concatenate([down[72:96], jnp.zeros((12, 72), F32)], 0),
                jnp.zeros((36, 40), F32),
            ],
            1,
        ).astype(BF16)


def spread_kernel(index, blocks, pm, pf, a_out, b_out):
    def part(c, xh, low, high):
        return blocks[index[c * 2 + xh], :, low:high].astype(F32)

    def wide(low, high):
        halves = [
            jnp.concatenate([part(c, xh, low, high) for c in range(8)], 1) for xh in range(2)
        ]
        return jnp.concatenate(halves, 0)

    gains = [
        jnp.concatenate(
            [part(0, xh, PK_GAIN, PK_GAIN + 1), part(0, xh, PK_GAIN + 1, PK_GAIN + 2)], 0
        )
        for xh in range(2)
    ]
    a = jnp.concatenate(
        [wide(PK_Q, PK_K), wide(PK_K, PK_V), wide(PK_V, PK_O)] + gains + [jnp.zeros((72, 62), F32)],
        1,
    )
    for p in range(3):
        a_out[:, p * A_STEP : (p + 1) * A_STEP] = a[24 * p : 24 * p + 24].astype(BF16)
    out = dot(wide(PK_O, PK_GAIN).astype(BF16), pm[...])
    for p in range(3):
        piece = out[24 * p : 24 * p + 24].astype(BF16)
        b_out[:, B_OUT + p * 512 : B_OUT + (p + 1) * 512] = piece[:, :512]
        b_out[:, B_OUT_TAIL + p * 64 : B_OUT_TAIL + (p + 1) * 64] = piece[:, 512:]
    b_out[:, B_OUT_TAIL + 192 :] = jnp.zeros((24, 64), BF16)
    for shift, low, high in ((0, PK_G, PK_U), (FF, PK_U, PK_D)):
        natural = wide(low, high).astype(BF16)
        for half in range(2):
            placed = dot(natural[:, half * HALF_FF : (half + 1) * HALF_FF], pf[...])
            for p in range(3):
                start = p * B_STEP + shift + half * HALF_FF
                b_out[:, start : start + HALF_FF] = placed[24 * p : 24 * p + 24].astype(BF16)
    for xh in range(2):
        pieces = []
        for c in range(8):
            pieces.append(
                jnp.concatenate(
                    [
                        part(c, xh, PK_D, PK_D + 72),
                        part(c, xh, PK_D + 72, PK_D + 144),
                        part(c, xh, PK_D + 144, PK_D + 216)[:24],
                    ],
                    0,
                )
            )
        down = dot(jnp.concatenate(pieces, 1).astype(BF16), pm[...])
        for i in range(4):
            p = xh * 4 + i
            piece = down[24 * i : 24 * i + 24].astype(BF16)
            b_out[:, B_DOWN + p * 512 : B_DOWN + (p + 1) * 512] = piece[:, :512]
            b_out[:, B_DOWN_TAIL + p * 64 : B_DOWN_TAIL + (p + 1) * 64] = piece[:, 512:]


def gather_kernel(a, b, pm, pf, out):
    a72 = jnp.concatenate(
        [a[:, p * A_STEP : (p + 1) * A_STEP].astype(F32) for p in range(3)], 0
    )
    o72 = jnp.concatenate(
        [
            jnp.concatenate(
                [
                    b[:, B_OUT + p * 512 : B_OUT + (p + 1) * 512].astype(F32),
                    b[:, B_OUT_TAIL + p * 64 : B_OUT_TAIL + (p + 1) * 64].astype(F32),
                ],
                1,
            )
            for p in range(3)
        ],
        0,
    )
    o72 = dot_back(o72.astype(BF16), pm[...])
    sides = []
    for shift in (0, FF):
        halves = []
        for half in range(2):
            stacked = jnp.concatenate(
                [
                    b[
                        :,
                        p * B_STEP + shift + half * HALF_FF : p * B_STEP
                        + shift
                        + (half + 1) * HALF_FF,
                    ].astype(F32)
                    for p in range(3)
                ],
                0,
            )
            halves.append(dot_back(stacked.astype(BF16), pf[...]))
        sides.append(jnp.concatenate(halves, 1))
    for xh in range(2):
        down = jnp.concatenate(
            [
                jnp.concatenate(
                    [
                        b[:, B_DOWN + p * 512 : B_DOWN + (p + 1) * 512].astype(F32),
                        b[:, B_DOWN_TAIL + p * 64 : B_DOWN_TAIL + (p + 1) * 64].astype(F32),
                    ],
                    1,
                )
                for p in range(xh * 4, xh * 4 + 4)
            ],
            0,
        )
        down = dot_back(down.astype(BF16), pm[...])
        rows = slice(xh * 36, xh * 36 + 36)
        gain = a72[:, 960 + xh : 961 + xh]
        gains = jnp.concatenate([gain[:36], gain[36:72]], 1)
        for c in range(8):
            cols = slice(c * 72, c * 72 + 72)
            piece = down[:, cols]
            out[c * 2 + xh] = jnp.concatenate(
                [
                    a72[rows, cols],
                    a72[rows, 576 + c * 24 : 600 + c * 24],
                    a72[rows, 768 + c * 24 : 792 + c * 24],
                    o72[rows, cols],
                    gains,
                    jnp.zeros((36, 62), F32),
                    sides[0][rows, c * 192 : c * 192 + 192],
                    sides[1][rows, c * 192 : c * 192 + 192],
                    piece[:36],
                    piece[36:72],
                    jnp.concatenate([piece[72:96], jnp.zeros((12, 72), F32)], 0),
                    jnp.zeros((36, 40), F32),
                ],
                1,
            ).astype(BF16)


def finish_kernel(r0, r1, vec, wq, wk, wv, wo, wg, wu, wd):
    diagonal = eye(36)
    for layer, ref in ((0, r0), (1, r1)):
        total = ref[0].astype(F32)
        for i in range(1, 16):
            total = total + ref[i].astype(F32)
        wq[layer] = total[:, PK_Q:PK_K]
        wk[layer] = total[:, PK_K:PK_V]
        wv[layer] = total[:, PK_V:PK_O]
        wo[layer] = total[:, PK_O:PK_GAIN]
        first = jnp.sum(diagonal * total[:, PK_GAIN : PK_GAIN + 1], 0, keepdims=True)
        second = jnp.sum(diagonal * total[:, PK_GAIN + 1 : PK_GAIN + 2], 0, keepdims=True)
        vec[layer : layer + 1, :] = jnp.concatenate([first, second], 1)
        wg[layer] = total[:, PK_G:PK_U]
        wu[layer] = total[:, PK_U:PK_D]
        wd[layer] = jnp.concatenate(
            [
                total[:, PK_D : PK_D + 72],
                total[:, PK_D + 72 : PK_D + 144],
                total[:24, PK_D + 144 : PK_D + 216],
            ],
            0,
        )


def swap_halves(tile):
    lane = lax.broadcasted_iota(jnp.int32, tile.shape, 1) % HEAD_DIM
    return jnp.where(
        lane < HEAD_DIM // 2,
        pltpu.roll(tile, 128 - HEAD_DIM // 2, 1),
        pltpu.roll(tile, HEAD_DIM // 2, 1),
    )


def enter_kernel(tokens, cotangent, pm, x_out, g_out):
    x_out[...] = dot(tokens[...], pm[...])
    g_out[...] = dot(cotangent[...], pm[...])


def pre_kernel(x_ref, a, pq, cosine, sine, normed_out, q_out, kv_out, gains_out):
    gains = dot_rows(a[:, 896:1024], pq[0:192, :])
    for p in range(1, 3):
        gains = gains + dot_rows(
            a[:, p * A_STEP + 896 : (p + 1) * A_STEP], pq[p * 192 : (p + 1) * 192, :]
        )
    gains = gains[64:72]
    gains_out[...] = gains
    x = x_ref[...]
    inverse = lax.rsqrt(jnp.mean(x * x, -1, keepdims=True) + norm_eps)
    normed = (x * inverse * gains[0:1]).astype(BF16)
    normed_out[...] = normed
    lin = dot(normed[:, :192], a[:, :A_STEP])
    for p in range(1, 3):
        lin = lin + dot(
            normed[:, p * 192 : (p + 1) * 192], a[:, p * A_STEP : (p + 1) * A_STEP]
        )
    turned = []
    for t in range(6):
        tile = lin[:, t * 128 : (t + 1) * 128]
        turned.append(tile * cosine[...] + swap_halves(tile) * sine[...])
    turned = jnp.concatenate(turned, 1)
    q_out[...] = (turned[:, :D] * score_scale).astype(BF16)
    kv_out[...] = jnp.concatenate([turned[:, D:768], lin[:, 768:960]], 1).astype(BF16)


def weight_back(left, b, main, tail, p):
    return dot_back(left[:, :512], b[:, main + p * 512 : main + (p + 1) * 512]) + dot_back(
        left[:, 512:], b[:, tail + p * 64 : tail + (p + 1) * 64]
    )


def post_kernel(last, o_ref, x_ref, gains, pm, b, mid_out, op_out, nm_out, gate_out, up_out, hid_out, x_out):
    op = dot(o_ref[...], pm[...]).astype(BF16)
    op_out[...] = op

    def through(left, main, tail, count):
        wide = None
        narrow = None
        for p in range(count):
            piece = left[:, p * 192 : (p + 1) * 192]
            one = dot(piece, b[:, main + p * 512 : main + (p + 1) * 512])
            two = dot(piece, b[:, tail + p * 64 : tail + (p + 1) * 64])
            wide = one if wide is None else wide + one
            narrow = two if narrow is None else narrow + two
        return jnp.concatenate([wide, narrow], 1)

    mid = x_ref[...] + through(op, B_OUT, B_OUT_TAIL, 3)
    mid_out[...] = mid
    inverse = lax.rsqrt(jnp.mean(mid * mid, -1, keepdims=True) + norm_eps)
    nm = (mid * inverse * gains[1:2, :]).astype(BF16)
    nm_out[...] = nm
    gate = dot(nm[:, :192], b[:, :FF])
    up = dot(nm[:, :192], b[:, FF : 2 * FF])
    for p in range(1, 3):
        piece = nm[:, p * 192 : (p + 1) * 192]
        gate = gate + dot(piece, b[:, p * B_STEP : p * B_STEP + FF])
        up = up + dot(piece, b[:, p * B_STEP + FF : (p + 1) * B_STEP])
    gate_out[...] = gate.astype(BF16)
    up_out[...] = up.astype(BF16)
    hid = (gate / (1.0 + jnp.exp(-gate)) * up).astype(BF16)
    hid_out[...] = hid
    out = mid + through(hid, B_DOWN, B_DOWN_TAIL, 8)
    if last:
        x_out[...] = dot_back(out.astype(BF16), pm[...]).astype(BF16)
    else:
        x_out[...] = out


def norm_back(dy, v, gain):
    inverse = lax.rsqrt(jnp.mean(v * v, -1, keepdims=True) + norm_eps)
    scaled = dy * gain
    back = inverse * scaled - v * (
        inverse * inverse * inverse * jnp.mean(scaled * v, -1, keepdims=True)
    )
    return back, jnp.sum(dy * v * inverse, 0, keepdims=True)


def mlp_back_kernel(
    g_ref, nm, gate_ref, up_ref, hid, mid, op, gains, pm, b, db, gm_out, do_out, dg_out
):
    g = g_ref[...]
    gb = g.astype(BF16)
    dh = []
    for p in range(8):
        piece = dot_rows(hid[:, p * 192 : (p + 1) * 192], gb)
        db[:, B_DOWN + p * 512 : B_DOWN + (p + 1) * 512] = piece[:, :512].astype(BF16)
        db[:, B_DOWN_TAIL + p * 64 : B_DOWN_TAIL + (p + 1) * 64] = piece[:, 512:].astype(BF16)
        dh.append(weight_back(gb, b, B_DOWN, B_DOWN_TAIL, p))
    dh = jnp.concatenate(dh, 1)
    gate = gate_ref[...].astype(F32)
    up = up_ref[...].astype(F32)
    sig = 1.0 / (1.0 + jnp.exp(-gate))
    d_gate = (dh * up * sig * (1.0 + gate * (1.0 - sig))).astype(BF16)
    d_up = (dh * (gate * sig)).astype(BF16)
    dnm = []
    for p in range(3):
        piece = nm[:, p * 192 : (p + 1) * 192]
        low = p * B_STEP
        db[:, low : low + FF] = dot_rows(piece, d_gate).astype(BF16)
        db[:, low + FF : low + 2 * FF] = dot_rows(piece, d_up).astype(BF16)
        dnm.append(
            dot_back(d_gate, b[:, low : low + FF]) + dot_back(d_up, b[:, low + FF : low + 2 * FF])
        )
    back, gain_grad = norm_back(jnp.concatenate(dnm, 1), mid[...], gains[1:2, :])
    dg_out[...] = gain_grad
    gm = g + back
    gm_out[...] = gm
    gmb = gm.astype(BF16)
    dop = []
    for p in range(3):
        piece = dot_rows(op[:, p * 192 : (p + 1) * 192], gmb)
        db[:, B_OUT + p * 512 : B_OUT + (p + 1) * 512] = piece[:, :512].astype(BF16)
        db[:, B_OUT_TAIL + p * 64 : B_OUT_TAIL + (p + 1) * 64] = piece[:, 512:].astype(BF16)
        dop.append(weight_back(gmb, b, B_OUT, B_OUT_TAIL, p))
    db[:, B_OUT_TAIL + 192 :] = jnp.zeros((192, 64), BF16)
    do_out[...] = dot_back(jnp.concatenate(dop, 1).astype(BF16), pm[...]).astype(BF16)


def qkv_back_kernel(
    last, dq, kv0, kv1, kv2, kv3, cosine, sine, normed, x_ref, a, gains, pq, pm, gm, dg2, da, x_out
):
    dkv = kv0[...].astype(F32) + kv1[...].astype(F32) + kv2[...].astype(F32) + kv3[...].astype(F32)
    rot = jnp.concatenate([dq[...], dkv[:, :KVD]], 1)
    turned = []
    for t in range(6):
        tile = rot[:, t * 128 : (t + 1) * 128]
        turned.append(tile * cosine[...] - swap_halves(tile) * sine[...])
    dqkv = jnp.concatenate(turned + [dkv[:, KVD:], jnp.zeros((ROWS, 64), F32)], 1).astype(BF16)
    dn = []
    for p in range(3):
        low = p * A_STEP
        da[:, low : low + A_STEP] = dot_rows(
            normed[:, p * 192 : (p + 1) * 192], dqkv
        ).astype(BF16)
        dn.append(dot_back(dqkv, a[:, low : low + A_STEP]))
    x = x_ref[...]
    back, dg1 = norm_back(jnp.concatenate(dn, 1), x, gains[0:1, :])
    rows = lax.broadcasted_iota(jnp.int32, (64, D), 0)
    stacked = jnp.where(rows == 0, dg1, jnp.where(rows == 1, dg2[...], 0.0)).astype(BF16)
    placed = dot_back(pq[...], stacked).astype(BF16)
    for p in range(3):
        da[:, p * A_STEP + 960 : (p + 1) * A_STEP] = placed[p * 192 : (p + 1) * 192]
    out = gm[...] + back
    if last:
        high = out.astype(BF16)
        low = (out - high.astype(F32)).astype(BF16)
        x_out[...] = dot_back(high, pm[...]) + dot_back(low, pm[...])
    else:
        x_out[...] = out


def load_heads(q_ref, scratch, run):
    for g in range(KV_HEADS):
        scratch[run * KV_HEADS + g] = jnp.concatenate(
            [
                q_ref[
                    run * BLOCK : (run + 1) * BLOCK,
                    (g * GROUP + h) * HEAD_DIM : (g * GROUP + h + 1) * HEAD_DIM,
                ]
                for h in range(GROUP)
            ],
            0,
        )


def sort_keys(table, kv_ref, ks, vs):
    for j in range(KEYS // BLOCK):
        start = pl.multiple_of(table[2 + j] * BLOCK, BLOCK)
        for g in range(KV_HEADS):
            ks[g, pl.ds(start, BLOCK), :] = kv_ref[
                j * BLOCK : (j + 1) * BLOCK, g * HEAD_DIM : (g + 1) * HEAD_DIM
            ]
            vs[g, pl.ds(start, BLOCK), :] = kv_ref[
                j * BLOCK : (j + 1) * BLOCK, KVD + g * HEAD_DIM : KVD + (g + 1) * HEAD_DIM
            ]


def step_of(table, it):
    first = (table[0] + 2) // 2
    second = it >= first
    run = jnp.where(second, 1, 0)
    chunk = jnp.where(second, it - first, it)
    block = jnp.where(second, table[1], table[0])
    return run, chunk, block


def seen(chunk, block):
    key = chunk * 256 + lax.broadcasted_iota(jnp.int32, (256, GROUP * BLOCK), 0)
    row = block * BLOCK + lax.broadcasted_iota(jnp.int32, (256, GROUP * BLOCK), 1) % BLOCK
    return key <= row


STEPS = KEYS // 256 + 1


def attend_kernel(table, q_ref, kv_ref, o_out, lse_out, ks, vs, qs, ms, ls, acc):
    sort_keys(table, kv_ref, ks, vs)
    load_heads(q_ref, qs, 0)
    load_heads(q_ref, qs, 1)
    ms[...] = jnp.full(ms.shape, masked_score, F32)
    ls[...] = jnp.zeros(ls.shape, F32)
    acc[...] = jnp.zeros(acc.shape, F32)

    def step(it, carry):
        run, chunk, block = step_of(table, it)
        mask = seen(chunk, block)
        start = pl.multiple_of(chunk * 256, 256)
        for g in range(KV_HEADS):
            at = run * KV_HEADS + g
            scores = dot_back(ks[g, pl.ds(start, 256), :], qs[at])
            scores = jnp.where(mask, scores, masked_score)
            before = ms[at]
            now = jnp.maximum(before, jnp.max(scores, 0, keepdims=True))
            raised = jnp.exp(scores - now)
            shrink = jnp.exp(before - now)
            ms[at] = now
            ls[at] = ls[at] * shrink + jnp.sum(raised, 0, keepdims=True)
            acc[at] = acc[at] * shrink + dot_rows(
                vs[g, pl.ds(start, 256), :], raised.astype(BF16)
            )
        return carry

    lax.fori_loop(0, STEPS, step, 0)
    for run in range(2):
        for g in range(KV_HEADS):
            at = run * KV_HEADS + g
            total = ls[at]
            lse_out[at] = ms[at] + jnp.log(total)
            heads = (acc[at] / total).T
            for h in range(GROUP):
                o_out[
                    run * BLOCK : (run + 1) * BLOCK,
                    (g * GROUP + h) * HEAD_DIM : (g * GROUP + h + 1) * HEAD_DIM,
                ] = heads[h * BLOCK : (h + 1) * BLOCK].astype(BF16)


def attend_back_kernel(
    table, q_ref, kv_ref, o_ref, do_ref, lse, dq_out, dkv_out, ks, vs, qs, dos, deltas, dks, dvs, dqs
):
    sort_keys(table, kv_ref, ks, vs)
    for run in range(2):
        load_heads(q_ref, qs, run)
        load_heads(do_ref, dos, run)
        for g in range(KV_HEADS):
            at = run * KV_HEADS + g
            o = jnp.concatenate(
                [
                    o_ref[
                        run * BLOCK : (run + 1) * BLOCK,
                        (g * GROUP + h) * HEAD_DIM : (g * GROUP + h + 1) * HEAD_DIM,
                    ]
                    for h in range(GROUP)
                ],
                0,
            )
            product = o.astype(F32) * dos[at].astype(F32)
            deltas[at] = jnp.sum(product.T, 0, keepdims=True)
    dks[...] = jnp.zeros(dks.shape, F32)
    dvs[...] = jnp.zeros(dvs.shape, F32)
    dqs[...] = jnp.zeros(dqs.shape, F32)

    def step(it, carry):
        run, chunk, block = step_of(table, it)
        mask = seen(chunk, block)
        start = pl.multiple_of(chunk * 256, 256)
        for g in range(KV_HEADS):
            at = run * KV_HEADS + g
            k = ks[g, pl.ds(start, 256), :]
            v = vs[g, pl.ds(start, 256), :]
            q = qs[at]
            do = dos[at]
            scores = jnp.where(mask, dot_back(k, q), masked_score)
            probs = jnp.exp(scores - lse[at])
            d_scores = (probs * (dot_back(v, do) - deltas[at])).astype(BF16)
            dvs[g, pl.ds(start, 256), :] += dot(probs.astype(BF16), do)
            dks[g, pl.ds(start, 256), :] += dot(d_scores, q)
            dqs[at] += dot_rows(k, d_scores)
        return carry

    lax.fori_loop(0, STEPS, step, 0)
    for run in range(2):
        for g in range(KV_HEADS):
            heads = (dqs[run * KV_HEADS + g] * score_scale).T
            for h in range(GROUP):
                dq_out[
                    run * BLOCK : (run + 1) * BLOCK,
                    (g * GROUP + h) * HEAD_DIM : (g * GROUP + h + 1) * HEAD_DIM,
                ] = heads[h * BLOCK : (h + 1) * BLOCK]
    for j in range(KEYS // BLOCK):
        start = pl.multiple_of(table[2 + j] * BLOCK, BLOCK)
        rows = slice(j * BLOCK, (j + 1) * BLOCK)
        dkv_out[rows, :] = jnp.concatenate(
            [dks[g, pl.ds(start, BLOCK), :] for g in range(KV_HEADS)]
            + [dvs[g, pl.ds(start, BLOCK), :] for g in range(KV_HEADS)],
            1,
        ).astype(BF16)


def attend(table, q, kv_all):
    slots = 2 * KV_HEADS
    return call(
        attend_kernel,
        [sds((ROWS, D), BF16), sds((slots, 1, GROUP * BLOCK), F32)],
        3,
        smem=(0,),
        scratch=[
            pltpu.VMEM((KV_HEADS, KEYS, HEAD_DIM), BF16),
            pltpu.VMEM((KV_HEADS, KEYS, HEAD_DIM), BF16),
            pltpu.VMEM((slots, GROUP * BLOCK, HEAD_DIM), BF16),
            pltpu.VMEM((slots, 1, GROUP * BLOCK), F32),
            pltpu.VMEM((slots, 1, GROUP * BLOCK), F32),
            pltpu.VMEM((slots, HEAD_DIM, GROUP * BLOCK), F32),
        ],
        flops=4 * HEADS * ROWS * 1152 * HEAD_DIM,
        bytes_accessed=4 << 20,
    )(table, q, kv_all)


def attend_back(table, q, kv_all, o, do, lse):
    slots = 2 * KV_HEADS
    return call(
        attend_back_kernel,
        [sds((ROWS, D), F32), sds((KEYS, 2 * KVD), BF16)],
        6,
        smem=(0,),
        scratch=[
            pltpu.VMEM((KV_HEADS, KEYS, HEAD_DIM), BF16),
            pltpu.VMEM((KV_HEADS, KEYS, HEAD_DIM), BF16),
            pltpu.VMEM((slots, GROUP * BLOCK, HEAD_DIM), BF16),
            pltpu.VMEM((slots, GROUP * BLOCK, HEAD_DIM), BF16),
            pltpu.VMEM((slots, 1, GROUP * BLOCK), F32),
            pltpu.VMEM((KV_HEADS, KEYS, HEAD_DIM), F32),
            pltpu.VMEM((KV_HEADS, KEYS, HEAD_DIM), F32),
            pltpu.VMEM((slots, HEAD_DIM, GROUP * BLOCK), F32),
        ],
        flops=10 * HEADS * ROWS * 1152 * HEAD_DIM,
        bytes_accessed=6 << 20,
    )(table, q, kv_all, o, do, lse)


def ring(shift):
    return [(i, (i + shift) % 4) for i in range(4)]


def ring_x(shift):
    pairs = []
    for x in range(4):
        to = (x + shift) % 4
        pairs.append(((x % 2) * 2 + x // 2, (to % 2) * 2 + to // 2))
    return pairs


SHIFTS = (1, -1, 2)


def from_x(value):
    return [value] + [lax.ppermute(value, ("xl", "xh"), ring_x(s)) for s in SHIFTS]


def from_z(value):
    return [value] + [lax.ppermute(value, "z", ring(s)) for s in SHIFTS]


def other_core(value):
    return lax.ppermute(value, "core", [(0, 1), (1, 0)])


def trade(value):
    return lax.ppermute(value, ("xl", "core"), [(0, 0), (1, 2), (2, 1), (3, 3)])


def block_index():
    z, xl, xh = (lax.axis_index(name) for name in OUTER)
    x = xh * 2 + xl
    place = jnp.array([0, 1, 3, 2], jnp.int32)
    out = []
    for bz in range(4):
        dz = place[(z - bz) % 4]
        for bl in range(2):
            for bh in range(2):
                out.append(dz * 4 + place[(x - (bh * 2 + bl)) % 4])
    return jnp.stack(out).astype(jnp.int32)


def fetch(pack, index, pm, pf):
    near = jnp.stack(from_x(pack))
    blocks = jnp.concatenate(from_z(near), 0)
    a, b = call(
        spread_kernel, [sds((24, A_WIDTH), BF16), sds((24, B_WIDTH), BF16)], 4, smem=(0,)
    )(index, blocks, pm, pf)
    return (
        lax.all_gather(a, INNER, axis=0, tiled=True),
        lax.all_gather(b, INNER, axis=0, tiled=True),
    )


def share_keys(kv):
    near = jnp.concatenate(from_z(kv), 0)
    return jnp.concatenate([near, other_core(near)], 0)


def return_keys(dkv):
    half = KEYS // 2
    near = (dkv[:half].astype(F32) + other_core(dkv[half:]).astype(F32)).astype(BF16)
    parts = [near[i * ROWS : (i + 1) * ROWS] for i in range(4)]
    return [parts[0]] + [
        lax.ppermute(part, "z", ring(-s)) for part, s in zip(parts[1:], SHIFTS)
    ]


def key_table(positions):
    starts = trade(positions[0, ::BLOCK]) // BLOCK
    z, core = lax.axis_index("z"), lax.axis_index("core")
    own = lax.dynamic_slice_in_dim(starts, (z * 2 + core) * 2, 2)
    order = []
    for k in range(2):
        for s in (0,) + SHIFTS:
            chunk = ((z - s) % 4) * 2 + (core + k) % 2
            order.append(lax.dynamic_slice_in_dim(starts, chunk * 2, 2))
    return own, jnp.concatenate(order)


def angles(places):
    half_dim = HEAD_DIM // 2
    inverse = rope_base ** (-2.0 * jnp.arange(half_dim).astype(F32) / HEAD_DIM)
    turned = places.astype(F32)[:, None] * inverse[None, :]
    cosine, sine = jnp.cos(turned), jnp.sin(turned)
    return jnp.concatenate([cosine] * 4, 1), jnp.concatenate([-sine, sine] * 2, 1)


def on_device(
    tokens, positions, vectors, w_query, w_key, w_value, w_out, w_gate, w_up, w_down, cotangent
):
    pm = jnp.asarray(one_hot(feature_order()), BF16)
    pf = jnp.asarray(one_hot(hidden_order()), BF16)
    pq = jnp.asarray(gain_matrix(), BF16)
    index = block_index()
    packs = call(pack_kernel, [sds((36, PACK), BF16)] * 2, 8)(
        vectors, w_query, w_key, w_value, w_out, w_gate, w_up, w_down
    )
    weights = [fetch(packs[layer], index, pm, pf) for layer in range(2)]

    own, order = key_table(positions)
    table_f = jnp.concatenate([own, order])
    places = (own[:, None] * BLOCK + jnp.arange(BLOCK)[None, :]).reshape(ROWS)
    cosine, sine = angles(places)
    x, grad = call(enter_kernel, [sds((ROWS, D), F32)] * 2, 3)(
        trade(tokens[0]), trade(cotangent[0]), pm
    )

    saved = []
    for layer in range(2):
        a, b = weights[layer]
        normed, q, kv, gains = call(
            pre_kernel,
            [sds((ROWS, D), BF16), sds((ROWS, D), BF16), sds((ROWS, 2 * KVD), BF16), sds((8, D), F32)],
            5,
        )(x, a, pq, cosine, sine)
        kv_all = share_keys(kv)
        o, lse = attend(table_f, q, kv_all)
        last = layer == 1
        mid, op, nm, gate, up, hid, x_next = call(
            functools.partial(post_kernel, last),
            [
                sds((ROWS, D), F32),
                sds((ROWS, D), BF16),
                sds((ROWS, D), BF16),
                sds((ROWS, FF), BF16),
                sds((ROWS, FF), BF16),
                sds((ROWS, FF), BF16),
                sds((ROWS, D), BF16 if last else F32),
            ],
            5,
        )(o, x, gains, pm, b)
        saved.append((x, normed, q, kv_all, gains, o, lse, mid, op, nm, gate, up, hid))
        x = x_next
    output = trade(x)[None]

    summed = [None, None]
    for layer in (1, 0):
        a, b = weights[layer]
        x, normed, q, kv_all, gains, o, lse, mid, op, nm, gate, up, hid = saved[layer]
        db, gm, do, dg2 = call(
            mlp_back_kernel,
            [sds((192, B_WIDTH), BF16), sds((ROWS, D), F32), sds((ROWS, D), BF16), sds((1, D), F32)],
            10,
        )(grad, nm, gate, up, hid, mid, op, gains, pm, b)
        db = lax.psum_scatter(db, INNER, scatter_dimension=0, tiled=True)
        dq, dkv = attend_back(table_f, q, kv_all, o, do, lse)
        parts = return_keys(dkv)
        da, grad = call(
            functools.partial(qkv_back_kernel, layer == 0),
            [sds((192, A_WIDTH), BF16), sds((ROWS, D), F32)],
            15,
        )(dq, *parts, cosine, sine, normed, x, a, gains, pq, pm, gm, dg2)
        da = lax.psum_scatter(da, INNER, scatter_dimension=0, tiled=True)
        blocks = call(gather_kernel, sds((16, 36, PACK), BF16), 4)(da, db, pm, pf)
        summed[layer] = lax.all_to_all(blocks, OUTER, 0, 0, tiled=True)
    grad_tokens = trade(grad)[None]
    outs = call(
        finish_kernel,
        [
            sds((2, 72), F32),
            sds((2, 36, 72), F32),
            sds((2, 36, 24), F32),
            sds((2, 36, 24), F32),
            sds((2, 36, 72), F32),
            sds((2, 36, 192), F32),
            sds((2, 36, 192), F32),
            sds((2, 96, 72), F32),
        ],
        2,
    )(*summed)
    return (output, grad_tokens, *outs)


def solution(mesh):
    fine = Mesh(np.asarray(mesh.devices).reshape(SIZES), AXES)
    split = P(None, FSDP, CTX)
    rows = P(FSDP, CTX, None)
    return jax.shard_map(
        on_device,
        mesh=fine,
        in_specs=(rows, P(FSDP, None), P(None, FSDP)) + (split,) * 7 + (rows,),
        out_specs=(rows, rows, P(None, FSDP)) + (split,) * 7,
        check_vma=False,
    )
```

```python
import functools

import jax
import jax.numpy as jnp
import numpy as np
from jax import lax
from jax.experimental import pallas as pl
from jax.experimental.pallas import tpu as pltpu
from jax.sharding import Mesh
from jax.sharding import PartitionSpec as P

D = 576
HEADS = 9
KV_HEADS = 3
HEAD_DIM = 64
GROUP = HEADS // KV_HEADS
FF = 1536
ROWS = 256
BLOCK = 128
KEYS = 2048
KVD = KV_HEADS * HEAD_DIM
HALF_FF = FF // 2

rope_base = 10000.0
norm_eps = 1e-05
masked_score = -1e30
score_scale = HEAD_DIM ** (-0.5)

F32 = jnp.float32
BF16 = jnp.bfloat16

AXES = ("z", "xl", "xh", "y", "core")
SIZES = (4, 2, 2, 4, 2)
CTX = ("z", "xl")
FSDP = ("xh", "y", "core")
INNER = ("y", "core")
OUTER = ("z", "xl", "xh")

PACK = 896
PACK_A = 128
PACK_B = PACK - PACK_A
PK_Q, PK_K, PK_V, PK_GAIN = 0, 72, 96, 120
PK_O, PK_G, PK_U, PK_D = 128, 200, 392, 584

A_STEP = 1024
A_WIDTH = 3 * A_STEP
B_STEP = 2 * FF
B_DOWN = 3 * B_STEP
B_OUT = B_DOWN + 8 * 512
B_DOWN_TAIL = B_OUT + 3 * 512
B_OUT_TAIL = B_DOWN_TAIL + 8 * 64
B_WIDTH = B_OUT_TAIL + 256

C_WIDTH = B_WIDTH + A_WIDTH


def feature_order():
    n = np.arange(D)
    owner, i = n // 36, n % 36
    xh, yc = owner // 8, owner % 8
    local = xh * 36 + i
    return (local // 24) * 192 + yc * 24 + local % 24


def hidden_order():
    n = np.arange(HALF_FF)
    yc, i = n // 96, n % 96
    return (i // 24) * 192 + yc * 24 + i % 24


def one_hot(places):
    size = len(places)
    out = np.zeros((size, size), np.float32)
    out[np.arange(size), places] = 1.0
    return out


def gain_matrix():
    n = np.arange(D)
    yc, local = n // 72, n % 72
    gathered = (local // 24) * 192 + yc * 24 + local % 24
    out = np.zeros((D, D), np.float32)
    out[gathered, feature_order()] = 1.0
    return out


def dot(left, right):
    return lax.dot_general(left, right, (((1,), (0,)), ((), ())), preferred_element_type=F32)


def dot_rows(left, right):
    return lax.dot_general(left, right, (((0,), (0,)), ((), ())), preferred_element_type=F32)


def dot_back(left, right):
    return lax.dot_general(left, right, (((1,), (1,)), ((), ())), preferred_element_type=F32)


def call(
    kernel, out_shape, n_in, vmem, smem=(), anywhere=(), scratch=(), flops=0, bytes_accessed=0
):
    def space(i):
        return pltpu.SMEM if i in smem else pl.ANY if i in anywhere else pltpu.VMEM

    in_specs = [pl.BlockSpec(memory_space=space(i)) for i in range(n_in)]
    many = isinstance(out_shape, (list, tuple))
    out_spec = pl.BlockSpec(memory_space=pltpu.VMEM)
    return pl.pallas_call(
        kernel,
        out_shape=out_shape,
        in_specs=in_specs,
        out_specs=[out_spec] * len(out_shape) if many else out_spec,
        scratch_shapes=list(scratch),
        compiler_params=pltpu.CompilerParams(vmem_limit_bytes=56 << 20),
        cost_estimate=pl.CostEstimate(
            flops=flops, bytes_accessed=bytes_accessed, transcendentals=0
        ),
    )


def sds(shape, dtype):
    return jax.ShapeDtypeStruct(shape, dtype)


def eye(size):
    rows = lax.broadcasted_iota(jnp.int32, (size, size), 0)
    cols = lax.broadcasted_iota(jnp.int32, (size, size), 1)
    return jnp.where(rows == cols, 1.0, 0.0).astype(F32)


def pack_kernel(vec, wq, wk, wv, wo, wg, wu, wd, out0, out1):
    diagonal = eye(36)
    for layer, out in ((0, out0), (1, out1)):
        gains = vec[layer : layer + 1, :].astype(F32)
        first = jnp.sum(diagonal * gains[:, :36], 1, keepdims=True)
        second = jnp.sum(diagonal * gains[:, 36:72], 1, keepdims=True)
        down = wd[layer].astype(F32).T
        out[...] = jnp.concatenate(
            [
                wq[...].astype(F32)[:, layer],
                wk[layer].astype(F32).T,
                wv[layer].astype(F32).T,
                first,
                second,
                jnp.zeros((36, 6), F32),
                wo[...].astype(F32)[:, layer],
                wg[...].astype(F32)[:, layer],
                wu[...].astype(F32)[:, layer],
                down[:36],
                down[36:72],
                jnp.concatenate([down[72:96], jnp.zeros((12, 72), F32)], 0),
                jnp.zeros((36, 96), F32),
            ],
            1,
        ).astype(BF16)


def part_of(index, blocks, c, xh, low, high):
    return blocks[index[c * 2 + xh], :, low:high].astype(F32)


def wide_of(index, blocks, low, high):
    halves = [
        jnp.concatenate([part_of(index, blocks, c, xh, low, high) for c in range(8)], 1)
        for xh in range(2)
    ]
    return jnp.concatenate(halves, 0)


def spread_a_kernel(index, blocks, a_out):
    part = functools.partial(part_of, index, blocks)
    wide = functools.partial(wide_of, index, blocks)
    gains = [
        jnp.concatenate(
            [part(0, xh, PK_GAIN, PK_GAIN + 1), part(0, xh, PK_GAIN + 1, PK_GAIN + 2)], 0
        )
        for xh in range(2)
    ]
    a = jnp.concatenate(
        [wide(PK_Q, PK_K), wide(PK_K, PK_V), wide(PK_V, PK_GAIN)] + gains + [jnp.zeros((72, 62), F32)],
        1,
    )
    for p in range(3):
        a_out[:, p * A_STEP : (p + 1) * A_STEP] = a[24 * p : 24 * p + 24].astype(BF16)


def spread_b_kernel(index, blocks, pm, pf, b_out):
    part = functools.partial(part_of, index, blocks)
    wide = functools.partial(wide_of, index, blocks)
    out = dot(wide(PK_O, PK_G).astype(BF16), pm[...])
    for p in range(3):
        piece = out[24 * p : 24 * p + 24].astype(BF16)
        b_out[:, B_OUT + p * 512 : B_OUT + (p + 1) * 512] = piece[:, :512]
        b_out[:, B_OUT_TAIL + p * 64 : B_OUT_TAIL + (p + 1) * 64] = piece[:, 512:]
    b_out[:, B_OUT_TAIL + 192 :] = jnp.zeros((24, 64), BF16)
    for shift, low, high in ((0, PK_G, PK_U), (FF, PK_U, PK_D)):
        natural = wide(low, high).astype(BF16)
        for half in range(2):
            placed = dot(natural[:, half * HALF_FF : (half + 1) * HALF_FF], pf[...])
            for p in range(3):
                start = p * B_STEP + shift + half * HALF_FF
                b_out[:, start : start + HALF_FF] = placed[24 * p : 24 * p + 24].astype(BF16)
    for xh in range(2):
        pieces = []
        for c in range(8):
            pieces.append(
                jnp.concatenate(
                    [
                        part(c, xh, PK_D, PK_D + 72),
                        part(c, xh, PK_D + 72, PK_D + 144),
                        part(c, xh, PK_D + 144, PK_D + 216)[:24],
                    ],
                    0,
                )
            )
        down = dot(jnp.concatenate(pieces, 1).astype(BF16), pm[...])
        for i in range(4):
            p = xh * 4 + i
            piece = down[24 * i : 24 * i + 24].astype(BF16)
            b_out[:, B_DOWN + p * 512 : B_DOWN + (p + 1) * 512] = piece[:, :512]
            b_out[:, B_DOWN_TAIL + p * 64 : B_DOWN_TAIL + (p + 1) * 64] = piece[:, 512:]


def gathered_a(a, out, lanes):
    a72 = jnp.concatenate([a[:, p * A_STEP : (p + 1) * A_STEP] for p in range(3)], 0)
    for xh in range(2):
        rows = slice(xh * 36, xh * 36 + 36)
        gain = a72[:, 960 + xh : 961 + xh]
        for c in range(8):
            out[c * 2 + xh, :, lanes] = jnp.concatenate(
                [
                    a72[rows, c * 72 : c * 72 + 72],
                    a72[rows, 576 + c * 24 : 600 + c * 24],
                    a72[rows, 768 + c * 24 : 792 + c * 24],
                    gain[:36],
                    gain[36:72],
                    jnp.zeros((36, 6), F32),
                ],
                1,
            ).astype(BF16)


def gathered_b(b, pm, pf, out, lanes):
    o72 = jnp.concatenate(
        [
            jnp.concatenate(
                [
                    b[:, B_OUT + p * 512 : B_OUT + (p + 1) * 512].astype(F32),
                    b[:, B_OUT_TAIL + p * 64 : B_OUT_TAIL + (p + 1) * 64].astype(F32),
                ],
                1,
            )
            for p in range(3)
        ],
        0,
    )
    o72 = dot_back(o72.astype(BF16), pm[...])
    sides = []
    for shift in (0, FF):
        halves = []
        for half in range(2):
            low = shift + half * HALF_FF
            stacked = jnp.concatenate(
                [
                    b[:, p * B_STEP + low : p * B_STEP + low + HALF_FF].astype(F32)
                    for p in range(3)
                ],
                0,
            )
            halves.append(dot_back(stacked.astype(BF16), pf[...]))
        sides.append(jnp.concatenate(halves, 1))
    for xh in range(2):
        down = jnp.concatenate(
            [
                jnp.concatenate(
                    [
                        b[:, B_DOWN + p * 512 : B_DOWN + (p + 1) * 512].astype(F32),
                        b[:, B_DOWN_TAIL + p * 64 : B_DOWN_TAIL + (p + 1) * 64].astype(F32),
                    ],
                    1,
                )
                for p in range(xh * 4, xh * 4 + 4)
            ],
            0,
        )
        down = dot_back(down.astype(BF16), pm[...])
        rows = slice(xh * 36, xh * 36 + 36)
        for c in range(8):
            cols = slice(c * 72, c * 72 + 72)
            piece = down[:, cols]
            out[c * 2 + xh, :, lanes] = jnp.concatenate(
                [
                    o72[rows, cols],
                    sides[0][rows, c * 192 : c * 192 + 192],
                    sides[1][rows, c * 192 : c * 192 + 192],
                    piece[:36],
                    piece[36:72],
                    jnp.concatenate([piece[72:96], jnp.zeros((12, 72), F32)], 0),
                    jnp.zeros((36, 96), F32),
                ],
                1,
            ).astype(BF16)


def gather_first_kernel(b, pm, pf, out):
    gathered_b(b, pm, pf, out, slice(0, PACK_B))


def gather_last_kernel(a0, a1, a2, a3, c, pm, pf, out):
    a = a0[...].astype(F32) + a1[...].astype(F32) + a2[...].astype(F32) + a3[...].astype(F32)
    gathered_a(a, out, slice(0, PACK_A))
    gathered_b(c, pm, pf, out, slice(PACK_A, PACK))
    gathered_a(c[:, B_WIDTH:].astype(F32), out, slice(PACK, PACK + PACK_A))


def finish_kernel(first_ref, last_ref, vec, wq, wk, wv, wo, wg, wu, wd):
    diagonal = eye(36)

    def added(ref, low, high):
        total = ref[0, :, low:high].astype(F32)
        for i in range(1, 16):
            total = total + ref[i, :, low:high].astype(F32)
        return total

    totals = (
        added(last_ref, 0, PACK),
        jnp.concatenate([added(last_ref, PACK, PACK + PACK_A), added(first_ref, 0, PACK_B)], 1),
    )
    for layer, total in enumerate(totals):
        wq[:, layer, :] = total[:, PK_Q:PK_K]
        wk[layer] = total[:, PK_K:PK_V].T
        wv[layer] = total[:, PK_V:PK_GAIN].T
        wo[:, layer, :] = total[:, PK_O:PK_G]
        first = jnp.sum(diagonal * total[:, PK_GAIN : PK_GAIN + 1], 0, keepdims=True)
        second = jnp.sum(diagonal * total[:, PK_GAIN + 1 : PK_GAIN + 2], 0, keepdims=True)
        vec[layer : layer + 1, :] = jnp.concatenate([first, second], 1)
        wg[:, layer, :] = total[:, PK_G:PK_U]
        wu[:, layer, :] = total[:, PK_U:PK_D]
        wd[layer] = jnp.concatenate(
            [
                total[:, PK_D : PK_D + 72],
                total[:, PK_D + 72 : PK_D + 144],
                total[:24, PK_D + 144 : PK_D + 216],
            ],
            0,
        ).T


def swap_halves(tile):
    lane = lax.broadcasted_iota(jnp.int32, tile.shape, 1) % HEAD_DIM
    return jnp.where(
        lane < HEAD_DIM // 2,
        pltpu.roll(tile, 128 - HEAD_DIM // 2, 1),
        pltpu.roll(tile, HEAD_DIM // 2, 1),
    )


def enter_kernel(tokens, cotangent, pm, x_out, g_out):
    x_out[...] = dot_rows(tokens[...], pm[...])
    g_out[...] = dot_rows(cotangent[...], pm[...])


def place_rows(source):
    lane = lax.broadcasted_iota(jnp.int32, (192, 192), 1)
    return jnp.where(lane == source[...], 1.0, 0.0).astype(BF16)


def pre_placed_kernel(source, a_in, x_ref, pq, cosine, sine, a, normed_out, q_out, kv_out, gains_out):
    a[...] = dot(place_rows(source), a_in[...]).astype(BF16)
    pre_kernel(x_ref, a, pq, cosine, sine, normed_out, q_out, kv_out, gains_out)


def pre_kernel(x_ref, a, pq, cosine, sine, normed_out, q_out, kv_out, gains_out):
    gains = dot_rows(a[:, 896:1024], pq[0:192, :])
    for p in range(1, 3):
        gains = gains + dot_rows(
            a[:, p * A_STEP + 896 : (p + 1) * A_STEP], pq[p * 192 : (p + 1) * 192, :]
        )
    gains = gains[64:72]
    gains_out[...] = gains
    x = x_ref[...]
    inverse = lax.rsqrt(jnp.mean(x * x, -1, keepdims=True) + norm_eps)
    normed = (x * inverse * gains[0:1]).astype(BF16)
    normed_out[...] = normed
    lin = dot(normed[:, :192], a[:, :A_STEP])
    for p in range(1, 3):
        lin = lin + dot(
            normed[:, p * 192 : (p + 1) * 192], a[:, p * A_STEP : (p + 1) * A_STEP]
        )
    turned = []
    for t in range(6):
        tile = lin[:, t * 128 : (t + 1) * 128]
        turned.append(tile * cosine[...] + swap_halves(tile) * sine[...])
    turned = jnp.concatenate(turned, 1)
    q_out[...] = (turned[:, :D] * score_scale).astype(BF16)
    for g in range(KV_HEADS):
        part = slice(g * HEAD_DIM, (g + 1) * HEAD_DIM)
        kv_out[:, g * PAIR : (g + 1) * PAIR] = jnp.concatenate(
            [turned[:, D:768][:, part], lin[:, 768:960][:, part]], 1
        ).astype(BF16)


def weight_back(left, b, main, tail, p):
    return dot_back(left[:, :512], b[:, main + p * 512 : main + (p + 1) * 512]) + dot_back(
        left[:, 512:], b[:, tail + p * 64 : tail + (p + 1) * 64]
    )


def post_kernel(last, o_ref, x_ref, gains, pm, b, mid_out, op_out, nm_out, gate_out, up_out, hid_out, x_out):
    op = dot(o_ref[...], pm[...]).astype(BF16)
    op_out[...] = op

    def through(left, main, tail, count):
        wide = None
        narrow = None
        for p in range(count):
            piece = left[:, p * 192 : (p + 1) * 192]
            one = dot(piece, b[:, main + p * 512 : main + (p + 1) * 512])
            two = dot(piece, b[:, tail + p * 64 : tail + (p + 1) * 64])
            wide = one if wide is None else wide + one
            narrow = two if narrow is None else narrow + two
        return jnp.concatenate([wide, narrow], 1)

    mid = x_ref[...] + through(op, B_OUT, B_OUT_TAIL, 3)
    mid_out[...] = mid
    inverse = lax.rsqrt(jnp.mean(mid * mid, -1, keepdims=True) + norm_eps)
    nm = (mid * inverse * gains[1:2, :]).astype(BF16)
    nm_out[...] = nm
    gate = dot(nm[:, :192], b[:, :FF])
    up = dot(nm[:, :192], b[:, FF : 2 * FF])
    for p in range(1, 3):
        piece = nm[:, p * 192 : (p + 1) * 192]
        gate = gate + dot(piece, b[:, p * B_STEP : p * B_STEP + FF])
        up = up + dot(piece, b[:, p * B_STEP + FF : (p + 1) * B_STEP])
    gate_out[...] = gate.astype(BF16)
    up_out[...] = up.astype(BF16)
    hid = (gate / (1.0 + jnp.exp(-gate)) * up).astype(BF16)
    hid_out[...] = hid
    out = mid + through(hid, B_DOWN, B_DOWN_TAIL, 8)
    if last:
        x_out[...] = dot_back(pm[...], out.astype(BF16)).astype(BF16)
    else:
        x_out[...] = out


def norm_back(dy, v, gain):
    inverse = lax.rsqrt(jnp.mean(v * v, -1, keepdims=True) + norm_eps)
    scaled = dy * gain
    back = inverse * scaled - v * (
        inverse * inverse * inverse * jnp.mean(scaled * v, -1, keepdims=True)
    )
    return back, jnp.sum(dy * v * inverse, 0, keepdims=True)


def mlp_back_carry_kernel(da, *refs):
    db = refs[10]
    db[:, B_WIDTH:] = da[...]
    mlp_back_kernel(*refs)


def mlp_back_kernel(
    g_ref, nm, gate_ref, up_ref, hid, mid, op, gains, pm, b, db, gm_out, do_out, dg_out
):
    g = g_ref[...]
    gb = g.astype(BF16)
    dh = []
    for p in range(8):
        piece = dot_rows(hid[:, p * 192 : (p + 1) * 192], gb)
        db[:, B_DOWN + p * 512 : B_DOWN + (p + 1) * 512] = piece[:, :512].astype(BF16)
        db[:, B_DOWN_TAIL + p * 64 : B_DOWN_TAIL + (p + 1) * 64] = piece[:, 512:].astype(BF16)
        dh.append(weight_back(gb, b, B_DOWN, B_DOWN_TAIL, p))
    dh = jnp.concatenate(dh, 1)
    gate = gate_ref[...].astype(F32)
    up = up_ref[...].astype(F32)
    sig = 1.0 / (1.0 + jnp.exp(-gate))
    d_gate = (dh * up * sig * (1.0 + gate * (1.0 - sig))).astype(BF16)
    d_up = (dh * (gate * sig)).astype(BF16)
    dnm = []
    for p in range(3):
        piece = nm[:, p * 192 : (p + 1) * 192]
        low = p * B_STEP
        db[:, low : low + FF] = dot_rows(piece, d_gate).astype(BF16)
        db[:, low + FF : low + 2 * FF] = dot_rows(piece, d_up).astype(BF16)
        dnm.append(
            dot_back(d_gate, b[:, low : low + FF]) + dot_back(d_up, b[:, low + FF : low + 2 * FF])
        )
    back, gain_grad = norm_back(jnp.concatenate(dnm, 1), mid[...], gains[1:2, :])
    dg_out[...] = gain_grad
    gm = g + back
    gm_out[...] = gm
    gmb = gm.astype(BF16)
    dop = []
    for p in range(3):
        piece = dot_rows(op[:, p * 192 : (p + 1) * 192], gmb)
        db[:, B_OUT + p * 512 : B_OUT + (p + 1) * 512] = piece[:, :512].astype(BF16)
        db[:, B_OUT_TAIL + p * 64 : B_OUT_TAIL + (p + 1) * 64] = piece[:, 512:].astype(BF16)
        dop.append(weight_back(gmb, b, B_OUT, B_OUT_TAIL, p))
    db[:, B_OUT_TAIL + 192 : B_WIDTH] = jnp.zeros((192, 64), BF16)
    do_out[...] = dot_back(jnp.concatenate(dop, 1).astype(BF16), pm[...]).astype(BF16)


def qkv_back_kernel(
    last,
    dq,
    kv0,
    kv1,
    kv2,
    kv3,
    cosine,
    sine,
    normed,
    x_ref,
    a,
    gains,
    pq,
    pm,
    gm,
    dg2,
    source,
    da,
    x_out,
):
    dkv = kv0[...].astype(F32) + kv1[...].astype(F32) + kv2[...].astype(F32) + kv3[...].astype(F32)
    d_key = [dkv[:, g * PAIR : g * PAIR + HEAD_DIM] for g in range(KV_HEADS)]
    d_value = [dkv[:, g * PAIR + HEAD_DIM : (g + 1) * PAIR] for g in range(KV_HEADS)]
    rot = jnp.concatenate([dq[...]] + d_key, 1)
    turned = []
    for t in range(6):
        tile = rot[:, t * 128 : (t + 1) * 128]
        turned.append(tile * cosine[...] - swap_halves(tile) * sine[...])
    dqkv = jnp.concatenate(turned + d_value + [jnp.zeros((ROWS, 64), F32)], 1).astype(BF16)
    dn = []
    for p in range(3):
        low = p * A_STEP
        da[:, low : low + A_STEP] = dot_rows(
            normed[:, p * 192 : (p + 1) * 192], dqkv
        ).astype(BF16)
        dn.append(dot_back(dqkv, a[:, low : low + A_STEP]))
    x = x_ref[...]
    back, dg1 = norm_back(jnp.concatenate(dn, 1), x, gains[0:1, :])
    rows = lax.broadcasted_iota(jnp.int32, (64, D), 0)
    stacked = jnp.where(rows == 0, dg1, jnp.where(rows == 1, dg2[...], 0.0)).astype(BF16)
    placed = dot_back(pq[...], stacked).astype(BF16)
    for p in range(3):
        da[:, p * A_STEP + 960 : (p + 1) * A_STEP] = placed[p * 192 : (p + 1) * 192]
    out = gm[...] + back
    if last:
        high = out.astype(BF16)
        low = (out - high.astype(F32)).astype(BF16)
        x_out[...] = dot_back(pm[...], high) + dot_back(pm[...], low)
        da[...] = dot_rows(place_rows(source), da[...]).astype(BF16)
    else:
        x_out[...] = out


PAIR = 2 * HEAD_DIM
WIDE = GROUP * BLOCK
CHUNK = 256
STEPS = KEYS // CHUNK + 1
SLOTS = 2 * KV_HEADS


def load_heads(ref, scratch, run, upper):
    zero = jnp.zeros((WIDE, HEAD_DIM), BF16)
    for g in range(KV_HEADS):
        heads = jnp.concatenate(
            [
                ref[
                    run * BLOCK : (run + 1) * BLOCK,
                    (g * GROUP + h) * HEAD_DIM : (g * GROUP + h + 1) * HEAD_DIM,
                ]
                for h in range(GROUP)
            ],
            0,
        )
        both = [zero, heads] if upper else [heads, zero]
        scratch[run * KV_HEADS + g] = jnp.concatenate(both, 1)


def sort_keys(table, pieces, kvs):
    for j in range(KEYS // BLOCK):
        start = pl.multiple_of(table[2 + j] * BLOCK, BLOCK)
        kvs[pl.ds(start, BLOCK), :] = pieces[j // 2][(j % 2) * BLOCK : (j % 2 + 1) * BLOCK, :]


def set_lead(lead):
    key = lax.broadcasted_iota(jnp.int32, (CHUNK, BLOCK), 0)
    row = lax.broadcasted_iota(jnp.int32, (CHUNK, BLOCK), 1)
    lead[...] = row - key


def head_columns(h):
    return slice(h * BLOCK, (h + 1) * BLOCK)


def step_of(table, it):
    first = (table[0] + 2) // 2
    second = it >= first
    run = jnp.where(second, 1, 0)
    chunk = jnp.where(second, it - first, it)
    block = jnp.where(second, table[1], table[0])
    return run, pl.multiple_of(chunk * CHUNK, CHUNK), chunk * CHUNK - block * BLOCK


def attend_kernel(table, q_ref, *refs):
    pieces, (o_out, lse_out, kvs, qs, lead, ms, ls, acc) = refs[:8], refs[8:]
    sort_keys(table, pieces, kvs)
    load_heads(q_ref, qs, 0, False)
    load_heads(q_ref, qs, 1, False)
    set_lead(lead)
    ms[...] = jnp.full(ms.shape, masked_score, F32)
    ls[...] = jnp.zeros(ls.shape, F32)
    acc[...] = jnp.zeros(acc.shape, F32)

    def step(it, carry):
        run, start, least = step_of(table, it)
        results = []
        for g in range(KV_HEADS):
            at = run * KV_HEADS + g
            kv = kvs[pl.ds(start, CHUNK), g * PAIR : (g + 1) * PAIR]
            turned = kv.T
            for h in range(GROUP):
                part = head_columns(h)
                scores = dot_back(kv, qs[at, part, :])
                scores = jnp.where(lead[...] >= least, scores, masked_score)
                before = ms[at, :, part]
                now = jnp.maximum(before, jnp.max(scores, 0, keepdims=True))
                raised = jnp.exp(scores - now)
                shrink = jnp.exp(before - now)
                total = ls[at, :, part] * shrink + jnp.sum(raised, 0, keepdims=True)
                out = dot(turned, raised.astype(BF16))[HEAD_DIM:]
                results.append((at, part, now, total, acc[at, :, part] * shrink + out))
        for at, part, now, total, out in results:
            ms[at, :, part] = now
            ls[at, :, part] = total
            acc[at, :, part] = out
        return carry

    lax.fori_loop(0, STEPS, step, 0, unroll=STEPS)
    for run in range(2):
        for g in range(KV_HEADS):
            at = run * KV_HEADS + g
            total = ls[at]
            lse_out[at] = ms[at] + jnp.log(total)
            heads = (acc[at] / total).T
            for h in range(GROUP):
                o_out[
                    run * BLOCK : (run + 1) * BLOCK,
                    (g * GROUP + h) * HEAD_DIM : (g * GROUP + h + 1) * HEAD_DIM,
                ] = heads[h * BLOCK : (h + 1) * BLOCK].astype(BF16)


def attend_back_kernel(table, q_ref, o_ref, do_ref, lse, *refs):
    pieces = refs[:8]
    dq_out, near_out, far_out, kvs, qs, dos, lead, deltas, dkvs, dqs = refs[8:]
    sort_keys(table, pieces, kvs)
    set_lead(lead)
    for run in range(2):
        load_heads(q_ref, qs, run, False)
        load_heads(do_ref, dos, run, True)
        rows = slice(run * BLOCK, (run + 1) * BLOCK)
        product = o_ref[rows, :].astype(F32) * do_ref[rows, :].astype(F32)
        turned = jnp.concatenate([product, jnp.zeros((BLOCK, HEAD_DIM), F32)], 1).T
        for g in range(KV_HEADS):
            deltas[run * KV_HEADS + g] = jnp.concatenate(
                [
                    jnp.sum(turned[h * HEAD_DIM : (h + 1) * HEAD_DIM], 0, keepdims=True)
                    for h in range(g * GROUP, (g + 1) * GROUP)
                ],
                1,
            )
    dkvs[...] = jnp.zeros(dkvs.shape, F32)
    dqs[...] = jnp.zeros(dqs.shape, F32)

    def step(it, carry):
        run, start, least = step_of(table, it)
        scores, d_probs, low_probs, d_scores, results = [], [], [], [], []
        for g in range(KV_HEADS):
            at = run * KV_HEADS + g
            kv = kvs[pl.ds(start, CHUNK), g * PAIR : (g + 1) * PAIR]
            scores.append(dot_back(kv, qs[at]))
            d_probs.append(dot_back(kv, dos[at]))
        ahead = jnp.concatenate([lead[...]] * GROUP, 1) >= least
        for g in range(KV_HEADS):
            at = run * KV_HEADS + g
            probs = jnp.exp(jnp.where(ahead, scores[g], masked_score) - lse[at])
            low_probs.append(probs.astype(BF16))
            d_scores.append((probs * (d_probs[g] - deltas[at])).astype(BF16))
        for g in range(KV_HEADS):
            at = run * KV_HEADS + g
            kv = kvs[pl.ds(start, CHUNK), g * PAIR : (g + 1) * PAIR]
            d_kv = dot(d_scores[g], qs[at]) + dot(low_probs[g], dos[at])
            results.append((at, d_kv, dot_rows(kv, d_scores[g])[:HEAD_DIM]))
        for g, (at, d_kv, d_q) in enumerate(results):
            dkvs[g, pl.ds(start, CHUNK), :] += d_kv
            dqs[at] += d_q
        return carry

    lax.fori_loop(0, STEPS, step, 0, unroll=STEPS)
    for run in range(2):
        for g in range(KV_HEADS):
            heads = (dqs[run * KV_HEADS + g] * score_scale).T
            for h in range(GROUP):
                dq_out[
                    run * BLOCK : (run + 1) * BLOCK,
                    (g * GROUP + h) * HEAD_DIM : (g * GROUP + h + 1) * HEAD_DIM,
                ] = heads[h * BLOCK : (h + 1) * BLOCK]
    for j in range(KEYS // BLOCK):
        start = pl.multiple_of(table[2 + j] * BLOCK, BLOCK)
        half = KEYS // BLOCK // 2
        out = near_out if j < half else far_out
        for g in range(KV_HEADS):
            out[(j % half) * BLOCK : (j % half + 1) * BLOCK, g * PAIR : (g + 1) * PAIR] = dkvs[
                g, pl.ds(start, BLOCK), :
            ].astype(BF16)


def attend(table, q, kv_all):
    return call(
        attend_kernel,
        [sds((ROWS, D), BF16), sds((SLOTS, 1, WIDE), F32)],
        10,
        18,
        smem=(0,),
        scratch=[
            pltpu.VMEM((KEYS, KV_HEADS * PAIR), BF16),
            pltpu.VMEM((SLOTS, WIDE, PAIR), BF16),
            pltpu.VMEM((CHUNK, BLOCK), jnp.int32),
            pltpu.VMEM((SLOTS, 1, WIDE), F32),
            pltpu.VMEM((SLOTS, 1, WIDE), F32),
            pltpu.VMEM((SLOTS, HEAD_DIM, WIDE), F32),
        ],
        flops=4 * HEADS * ROWS * 1152 * HEAD_DIM,
        bytes_accessed=4 << 20,
    )(table, q, *kv_all)


def attend_back(table, q, kv_all, o, do, lse):
    return call(
        attend_back_kernel,
        [sds((ROWS, D), F32)] + [sds((KEYS // 2, 2 * KVD), BF16)] * 2,
        13,
        26,
        smem=(0,),
        scratch=[
            pltpu.VMEM((KEYS, KV_HEADS * PAIR), BF16),
            pltpu.VMEM((SLOTS, WIDE, PAIR), BF16),
            pltpu.VMEM((SLOTS, WIDE, PAIR), BF16),
            pltpu.VMEM((CHUNK, BLOCK), jnp.int32),
            pltpu.VMEM((SLOTS, 1, WIDE), F32),
            pltpu.VMEM((KV_HEADS, KEYS, PAIR), F32),
            pltpu.VMEM((SLOTS, HEAD_DIM, WIDE), F32),
        ],
        flops=10 * HEADS * ROWS * 1152 * HEAD_DIM,
        bytes_accessed=6 << 20,
    )(table, q, o, do, lse, *kv_all)


def ring(shift):
    return [(i, (i + shift) % 4) for i in range(4)]


def ring_x(shift):
    pairs = []
    for x in range(4):
        to = (x + shift) % 4
        pairs.append(((x % 2) * 2 + x // 2, (to % 2) * 2 + to // 2))
    return pairs


SHIFTS = (1, -1, 2)


def from_x(value):
    return [value] + [lax.ppermute(value, ("xl", "xh"), ring_x(s)) for s in SHIFTS]


def from_ring(value, axis):
    return [value] + [lax.ppermute(value, axis, ring(s)) for s in SHIFTS]


def other_core(value):
    return lax.ppermute(value, "core", [(0, 1), (1, 0)])


def trade(value):
    return lax.ppermute(value, ("xl", "core"), [(0, 0), (1, 2), (2, 1), (3, 3)])


def place_of(distance):
    distance = distance % 4
    return distance ^ (distance >> 1)


def block_index():
    z, xl, xh = (lax.axis_index(name) for name in OUTER)
    block = jnp.arange(16, dtype=jnp.int32)
    along_x = place_of(xh * 2 + xl - (block % 2) * 2 - (block // 2) % 2)
    return place_of(z - block // 4) * 4 + along_x


def row_source():
    y, core = lax.axis_index("y"), lax.axis_index("core")
    rows = jnp.arange(192, dtype=jnp.int32)
    owner, j = rows // 24, rows % 24
    piece = ((owner + core) % 2) * 4 + place_of(y - owner // 2)
    return (piece * 24 + j)[:, None]


def spread_a(index, blocks):
    return call(spread_a_kernel, sds((24, A_WIDTH), BF16), 2, 12, smem=(0,))(index, blocks)


def spread_b(index, blocks, pm, pf):
    return call(spread_b_kernel, sds((24, B_WIDTH), BF16), 4, 16, smem=(0,))(index, blocks, pm, pf)


def share(near):
    return near + [other_core(piece) for piece in near]


def return_pieces(near, far, axis):
    near = (near.astype(F32) + other_core(far).astype(F32)).astype(BF16)
    step = near.shape[0] // 4
    parts = [near[i * step : (i + 1) * step] for i in range(4)]
    return [parts[0]] + [
        lax.ppermute(part, axis, ring(-s)) for part, s in zip(parts[1:], SHIFTS)
    ]


def key_table(positions):
    starts = trade(positions[0, ::BLOCK]) // BLOCK
    z, core = lax.axis_index("z"), lax.axis_index("core")
    j = np.arange(18) - 2
    shift = np.where(j < 0, 0, np.array((0,) + SHIFTS)[(j // 2) % 4]).astype(np.int32)
    far = np.where(j < 0, 0, j // 8).astype(np.int32)
    wanted = (((z - shift) % 4) * 2 + (core + far) % 2) * 2 + (j % 2).astype(np.int32)
    match = wanted[:, None] == jnp.arange(16, dtype=jnp.int32)[None, :]
    return jnp.sum(jnp.where(match, starts[None, :], 0), 1)


def angles(places):
    half_dim = HEAD_DIM // 2
    inverse = rope_base ** (-2.0 * jnp.arange(half_dim).astype(F32) / HEAD_DIM)
    turned = places.astype(F32)[:, None] * inverse[None, :]
    cosine, sine = jnp.cos(turned), jnp.sin(turned)
    return jnp.concatenate([cosine] * 4, 1), jnp.concatenate([-sine, sine] * 2, 1)


def after(value, *others):
    return lax.optimization_barrier((value, *others))[0]


def on_device(
    tokens, positions, vectors, w_query, w_key, w_value, w_out, w_gate, w_up, w_down, cotangent
):
    pm = jnp.asarray(one_hot(feature_order()), BF16)
    pf = jnp.asarray(one_hot(hidden_order()), BF16)
    pq = jnp.asarray(gain_matrix(), BF16)
    index = block_index()
    source = row_source()
    layer_second = (1, 0, 2)
    turned = (0, 2, 1)
    packs = call(pack_kernel, [sds((36, PACK), BF16)] * 2, 8, 8)(
        vectors,
        w_query.transpose(layer_second),
        w_key.transpose(turned),
        w_value.transpose(turned),
        w_out.transpose(layer_second),
        w_gate.transpose(layer_second),
        w_up.transpose(layer_second),
        w_down.transpose(turned),
    )
    table = key_table(positions)
    places = (table[:2, None] * BLOCK + jnp.arange(BLOCK)[None, :]).reshape(ROWS)
    cosine, sine = angles(places)
    x, grad = call(enter_kernel, [sds((ROWS, D), F32)] * 2, 3, 8)(
        trade(tokens[0].T), trade(cotangent[0].T), pm
    )

    blocks = jnp.concatenate(from_ring(jnp.stack(from_x(packs[0])), "z"), 0)
    blocks = after(blocks, x, table, cosine, sine, source, index)
    a_near = spread_a(index, blocks)
    b_near = spread_b(index, after(blocks, a_near), pm, pf)
    b0 = lax.all_gather(b_near, INNER, axis=0, tiled=True)
    near = from_ring(a_near, "y")
    a0 = jnp.concatenate(share(near), 0)
    blocks = jnp.stack(from_x(after(packs[1], b_near, near[1])))

    weights = []
    saved = []
    for layer in range(2):
        a, normed, q, kv, gains = call(
            pre_placed_kernel,
            [
                sds((192, A_WIDTH), BF16),
                sds((ROWS, D), BF16),
                sds((ROWS, D), BF16),
                sds((ROWS, 2 * KVD), BF16),
                sds((8, D), F32),
            ],
            6,
            16,
        )(source, a0 if layer == 0 else a1, x, pq, cosine, sine)
        near = from_ring(kv, "z")
        if layer == 0:
            blocks = jnp.concatenate(from_ring(after(blocks, q), "z"), 0)
            b_near = spread_b(index, blocks, pm, pf)
            a_near = spread_a(index, blocks)
            b1 = lax.all_gather(b_near, INNER, axis=0, tiled=True)
            a1 = jnp.concatenate(share(from_ring(after(a_near, near[1]), "y")), 0)
        kv_all = share(near)
        o, lse = attend(table, q, kv_all)
        last = layer == 1
        b = b1 if last else b0
        mid, op, nm, gate, up, hid, x_next = call(
            functools.partial(post_kernel, last),
            [
                sds((ROWS, D), F32),
                sds((ROWS, D), BF16),
                sds((ROWS, D), BF16),
                sds((ROWS, FF), BF16),
                sds((ROWS, FF), BF16),
                sds((ROWS, FF), BF16),
                sds((D, ROWS), BF16) if last else sds((ROWS, D), F32),
            ],
            5,
            28,
        )(o, x, gains, pm, b)
        weights.append((a, b))
        saved.append((x, normed, q, kv_all, gains, o, lse, mid, op, nm, gate, up, hid))
        x = x_next
    output = trade(x).T[None]

    for layer in (1, 0):
        a, b = weights[layer]
        x, normed, q, kv_all, gains, o, lse, mid, op, nm, gate, up, hid = saved[layer]
        last = layer == 0
        db, gm, do, dg2 = call(
            mlp_back_carry_kernel if last else mlp_back_kernel,
            [
                sds((192, C_WIDTH if last else B_WIDTH), BF16),
                sds((ROWS, D), F32),
                sds((ROWS, D), BF16),
                sds((1, D), F32),
            ],
            11 if last else 10,
            40,
        )(*((da,) if last else ()), grad, nm, gate, up, hid, mid, op, gains, pm, b)
        summed = lax.psum_scatter(db, INNER, scatter_dimension=0, tiled=True)
        dq, near, far = attend_back(table, q, kv_all, o, do, lse)
        parts = return_pieces(near, far, "z")
        if last:
            blocks = call(gather_first_kernel, sds((16, 36, PACK_B), BF16), 3, 16)(
                after(first, dq), pm, pf
            )
            first = lax.all_to_all(blocks, OUTER, 0, 0, tiled=True)
        else:
            first = summed
        da, grad = call(
            functools.partial(qkv_back_kernel, last),
            [sds((192, A_WIDTH), BF16), sds((D, ROWS) if last else (ROWS, D), F32)],
            16,
            20,
        )(dq, *parts, cosine, sine, normed, x, a, gains, pq, pm, gm, dg2, source)
    parts = return_pieces(da[:96], da[96:], "y")
    blocks = call(gather_last_kernel, sds((16, 36, PACK + PACK_A), BF16), 7, 20)(
        *parts, summed, pm, pf
    )
    rest = lax.all_to_all(blocks, OUTER, 0, 0, tiled=True)
    grad_tokens = trade(grad).T[None]
    outs = call(
        finish_kernel,
        [
            sds((2, 72), F32),
            sds((36, 2, 72), F32),
            sds((2, 24, 36), F32),
            sds((2, 24, 36), F32),
            sds((36, 2, 72), F32),
            sds((36, 2, 192), F32),
            sds((36, 2, 192), F32),
            sds((2, 72, 96), F32),
        ],
        2,
        16,
    )(first, rest)
    order = (None, layer_second, turned, turned, layer_second, layer_second, layer_second, turned)
    outs = [out if axes is None else out.transpose(axes) for out, axes in zip(outs, order)]
    return (output, grad_tokens, *outs)


def solution(mesh):
    fine = Mesh(np.asarray(mesh.devices).reshape(SIZES), AXES)
    split = P(None, FSDP, CTX)
    rows = P(FSDP, CTX, None)
    return jax.shard_map(
        on_device,
        mesh=fine,
        in_specs=(rows, P(FSDP, None), P(None, FSDP)) + (split,) * 7 + (rows,),
        out_specs=(rows, rows, P(None, FSDP)) + (split,) * 7,
        check_vma=False,
    )
```

```python
import functools

import jax
import jax.numpy as jnp
import numpy as np
from jax import lax
from jax.experimental import pallas as pl
from jax.experimental.pallas import tpu as pltpu
from jax.sharding import Mesh
from jax.sharding import PartitionSpec as P

D = 576
HEADS = 9
KV_HEADS = 3
HEAD_DIM = 64
GROUP = HEADS // KV_HEADS
FF = 1536
ROWS = 256
BLOCK = 128
KEYS = 2048
KVD = KV_HEADS * HEAD_DIM
HALF_FF = FF // 2

rope_base = 10000.0
norm_eps = 1e-05
masked_score = -1e30
score_scale = HEAD_DIM ** (-0.5)

F32 = jnp.float32
BF16 = jnp.bfloat16

AXES = ("z", "xl", "xh", "y", "core")
SIZES = (4, 2, 2, 4, 2)
CTX = ("z", "xl")
FSDP = ("xh", "y", "core")
INNER = ("y", "core")
OUTER = ("z", "xl", "xh")

PACK = 896
PACK_A = 128
PACK_B = PACK - PACK_A
PK_Q, PK_K, PK_V, PK_GAIN = 0, 72, 96, 120
PK_O, PK_G, PK_U, PK_D = 128, 200, 392, 584

A_STEP = 1024
A_WIDTH = 3 * A_STEP
B_STEP = 2 * FF
B_DOWN = 3 * B_STEP
B_OUT = B_DOWN + 8 * 512
B_DOWN_TAIL = B_OUT + 3 * 512
B_OUT_TAIL = B_DOWN_TAIL + 8 * 64
B_WIDTH = B_OUT_TAIL + 256

C_WIDTH = B_WIDTH + A_WIDTH

BYTES_PER_MICRO = 3.4e6


def feature_order():
    n = np.arange(D)
    owner, i = n // 36, n % 36
    xh, yc = owner // 8, owner % 8
    local = xh * 36 + i
    return (local // 24) * 192 + yc * 24 + local % 24


def hidden_order():
    n = np.arange(HALF_FF)
    yc, i = n // 96, n % 96
    return (i // 24) * 192 + yc * 24 + i % 24


def one_hot(places):
    size = len(places)
    out = np.zeros((size, size), np.float32)
    out[np.arange(size), places] = 1.0
    return out


def gain_matrix():
    n = np.arange(D)
    yc, local = n // 72, n % 72
    gathered = (local // 24) * 192 + yc * 24 + local % 24
    out = np.zeros((D, D), np.float32)
    out[gathered, feature_order()] = 1.0
    return out


def dot(left, right):
    return lax.dot_general(left, right, (((1,), (0,)), ((), ())), preferred_element_type=F32)


def dot_rows(left, right):
    return lax.dot_general(left, right, (((0,), (0,)), ((), ())), preferred_element_type=F32)


def dot_back(left, right):
    return lax.dot_general(left, right, (((1,), (1,)), ((), ())), preferred_element_type=F32)


def call(kernel, out_shape, n_in, micros, smem=(), scratch=()):
    in_specs = [
        pl.BlockSpec(memory_space=pltpu.SMEM if i in smem else pltpu.VMEM) for i in range(n_in)
    ]
    many = isinstance(out_shape, (list, tuple))
    out_spec = pl.BlockSpec(memory_space=pltpu.VMEM)
    return pl.pallas_call(
        kernel,
        out_shape=out_shape,
        in_specs=in_specs,
        out_specs=[out_spec] * len(out_shape) if many else out_spec,
        scratch_shapes=list(scratch),
        compiler_params=pltpu.CompilerParams(vmem_limit_bytes=56 << 20),
        cost_estimate=pl.CostEstimate(
            flops=0, bytes_accessed=int(micros * BYTES_PER_MICRO), transcendentals=0
        ),
    )


def sds(shape, dtype):
    return jax.ShapeDtypeStruct(shape, dtype)


def eye(size):
    rows = lax.broadcasted_iota(jnp.int32, (size, size), 0)
    cols = lax.broadcasted_iota(jnp.int32, (size, size), 1)
    return jnp.where(rows == cols, 1.0, 0.0).astype(F32)


def pack_kernel(vec, wq, wk, wv, wo, wg, wu, wd, out):
    diagonal = eye(36)
    for layer in range(2):
        gains = vec[layer : layer + 1, :].astype(F32)
        first = jnp.sum(diagonal * gains[:, :36], 1, keepdims=True)
        second = jnp.sum(diagonal * gains[:, 36:72], 1, keepdims=True)
        down = wd[layer].astype(F32).T
        block = jnp.concatenate(
            [
                wq[...].astype(F32)[:, layer],
                wk[layer].astype(F32).T,
                wv[layer].astype(F32).T,
                first,
                second,
                jnp.zeros((36, 6), F32),
                wo[...].astype(F32)[:, layer],
                wg[...].astype(F32)[:, layer],
                wu[...].astype(F32)[:, layer],
                down[:36],
                down[36:72],
                jnp.concatenate([down[72:96], jnp.zeros((12, 72), F32)], 0),
                jnp.zeros((36, 96), F32),
            ],
            1,
        ).astype(BF16)
        out[:, layer * PACK_A : (layer + 1) * PACK_A] = block[:, :PACK_A]
        low = 2 * PACK_A + layer * PACK_B
        out[:, low : low + PACK_B] = block[:, PACK_A:]


def part_of(index, blocks, c, xh, low, high):
    return blocks[index[c * 2 + xh], :, low:high].astype(F32)


def wide_of(index, blocks, low, high):
    halves = [
        jnp.concatenate([part_of(index, blocks, c, xh, low, high) for c in range(8)], 1)
        for xh in range(2)
    ]
    return jnp.concatenate(halves, 0)


def spread_a_kernel(index, r0, r1, r2, r3, out0, out1, blocks):
    for i, piece in enumerate((r0, r1, r2, r3)):
        blocks[4 * i : 4 * i + 4] = piece[:, :, : 2 * PACK_A]
    part = functools.partial(part_of, index, blocks)
    wide = functools.partial(wide_of, index, blocks)
    for layer, out in enumerate((out0, out1)):
        low = layer * PACK_A
        gains = []
        for xh in range(2):
            both = part(0, xh, low + PK_GAIN, low + PK_GAIN + 2)
            gains.append(jnp.concatenate([both[:, :1], both[:, 1:]], 0))
        a = jnp.concatenate(
            [
                wide(low + PK_Q, low + PK_K),
                wide(low + PK_K, low + PK_V),
                wide(low + PK_V, low + PK_GAIN),
            ]
            + gains
            + [jnp.zeros((72, 62), F32)],
            1,
        )
        for p in range(3):
            out[:, p * A_STEP : (p + 1) * A_STEP] = a[24 * p : 24 * p + 24].astype(BF16)


def spread_b_kernel(first, index, r0, r1, r2, r3, pm, pf, b_out, blocks):
    for i, piece in enumerate((r0, r1, r2, r3)):
        blocks[4 * i : 4 * i + 4] = piece[:, :, first : first + PACK_B]
    part = functools.partial(part_of, index, blocks)
    wide = functools.partial(wide_of, index, blocks)
    out = dot(wide(0, PK_G - PK_O).astype(BF16), pm[...])
    for p in range(3):
        piece = out[24 * p : 24 * p + 24].astype(BF16)
        b_out[:, B_OUT + p * 512 : B_OUT + (p + 1) * 512] = piece[:, :512]
        b_out[:, B_OUT_TAIL + p * 64 : B_OUT_TAIL + (p + 1) * 64] = piece[:, 512:]
    b_out[:, B_OUT_TAIL + 192 :] = jnp.zeros((24, 64), BF16)
    for shift, low, high in ((0, PK_G - PK_O, PK_U - PK_O), (FF, PK_U - PK_O, PK_D - PK_O)):
        natural = wide(low, high).astype(BF16)
        for half in range(2):
            placed = dot(natural[:, half * HALF_FF : (half + 1) * HALF_FF], pf[...])
            for p in range(3):
                start = p * B_STEP + shift + half * HALF_FF
                b_out[:, start : start + HALF_FF] = placed[24 * p : 24 * p + 24].astype(BF16)
    down_at = PK_D - PK_O
    for xh in range(2):
        pieces = []
        for c in range(8):
            pieces.append(
                jnp.concatenate(
                    [
                        part(c, xh, down_at, down_at + 72),
                        part(c, xh, down_at + 72, down_at + 144),
                        part(c, xh, down_at + 144, down_at + 216)[:24],
                    ],
                    0,
                )
            )
        down = dot(jnp.concatenate(pieces, 1).astype(BF16), pm[...])
        for i in range(4):
            p = xh * 4 + i
            piece = down[24 * i : 24 * i + 24].astype(BF16)
            b_out[:, B_DOWN + p * 512 : B_DOWN + (p + 1) * 512] = piece[:, :512]
            b_out[:, B_DOWN_TAIL + p * 64 : B_DOWN_TAIL + (p + 1) * 64] = piece[:, 512:]


def gathered_a(a, out, lanes):
    a72 = jnp.concatenate([a[:, p * A_STEP : (p + 1) * A_STEP] for p in range(3)], 0)
    for xh in range(2):
        rows = slice(xh * 36, xh * 36 + 36)
        gain = a72[:, 960 + xh : 961 + xh]
        for c in range(8):
            out[c * 2 + xh, :, lanes] = jnp.concatenate(
                [
                    a72[rows, c * 72 : c * 72 + 72],
                    a72[rows, 576 + c * 24 : 600 + c * 24],
                    a72[rows, 768 + c * 24 : 792 + c * 24],
                    gain[:36],
                    gain[36:72],
                    jnp.zeros((36, 6), F32),
                ],
                1,
            ).astype(BF16)


def gathered_b(b, pm, pf, out, lanes):
    o72 = jnp.concatenate(
        [
            jnp.concatenate(
                [
                    b[:, B_OUT + p * 512 : B_OUT + (p + 1) * 512].astype(F32),
                    b[:, B_OUT_TAIL + p * 64 : B_OUT_TAIL + (p + 1) * 64].astype(F32),
                ],
                1,
            )
            for p in range(3)
        ],
        0,
    )
    o72 = dot_back(o72.astype(BF16), pm[...])
    sides = []
    for shift in (0, FF):
        halves = []
        for half in range(2):
            low = shift + half * HALF_FF
            stacked = jnp.concatenate(
                [
                    b[:, p * B_STEP + low : p * B_STEP + low + HALF_FF].astype(F32)
                    for p in range(3)
                ],
                0,
            )
            halves.append(dot_back(stacked.astype(BF16), pf[...]))
        sides.append(jnp.concatenate(halves, 1))
    for xh in range(2):
        down = jnp.concatenate(
            [
                jnp.concatenate(
                    [
                        b[:, B_DOWN + p * 512 : B_DOWN + (p + 1) * 512].astype(F32),
                        b[:, B_DOWN_TAIL + p * 64 : B_DOWN_TAIL + (p + 1) * 64].astype(F32),
                    ],
                    1,
                )
                for p in range(xh * 4, xh * 4 + 4)
            ],
            0,
        )
        down = dot_back(down.astype(BF16), pm[...])
        rows = slice(xh * 36, xh * 36 + 36)
        for c in range(8):
            cols = slice(c * 72, c * 72 + 72)
            piece = down[:, cols]
            out[c * 2 + xh, :, lanes] = jnp.concatenate(
                [
                    o72[rows, cols],
                    sides[0][rows, c * 192 : c * 192 + 192],
                    sides[1][rows, c * 192 : c * 192 + 192],
                    piece[:36],
                    piece[36:72],
                    jnp.concatenate([piece[72:96], jnp.zeros((12, 72), F32)], 0),
                    jnp.zeros((36, 96), F32),
                ],
                1,
            ).astype(BF16)


def gather_first_kernel(b, pm, pf, out):
    gathered_b(b, pm, pf, out, slice(0, PACK_B))


def gather_last_kernel(a0, a1, a2, a3, a4, c, pm, pf, out):
    a = a0[...].astype(F32)
    for ref in (a1, a2, a3, a4):
        a = a + ref[...].astype(F32)
    gathered_a(a, out, slice(0, PACK_A))
    gathered_b(c, pm, pf, out, slice(PACK_A, PACK))
    gathered_a(c[:, B_WIDTH:].astype(F32), out, slice(PACK, PACK + PACK_A))


def finish_kernel(first_ref, last_ref, vec, wq, wk, wv, wo, wg, wu, wd):
    diagonal = eye(36)

    def added(ref, low, high):
        total = ref[0, :, low:high].astype(F32)
        for i in range(1, 16):
            total = total + ref[i, :, low:high].astype(F32)
        return total

    totals = (
        added(last_ref, 0, PACK),
        jnp.concatenate([added(last_ref, PACK, PACK + PACK_A), added(first_ref, 0, PACK_B)], 1),
    )
    for layer, total in enumerate(totals):
        wq[:, layer, :] = total[:, PK_Q:PK_K]
        wk[layer] = total[:, PK_K:PK_V].T
        wv[layer] = total[:, PK_V:PK_GAIN].T
        wo[:, layer, :] = total[:, PK_O:PK_G]
        first = jnp.sum(diagonal * total[:, PK_GAIN : PK_GAIN + 1], 0, keepdims=True)
        second = jnp.sum(diagonal * total[:, PK_GAIN + 1 : PK_GAIN + 2], 0, keepdims=True)
        vec[layer : layer + 1, :] = jnp.concatenate([first, second], 1)
        wg[:, layer, :] = total[:, PK_G:PK_U]
        wu[:, layer, :] = total[:, PK_U:PK_D]
        wd[layer] = jnp.concatenate(
            [
                total[:, PK_D : PK_D + 72],
                total[:, PK_D + 72 : PK_D + 144],
                total[:24, PK_D + 144 : PK_D + 216],
            ],
            0,
        ).T


def swap_halves(tile):
    lane = lax.broadcasted_iota(jnp.int32, tile.shape, 1) % HEAD_DIM
    return jnp.where(
        lane < HEAD_DIM // 2,
        pltpu.roll(tile, 128 - HEAD_DIM // 2, 1),
        pltpu.roll(tile, HEAD_DIM // 2, 1),
    )


def enter_kernel(traded, pm, x_out, g_out):
    x_out[...] = dot_rows(traded[:D, :], pm[...])
    g_out[...] = dot_rows(traded[D : 2 * D, :], pm[...])


def place_rows(source):
    lane = lax.broadcasted_iota(jnp.int32, (192, 192), 1)
    return jnp.where(lane == source[...], 1.0, 0.0).astype(BF16)


def pre_placed_kernel(source, a_in, x_ref, pq, cosine, sine, a, normed_out, q_out, kv_out, gains_out):
    a[...] = dot(place_rows(source), a_in[...]).astype(BF16)
    pre_kernel(x_ref, a, pq, cosine, sine, normed_out, q_out, kv_out, gains_out)


def pre_kernel(x_ref, a, pq, cosine, sine, normed_out, q_out, kv_out, gains_out):
    gains = dot_rows(a[:, 896:1024], pq[0:192, :])
    for p in range(1, 3):
        gains = gains + dot_rows(
            a[:, p * A_STEP + 896 : (p + 1) * A_STEP], pq[p * 192 : (p + 1) * 192, :]
        )
    gains = gains[64:72]
    gains_out[...] = gains
    x = x_ref[...]
    inverse = lax.rsqrt(jnp.mean(x * x, -1, keepdims=True) + norm_eps)
    normed = (x * inverse * gains[0:1]).astype(BF16)
    normed_out[...] = normed
    lin = dot(normed[:, :192], a[:, :A_STEP])
    for p in range(1, 3):
        lin = lin + dot(
            normed[:, p * 192 : (p + 1) * 192], a[:, p * A_STEP : (p + 1) * A_STEP]
        )
    turned = []
    for t in range(6):
        tile = lin[:, t * 128 : (t + 1) * 128]
        turned.append(tile * cosine[...] + swap_halves(tile) * sine[...])
    turned = jnp.concatenate(turned, 1)
    q_out[...] = (turned[:, :D] * score_scale).astype(BF16)
    for g in range(KV_HEADS):
        part = slice(g * HEAD_DIM, (g + 1) * HEAD_DIM)
        kv_out[:, g * PAIR : (g + 1) * PAIR] = jnp.concatenate(
            [turned[:, D:768][:, part], lin[:, 768:960][:, part]], 1
        ).astype(BF16)


def weight_back(left, b, main, tail, p):
    return dot_back(left[:, :512], b[:, main + p * 512 : main + (p + 1) * 512]) + dot_back(
        left[:, 512:], b[:, tail + p * 64 : tail + (p + 1) * 64]
    )


def post_kernel(last, o_ref, x_ref, gains, pm, b, mid_out, op_out, nm_out, gate_out, up_out, hid_out, x_out):
    op = dot(o_ref[...], pm[...]).astype(BF16)
    op_out[...] = op

    def through(left, main, tail, count):
        wide = None
        narrow = None
        for p in range(count):
            piece = left[:, p * 192 : (p + 1) * 192]
            one = dot(piece, b[:, main + p * 512 : main + (p + 1) * 512])
            two = dot(piece, b[:, tail + p * 64 : tail + (p + 1) * 64])
            wide = one if wide is None else wide + one
            narrow = two if narrow is None else narrow + two
        return jnp.concatenate([wide, narrow], 1)

    mid = x_ref[...] + through(op, B_OUT, B_OUT_TAIL, 3)
    mid_out[...] = mid
    inverse = lax.rsqrt(jnp.mean(mid * mid, -1, keepdims=True) + norm_eps)
    nm = (mid * inverse * gains[1:2, :]).astype(BF16)
    nm_out[...] = nm
    gate = dot(nm[:, :192], b[:, :FF])
    up = dot(nm[:, :192], b[:, FF : 2 * FF])
    for p in range(1, 3):
        piece = nm[:, p * 192 : (p + 1) * 192]
        gate = gate + dot(piece, b[:, p * B_STEP : p * B_STEP + FF])
        up = up + dot(piece, b[:, p * B_STEP + FF : (p + 1) * B_STEP])
    gate_out[...] = gate.astype(BF16)
    up_out[...] = up.astype(BF16)
    hid = (gate / (1.0 + jnp.exp(-gate)) * up).astype(BF16)
    hid_out[...] = hid
    out = mid + through(hid, B_DOWN, B_DOWN_TAIL, 8)
    if last:
        x_out[...] = dot_back(pm[...], out.astype(BF16)).astype(BF16)
    else:
        x_out[...] = out


def norm_back(dy, v, gain):
    inverse = lax.rsqrt(jnp.mean(v * v, -1, keepdims=True) + norm_eps)
    scaled = dy * gain
    back = inverse * scaled - v * (
        inverse * inverse * inverse * jnp.mean(scaled * v, -1, keepdims=True)
    )
    return back, jnp.sum(dy * v * inverse, 0, keepdims=True)


def mlp_back_carry_kernel(da, *refs):
    db = refs[10]
    db[:, B_WIDTH:] = da[...]
    mlp_back_kernel(*refs)


def mlp_back_kernel(
    g_ref, nm, gate_ref, up_ref, hid, mid, op, gains, pm, b, db, gm_out, do_out, dg_out
):
    g = g_ref[...]
    gb = g.astype(BF16)
    dh = []
    for p in range(8):
        piece = dot_rows(hid[:, p * 192 : (p + 1) * 192], gb)
        db[:, B_DOWN + p * 512 : B_DOWN + (p + 1) * 512] = piece[:, :512].astype(BF16)
        db[:, B_DOWN_TAIL + p * 64 : B_DOWN_TAIL + (p + 1) * 64] = piece[:, 512:].astype(BF16)
        dh.append(weight_back(gb, b, B_DOWN, B_DOWN_TAIL, p))
    dh = jnp.concatenate(dh, 1)
    gate = gate_ref[...].astype(F32)
    up = up_ref[...].astype(F32)
    sig = 1.0 / (1.0 + jnp.exp(-gate))
    d_gate = (dh * up * sig * (1.0 + gate * (1.0 - sig))).astype(BF16)
    d_up = (dh * (gate * sig)).astype(BF16)
    dnm = []
    for p in range(3):
        piece = nm[:, p * 192 : (p + 1) * 192]
        low = p * B_STEP
        db[:, low : low + FF] = dot_rows(piece, d_gate).astype(BF16)
        db[:, low + FF : low + 2 * FF] = dot_rows(piece, d_up).astype(BF16)
        dnm.append(
            dot_back(d_gate, b[:, low : low + FF]) + dot_back(d_up, b[:, low + FF : low + 2 * FF])
        )
    back, gain_grad = norm_back(jnp.concatenate(dnm, 1), mid[...], gains[1:2, :])
    dg_out[...] = gain_grad
    gm = g + back
    gm_out[...] = gm
    gmb = gm.astype(BF16)
    dop = []
    for p in range(3):
        piece = dot_rows(op[:, p * 192 : (p + 1) * 192], gmb)
        db[:, B_OUT + p * 512 : B_OUT + (p + 1) * 512] = piece[:, :512].astype(BF16)
        db[:, B_OUT_TAIL + p * 64 : B_OUT_TAIL + (p + 1) * 64] = piece[:, 512:].astype(BF16)
        dop.append(weight_back(gmb, b, B_OUT, B_OUT_TAIL, p))
    db[:, B_OUT_TAIL + 192 : B_WIDTH] = jnp.zeros((192, 64), BF16)
    do_out[...] = dot_back(jnp.concatenate(dop, 1).astype(BF16), pm[...]).astype(BF16)


def qkv_back_kernel(
    last,
    dq,
    kv0,
    kv1,
    kv2,
    kv3,
    kv4,
    cosine,
    sine,
    normed,
    x_ref,
    a,
    gains,
    pq,
    pm,
    gm,
    dg2,
    source,
    x_out,
    *da_refs,
):
    da = da_refs[-1]
    dkv = kv0[...].astype(F32)
    for ref in (kv1, kv2, kv3, kv4):
        dkv = dkv + ref[...].astype(F32)
    d_key = [dkv[:, g * PAIR : g * PAIR + HEAD_DIM] for g in range(KV_HEADS)]
    d_value = [dkv[:, g * PAIR + HEAD_DIM : (g + 1) * PAIR] for g in range(KV_HEADS)]
    rot = jnp.concatenate([dq[...]] + d_key, 1)
    turned = []
    for t in range(6):
        tile = rot[:, t * 128 : (t + 1) * 128]
        turned.append(tile * cosine[...] - swap_halves(tile) * sine[...])
    dqkv = jnp.concatenate(turned + d_value + [jnp.zeros((ROWS, 64), F32)], 1).astype(BF16)
    dn = []
    for p in range(3):
        low = p * A_STEP
        da[:, low : low + A_STEP] = dot_rows(
            normed[:, p * 192 : (p + 1) * 192], dqkv
        ).astype(BF16)
        dn.append(dot_back(dqkv, a[:, low : low + A_STEP]))
    x = x_ref[...]
    back, dg1 = norm_back(jnp.concatenate(dn, 1), x, gains[0:1, :])
    rows = lax.broadcasted_iota(jnp.int32, (64, D), 0)
    stacked = jnp.where(rows == 0, dg1, jnp.where(rows == 1, dg2[...], 0.0)).astype(BF16)
    placed = dot_back(pq[...], stacked).astype(BF16)
    for p in range(3):
        da[:, p * A_STEP + 960 : (p + 1) * A_STEP] = placed[p * 192 : (p + 1) * 192]
    out = gm[...] + back
    if last:
        x_out[...] = dot_back(pm[...], out.astype(BF16)).astype(BF16)
        placed = dot_rows(place_rows(source), da[...])
        for i, ref in enumerate(da_refs[:8]):
            ref[...] = placed[i * 24 : (i + 1) * 24].astype(BF16)
    else:
        x_out[...] = out


PAIR = 2 * HEAD_DIM
WIDE = GROUP * BLOCK
CHUNK = 256
STEPS = KEYS // CHUNK + 1
SLOTS = 2 * KV_HEADS


def load_heads(ref, scratch, run, upper):
    zero = jnp.zeros((WIDE, HEAD_DIM), BF16)
    for g in range(KV_HEADS):
        heads = jnp.concatenate(
            [
                ref[
                    run * BLOCK : (run + 1) * BLOCK,
                    (g * GROUP + h) * HEAD_DIM : (g * GROUP + h + 1) * HEAD_DIM,
                ]
                for h in range(GROUP)
            ],
            0,
        )
        both = [zero, heads] if upper else [heads, zero]
        scratch[run * KV_HEADS + g] = jnp.concatenate(both, 1)


def sort_keys(table, pieces, kvs):
    for j in range(KEYS // BLOCK):
        start = pl.multiple_of(table[2 + j] * BLOCK, BLOCK)
        kvs[pl.ds(start, BLOCK), :] = pieces[j // 2][(j % 2) * BLOCK : (j % 2 + 1) * BLOCK, :]


def set_lead(lead):
    key = lax.broadcasted_iota(jnp.int32, (CHUNK, BLOCK), 0)
    row = lax.broadcasted_iota(jnp.int32, (CHUNK, BLOCK), 1)
    lead[...] = row - key


def head_columns(h):
    return slice(h * BLOCK, (h + 1) * BLOCK)


def step_of(table, it):
    first = (table[0] + 2) // 2
    second = it >= first
    run = jnp.where(second, 1, 0)
    chunk = jnp.where(second, it - first, it)
    block = jnp.where(second, table[1], table[0])
    return run, pl.multiple_of(chunk * CHUNK, CHUNK), chunk * CHUNK - block * BLOCK


def attend_kernel(table, q_ref, *refs):
    pieces, (o_out, lse_out, kvs, qs, lead, ms, ls, acc) = refs[:8], refs[8:]
    sort_keys(table, pieces, kvs)
    load_heads(q_ref, qs, 0, False)
    load_heads(q_ref, qs, 1, False)
    set_lead(lead)
    ms[...] = jnp.full(ms.shape, masked_score, F32)
    ls[...] = jnp.zeros(ls.shape, F32)
    acc[...] = jnp.zeros(acc.shape, F32)

    def step(it, carry):
        run, start, least = step_of(table, it)
        results = []
        for g in range(KV_HEADS):
            at = run * KV_HEADS + g
            kv = kvs[pl.ds(start, CHUNK), g * PAIR : (g + 1) * PAIR]
            turned = kv.T
            for h in range(GROUP):
                part = head_columns(h)
                scores = dot_back(kv, qs[at, part, :])
                scores = jnp.where(lead[...] >= least, scores, masked_score)
                before = ms[at, :, part]
                now = jnp.maximum(before, jnp.max(scores, 0, keepdims=True))
                raised = jnp.exp(scores - now)
                shrink = jnp.exp(before - now)
                total = ls[at, :, part] * shrink + jnp.sum(raised, 0, keepdims=True)
                out = dot(turned, raised.astype(BF16))[HEAD_DIM:]
                results.append((at, part, now, total, acc[at, :, part] * shrink + out))
        for at, part, now, total, out in results:
            ms[at, :, part] = now
            ls[at, :, part] = total
            acc[at, :, part] = out
        return carry

    lax.fori_loop(0, STEPS, step, 0, unroll=STEPS)
    for run in range(2):
        for g in range(KV_HEADS):
            at = run * KV_HEADS + g
            total = ls[at]
            lse_out[at] = ms[at] + jnp.log(total)
            heads = (acc[at] / total).T
            for h in range(GROUP):
                o_out[
                    run * BLOCK : (run + 1) * BLOCK,
                    (g * GROUP + h) * HEAD_DIM : (g * GROUP + h + 1) * HEAD_DIM,
                ] = heads[h * BLOCK : (h + 1) * BLOCK].astype(BF16)


def attend_back_kernel(table, q_ref, o_ref, do_ref, lse, *refs):
    pieces = refs[:8]
    dq_out, outs, (kvs, qs, dos, lead, deltas, dkvs, dqs) = refs[8], refs[9:17], refs[17:]
    sort_keys(table, pieces, kvs)
    set_lead(lead)
    for run in range(2):
        load_heads(q_ref, qs, run, False)
        load_heads(do_ref, dos, run, True)
        rows = slice(run * BLOCK, (run + 1) * BLOCK)
        product = o_ref[rows, :].astype(F32) * do_ref[rows, :].astype(F32)
        turned = jnp.concatenate([product, jnp.zeros((BLOCK, HEAD_DIM), F32)], 1).T
        for g in range(KV_HEADS):
            deltas[run * KV_HEADS + g] = jnp.concatenate(
                [
                    jnp.sum(turned[h * HEAD_DIM : (h + 1) * HEAD_DIM], 0, keepdims=True)
                    for h in range(g * GROUP, (g + 1) * GROUP)
                ],
                1,
            )
    dkvs[...] = jnp.zeros(dkvs.shape, F32)
    dqs[...] = jnp.zeros(dqs.shape, F32)

    def step(it, carry):
        run, start, least = step_of(table, it)
        scores, d_probs, low_probs, d_scores, results = [], [], [], [], []
        for g in range(KV_HEADS):
            at = run * KV_HEADS + g
            kv = kvs[pl.ds(start, CHUNK), g * PAIR : (g + 1) * PAIR]
            scores.append(dot_back(kv, qs[at]))
            d_probs.append(dot_back(kv, dos[at]))
        ahead = jnp.concatenate([lead[...]] * GROUP, 1) >= least
        for g in range(KV_HEADS):
            at = run * KV_HEADS + g
            probs = jnp.exp(jnp.where(ahead, scores[g], masked_score) - lse[at])
            low_probs.append(probs.astype(BF16))
            d_scores.append((probs * (d_probs[g] - deltas[at])).astype(BF16))
        for g in range(KV_HEADS):
            at = run * KV_HEADS + g
            kv = kvs[pl.ds(start, CHUNK), g * PAIR : (g + 1) * PAIR]
            d_kv = dot(d_scores[g], qs[at]) + dot(low_probs[g], dos[at])
            results.append((at, d_kv, dot_rows(kv, d_scores[g])[:HEAD_DIM]))
        for g, (at, d_kv, d_q) in enumerate(results):
            dkvs[g, pl.ds(start, CHUNK), :] += d_kv
            dqs[at] += d_q
        return carry

    lax.fori_loop(0, STEPS, step, 0, unroll=STEPS)
    for run in range(2):
        for g in range(KV_HEADS):
            heads = (dqs[run * KV_HEADS + g] * score_scale).T
            for h in range(GROUP):
                dq_out[
                    run * BLOCK : (run + 1) * BLOCK,
                    (g * GROUP + h) * HEAD_DIM : (g * GROUP + h + 1) * HEAD_DIM,
                ] = heads[h * BLOCK : (h + 1) * BLOCK]
    for j in range(KEYS // BLOCK):
        start = pl.multiple_of(table[2 + j] * BLOCK, BLOCK)
        rows = slice((j % 2) * BLOCK, (j % 2 + 1) * BLOCK)
        for g in range(KV_HEADS):
            outs[j // 2][rows, g * PAIR : (g + 1) * PAIR] = dkvs[
                g, pl.ds(start, BLOCK), :
            ].astype(BF16)


def attend(table, q, kv_all):
    return call(
        attend_kernel,
        [sds((ROWS, D), BF16), sds((SLOTS, 1, WIDE), F32)],
        10,
        6.9,
        smem=(0,),
        scratch=[
            pltpu.VMEM((KEYS, KV_HEADS * PAIR), BF16),
            pltpu.VMEM((SLOTS, WIDE, PAIR), BF16),
            pltpu.VMEM((CHUNK, BLOCK), jnp.int32),
            pltpu.VMEM((SLOTS, 1, WIDE), F32),
            pltpu.VMEM((SLOTS, 1, WIDE), F32),
            pltpu.VMEM((SLOTS, HEAD_DIM, WIDE), F32),
        ],
    )(table, q, *kv_all)


def attend_back(table, q, kv_all, o, do, lse):
    return call(
        attend_back_kernel,
        [sds((ROWS, D), F32)] + [sds((ROWS, 2 * KVD), BF16)] * 8,
        13,
        11.3,
        smem=(0,),
        scratch=[
            pltpu.VMEM((KEYS, KV_HEADS * PAIR), BF16),
            pltpu.VMEM((SLOTS, WIDE, PAIR), BF16),
            pltpu.VMEM((SLOTS, WIDE, PAIR), BF16),
            pltpu.VMEM((CHUNK, BLOCK), jnp.int32),
            pltpu.VMEM((SLOTS, 1, WIDE), F32),
            pltpu.VMEM((KV_HEADS, KEYS, PAIR), F32),
            pltpu.VMEM((SLOTS, HEAD_DIM, WIDE), F32),
        ],
    )(table, q, o, do, lse, *kv_all)


def ring(shift):
    return [(i, (i + shift) % 4) for i in range(4)]


def ring_x(shift):
    pairs = []
    for x in range(4):
        to = (x + shift) % 4
        pairs.append(((x % 2) * 2 + x // 2, (to % 2) * 2 + to // 2))
    return pairs


SHIFTS = (1, -1, 2)


def from_x(value):
    return [value] + [lax.ppermute(value, ("xl", "xh"), ring_x(s)) for s in SHIFTS]


def from_ring(value, axis):
    return [value] + [lax.ppermute(value, axis, ring(s)) for s in SHIFTS]


def other_core(value):
    return lax.ppermute(value, "core", [(0, 1), (1, 0)])


def trade(value):
    return lax.ppermute(value, ("xl", "core"), [(0, 0), (1, 2), (2, 1), (3, 3)])


def place_of(distance):
    distance = distance % 4
    return distance ^ (distance >> 1)


def block_index():
    z, xl, xh = (lax.axis_index(name) for name in OUTER)
    block = jnp.arange(16, dtype=jnp.int32)
    along_x = place_of(xh * 2 + xl - (block % 2) * 2 - (block // 2) % 2)
    return place_of(z - block // 4) * 4 + along_x


def row_source():
    y, core = lax.axis_index("y"), lax.axis_index("core")
    rows = jnp.arange(192, dtype=jnp.int32)
    owner, j = rows // 24, rows % 24
    piece = ((owner + core) % 2) * 4 + place_of(y - owner // 2)
    return (piece * 24 + j)[:, None]


def spread_a(index, blocks):
    return call(
        spread_a_kernel,
        [sds((24, A_WIDTH), BF16)] * 2,
        5,
        3.0,
        smem=(0,),
        scratch=[pltpu.VMEM((16, 36, 2 * PACK_A), BF16)],
    )(index, *blocks)


def spread_b(first, index, blocks, pm, pf):
    return call(
        functools.partial(spread_b_kernel, first),
        sds((24, B_WIDTH), BF16),
        7,
        4.3,
        smem=(0,),
        scratch=[pltpu.VMEM((16, 36, PACK_B), BF16)],
    )(index, *blocks, pm, pf)


def share(near):
    return near + [other_core(piece) for piece in near]


def return_pieces(near, far, axis):
    far = [other_core(piece) for piece in far]
    both = [(n.astype(F32) + f.astype(F32)).astype(BF16) for n, f in zip(near[1:], far[1:])]
    back = [lax.ppermute(piece, axis, ring(-s)) for piece, s in zip(both, SHIFTS)]
    return [near[0], far[0]] + back


def key_table(starts):
    z, core = lax.axis_index("z"), lax.axis_index("core")
    j = np.arange(18) - 2
    shift = np.where(j < 0, 0, np.array((0,) + SHIFTS)[(j // 2) % 4]).astype(np.int32)
    far = np.where(j < 0, 0, j // 8).astype(np.int32)
    wanted = (((z - shift) % 4) * 2 + (core + far) % 2) * 2 + (j % 2).astype(np.int32)
    match = wanted[:, None] == jnp.arange(16, dtype=jnp.int32)[None, :]
    return jnp.sum(jnp.where(match, starts[None, :], 0), 1)


def angles(places):
    half_dim = HEAD_DIM // 2
    inverse = rope_base ** (-2.0 * jnp.arange(half_dim).astype(F32) / HEAD_DIM)
    turned = places.astype(F32)[:, None] * inverse[None, :]
    cosine, sine = jnp.cos(turned), jnp.sin(turned)
    return jnp.concatenate([cosine] * 4, 1), jnp.concatenate([-sine, sine] * 2, 1)


def after(value, *others):
    return lax.optimization_barrier((value, *others))[0]


def on_device(
    tokens, positions, vectors, w_query, w_key, w_value, w_out, w_gate, w_up, w_down, cotangent
):
    pm = jnp.asarray(one_hot(feature_order()), BF16)
    pf = jnp.asarray(one_hot(hidden_order()), BF16)
    pq = jnp.asarray(gain_matrix(), BF16)
    index = block_index()
    source = row_source()
    layer_second = (1, 0, 2)
    turned = (0, 2, 1)
    pack = call(pack_kernel, sds((36, 2 * PACK), BF16), 8, 1.9)(
        vectors,
        w_query.transpose(layer_second),
        w_key.transpose(turned),
        w_value.transpose(turned),
        w_out.transpose(layer_second),
        w_gate.transpose(layer_second),
        w_up.transpose(layer_second),
        w_down.transpose(turned),
    )
    blocks = from_ring(jnp.stack(from_x(pack)), "z")
    a_near, a1_near = spread_a(index, blocks)
    near = from_ring(a_near, "y")
    b0 = lax.all_gather(
        spread_b(2 * PACK_A, index, blocks, pm, pf), INNER, axis=0, tiled=True
    )
    a_near = jnp.concatenate(share(near), 0)

    starts = jnp.broadcast_to((positions[0, ::BLOCK] // BLOCK).astype(BF16)[:, None], (16, ROWS))
    traded = jnp.concatenate([tokens[0].T, cotangent[0].T, starts], 0)
    traded = trade(after(traded, blocks[3]))
    table = key_table(traded[2 * D :, 0].astype(jnp.int32))
    places = (table[:2, None] * BLOCK + jnp.arange(BLOCK)[None, :]).reshape(ROWS)
    cosine, sine = angles(places)
    x, grad = call(enter_kernel, [sds((ROWS, D), F32)] * 2, 2, 2.9)(traded, pm)

    weights = []
    saved = []
    for layer in range(2):
        a, normed, q, kv, gains = call(
            pre_placed_kernel,
            [
                sds((192, A_WIDTH), BF16),
                sds((ROWS, D), BF16),
                sds((ROWS, D), BF16),
                sds((ROWS, 2 * KVD), BF16),
                sds((8, D), F32),
            ],
            6,
            4.4,
        )(source, a_near, x, pq, cosine, sine)
        near = from_ring(kv, "z")
        if layer == 0:
            a1_near = from_ring(after(a1_near, *near[1:]), "y")
            blocks = [after(blocks[0], *near[1:])] + blocks[1:]
            b1_near = spread_b(2 * PACK_A + PACK_B, index, blocks, pm, pf)
            b1 = lax.all_gather(b1_near, INNER, axis=0, tiled=True)
        kv_all = share(near)
        o, lse = attend(table, q, kv_all)
        if layer == 0:
            a_near = jnp.concatenate(share([after(piece, o) for piece in a1_near]), 0)
        last = layer == 1
        b = b1 if last else b0
        mid, op, nm, gate, up, hid, x_next = call(
            functools.partial(post_kernel, last),
            [
                sds((ROWS, D), F32),
                sds((ROWS, D), BF16),
                sds((ROWS, D), BF16),
                sds((ROWS, FF), BF16),
                sds((ROWS, FF), BF16),
                sds((ROWS, FF), BF16),
                sds((D, ROWS), BF16) if last else sds((ROWS, D), F32),
            ],
            5,
            7.9,
        )(o, x, gains, pm, b)
        weights.append((a, b))
        saved.append((x, normed, q, kv_all, gains, o, lse, mid, op, nm, gate, up, hid))
        x = x_next
    output = trade(x)

    for layer in (1, 0):
        a, b = weights[layer]
        x, normed, q, kv_all, gains, o, lse, mid, op, nm, gate, up, hid = saved[layer]
        last = layer == 0
        db, gm, do, dg2 = call(
            mlp_back_carry_kernel if last else mlp_back_kernel,
            [
                sds((192, C_WIDTH if last else B_WIDTH), BF16),
                sds((ROWS, D), F32),
                sds((ROWS, D), BF16),
                sds((1, D), F32),
            ],
            11 if last else 10,
            13.0,
        )(*((da,) if last else ()), grad, nm, gate, up, hid, mid, op, gains, pm, b)
        summed = lax.psum_scatter(db, INNER, scatter_dimension=0, tiled=True)
        dq, *pieces = attend_back(table, q, kv_all, o, do, lse)
        parts = return_pieces(pieces[:4], pieces[4:], "z")
        if last:
            first = call(gather_first_kernel, sds((16, 36, PACK_B), BF16), 3, 5.0)(
                after(first, parts[1]), pm, pf
            )
            parts[0] = after(parts[0], first)
            outs = [sds((D, ROWS), BF16)] + [sds((24, A_WIDTH), BF16)] * 8
            scratch = [pltpu.VMEM((192, A_WIDTH), BF16)]
        else:
            first = summed
            parts[0] = after(parts[0], output)
            outs = [sds((ROWS, D), F32), sds((192, A_WIDTH), BF16)]
            scratch = []
        grad, *pieces = call(
            functools.partial(qkv_back_kernel, last), outs, 17, 6.4, scratch=scratch
        )(dq, *parts, cosine, sine, normed, x, a, gains, pq, pm, gm, dg2, source)
        da = pieces[0]
    parts = return_pieces(pieces[:4], pieces[4:], "y")
    first = lax.all_to_all(first, OUTER, 0, 0, tiled=True)
    grad = trade(grad)
    blocks = call(gather_last_kernel, sds((16, 36, PACK + PACK_A), BF16), 8, 5.4)(
        *parts, after(summed, grad), pm, pf
    )
    rest = lax.all_to_all(blocks, OUTER, 0, 0, tiled=True)
    outs = call(
        finish_kernel,
        [
            sds((2, 72), F32),
            sds((36, 2, 72), F32),
            sds((2, 24, 36), F32),
            sds((2, 24, 36), F32),
            sds((36, 2, 72), F32),
            sds((36, 2, 192), F32),
            sds((36, 2, 192), F32),
            sds((2, 72, 96), F32),
        ],
        2,
        2.9,
    )(first, rest)
    order = (None, layer_second, turned, turned, layer_second, layer_second, layer_second, turned)
    outs = [out if axes is None else out.transpose(axes) for out, axes in zip(outs, order)]
    return (output.T[None], grad.astype(F32).T[None], *outs)


def solution(mesh):
    fine = Mesh(np.asarray(mesh.devices).reshape(SIZES), AXES)
    split = P(None, FSDP, CTX)
    rows = P(FSDP, CTX, None)
    return jax.shard_map(
        on_device,
        mesh=fine,
        in_specs=(rows, P(FSDP, None), P(None, FSDP)) + (split,) * 7 + (rows,),
        out_specs=(rows, rows, P(None, FSDP)) + (split,) * 7,
        check_vma=False,
    )
```

```python
import functools

import jax
import jax.numpy as jnp
import numpy as np
from jax import lax
from jax.experimental import pallas as pl
from jax.experimental.pallas import tpu as pltpu
from jax.sharding import Mesh
from jax.sharding import PartitionSpec as P

D = 576
HEADS = 9
KV_HEADS = 3
HEAD_DIM = 64
GROUP = HEADS // KV_HEADS
FF = 1536
ROWS = 256
BLOCK = 128
KEYS = 2048
KVD = KV_HEADS * HEAD_DIM
HALF_FF = FF // 2

rope_base = 10000.0
norm_eps = 1e-05
masked_score = -1e30
score_scale = HEAD_DIM ** (-0.5)

F32 = jnp.float32
BF16 = jnp.bfloat16

AXES = ("z", "xl", "xh", "y", "core")
SIZES = (4, 2, 2, 4, 2)
CTX = ("z", "xl")
FSDP = ("xh", "y", "core")
INNER = ("y", "core")
OUTER = ("z", "xl", "xh")

PACK = 896
PACK_A = 128
PACK_B = PACK - PACK_A
PACK_FIRST = PACK + PACK_A
PK_Q, PK_K, PK_V, PK_GAIN = 0, 72, 96, 120
PK_O, PK_G, PK_U, PK_D = 128, 200, 392, 584

A_STEP = 1024
A_WIDTH = 3 * A_STEP
B_STEP = 2 * FF
B_DOWN = 3 * B_STEP
B_OUT = B_DOWN + 8 * 512
B_DOWN_TAIL = B_OUT + 3 * 512
B_OUT_TAIL = B_DOWN_TAIL + 8 * 64
B_WIDTH = B_OUT_TAIL + 256

C_WIDTH = B_WIDTH + A_WIDTH

BYTES_PER_MICRO = 3.4e6
FLOPS_PER_MICRO = 1e9


def feature_order():
    n = np.arange(D)
    owner, i = n // 36, n % 36
    xh, yc = owner // 8, owner % 8
    local = xh * 36 + i
    return (local // 24) * 192 + yc * 24 + local % 24


def hidden_order():
    n = np.arange(HALF_FF)
    yc, i = n // 96, n % 96
    return (i // 24) * 192 + yc * 24 + i % 24


def one_hot(places):
    size = len(places)
    out = np.zeros((size, size), np.float32)
    out[np.arange(size), places] = 1.0
    return out


def gain_matrix():
    n = np.arange(D)
    yc, local = n // 72, n % 72
    gathered = (local // 24) * 192 + yc * 24 + local % 24
    out = np.zeros((D, D), np.float32)
    out[gathered, feature_order()] = 1.0
    return out


def dot(left, right):
    return lax.dot_general(left, right, (((1,), (0,)), ((), ())), preferred_element_type=F32)


def dot_rows(left, right):
    return lax.dot_general(left, right, (((0,), (0,)), ((), ())), preferred_element_type=F32)


def dot_back(left, right):
    return lax.dot_general(left, right, (((1,), (1,)), ((), ())), preferred_element_type=F32)


def call(kernel, out_shape, n_in, micros, smem=(), left=(), left_out=(), scratch=()):
    def spec(i, left):
        return pl.BlockSpec(
            memory_space=pltpu.SMEM if i in smem else pl.ANY if i in left else pltpu.VMEM
        )

    in_specs = [spec(i, left) for i in range(n_in)]
    many = isinstance(out_shape, (list, tuple))
    return pl.pallas_call(
        kernel,
        out_shape=out_shape,
        in_specs=in_specs,
        out_specs=[
            pl.BlockSpec(memory_space=pl.ANY if i in left_out else pltpu.VMEM)
            for i in range(len(out_shape))
        ]
        if many
        else pl.BlockSpec(memory_space=pltpu.VMEM),
        scratch_shapes=list(scratch),
        compiler_params=pltpu.CompilerParams(vmem_limit_bytes=56 << 20),
        cost_estimate=pl.CostEstimate(
            flops=int(micros * FLOPS_PER_MICRO),
            bytes_accessed=int(micros * BYTES_PER_MICRO),
            transcendentals=0,
        ),
    )


def sds(shape, dtype):
    return jax.ShapeDtypeStruct(shape, dtype)


def eye(size):
    rows = lax.broadcasted_iota(jnp.int32, (size, size), 0)
    cols = lax.broadcasted_iota(jnp.int32, (size, size), 1)
    return jnp.where(rows == cols, 1.0, 0.0).astype(F32)


def pack_kernel(vec, wq, wk, wv, wo, wg, wu, wd, out, later):
    diagonal = eye(36)
    for layer in range(2):
        gains = vec[layer : layer + 1, :].astype(F32)
        first = jnp.sum(diagonal * gains[:, :36], 1, keepdims=True)
        second = jnp.sum(diagonal * gains[:, 36:72], 1, keepdims=True)
        down = wd[layer].astype(F32).T
        block = jnp.concatenate(
            [
                wq[...].astype(F32)[:, layer],
                wk[layer].astype(F32).T,
                wv[layer].astype(F32).T,
                first,
                second,
                jnp.zeros((36, 6), F32),
                wo[...].astype(F32)[:, layer],
                wg[...].astype(F32)[:, layer],
                wu[...].astype(F32)[:, layer],
                down[:36],
                down[36:72],
                jnp.concatenate([down[72:96], jnp.zeros((12, 72), F32)], 0),
                jnp.zeros((36, 96), F32),
            ],
            1,
        ).astype(BF16)
        out[:, layer * PACK_A : (layer + 1) * PACK_A] = block[:, :PACK_A]
        if layer == 0:
            out[:, 2 * PACK_A :] = block[:, PACK_A:]
        else:
            later[...] = block[:, PACK_A:]


def part_of(index, blocks, c, xh, low, high):
    return blocks[index[c * 2 + xh], :, low:high].astype(F32)


def wide_of(index, blocks, low, high):
    halves = [
        jnp.concatenate([part_of(index, blocks, c, xh, low, high) for c in range(8)], 1)
        for xh in range(2)
    ]
    return jnp.concatenate(halves, 0)


def spread_a_kernel(index, r0, r1, r2, r3, out0, out1, blocks):
    for i, piece in enumerate((r0, r1, r2, r3)):
        blocks[4 * i : 4 * i + 4] = piece[:, :, : 2 * PACK_A]
    part = functools.partial(part_of, index, blocks)
    wide = functools.partial(wide_of, index, blocks)
    for layer, out in enumerate((out0, out1)):
        low = layer * PACK_A
        gains = []
        for xh in range(2):
            both = part(0, xh, low + PK_GAIN, low + PK_GAIN + 2)
            gains.append(jnp.concatenate([both[:, :1], both[:, 1:]], 0))
        a = jnp.concatenate(
            [
                wide(low + PK_Q, low + PK_K),
                wide(low + PK_K, low + PK_V),
                wide(low + PK_V, low + PK_GAIN),
            ]
            + gains
            + [jnp.zeros((72, 62), F32)],
            1,
        )
        for p in range(3):
            out[:, p * A_STEP : (p + 1) * A_STEP] = a[24 * p : 24 * p + 24].astype(BF16)


def spread_b_kernel(first, index, r0, r1, r2, r3, pm, pf, b_out, blocks):
    for i, piece in enumerate((r0, r1, r2, r3)):
        blocks[4 * i : 4 * i + 4] = piece[:, :, first : first + PACK_B]
    part = functools.partial(part_of, index, blocks)
    wide = functools.partial(wide_of, index, blocks)
    out = dot(wide(0, PK_G - PK_O).astype(BF16), pm[...])
    for p in range(3):
        piece = out[24 * p : 24 * p + 24].astype(BF16)
        b_out[:, B_OUT + p * 512 : B_OUT + (p + 1) * 512] = piece[:, :512]
        b_out[:, B_OUT_TAIL + p * 64 : B_OUT_TAIL + (p + 1) * 64] = piece[:, 512:]
    b_out[:, B_OUT_TAIL + 192 :] = jnp.zeros((24, 64), BF16)
    for shift, low, high in ((0, PK_G - PK_O, PK_U - PK_O), (FF, PK_U - PK_O, PK_D - PK_O)):
        natural = wide(low, high).astype(BF16)
        for half in range(2):
            placed = dot(natural[:, half * HALF_FF : (half + 1) * HALF_FF], pf[...])
            for p in range(3):
                start = p * B_STEP + shift + half * HALF_FF
                b_out[:, start : start + HALF_FF] = placed[24 * p : 24 * p + 24].astype(BF16)
    down_at = PK_D - PK_O
    for xh in range(2):
        pieces = []
        for c in range(8):
            pieces.append(
                jnp.concatenate(
                    [
                        part(c, xh, down_at, down_at + 72),
                        part(c, xh, down_at + 72, down_at + 144),
                        part(c, xh, down_at + 144, down_at + 216)[:24],
                    ],
                    0,
                )
            )
        down = dot(jnp.concatenate(pieces, 1).astype(BF16), pm[...])
        for i in range(4):
            p = xh * 4 + i
            piece = down[24 * i : 24 * i + 24].astype(BF16)
            b_out[:, B_DOWN + p * 512 : B_DOWN + (p + 1) * 512] = piece[:, :512]
            b_out[:, B_DOWN_TAIL + p * 64 : B_DOWN_TAIL + (p + 1) * 64] = piece[:, 512:]


def gathered_a(a, out, lanes):
    a72 = jnp.concatenate([a[:, p * A_STEP : (p + 1) * A_STEP] for p in range(3)], 0)
    for xh in range(2):
        rows = slice(xh * 36, xh * 36 + 36)
        gain = a72[:, 960 + xh : 961 + xh]
        for c in range(8):
            out[c * 2 + xh, :, lanes] = jnp.concatenate(
                [
                    a72[rows, c * 72 : c * 72 + 72],
                    a72[rows, 576 + c * 24 : 600 + c * 24],
                    a72[rows, 768 + c * 24 : 792 + c * 24],
                    gain[:36],
                    gain[36:72],
                    jnp.zeros((36, 6), F32),
                ],
                1,
            ).astype(BF16)


def gathered_b(b, pm, pf, out, lanes):
    o72 = jnp.concatenate(
        [
            jnp.concatenate(
                [
                    b[:, B_OUT + p * 512 : B_OUT + (p + 1) * 512].astype(F32),
                    b[:, B_OUT_TAIL + p * 64 : B_OUT_TAIL + (p + 1) * 64].astype(F32),
                ],
                1,
            )
            for p in range(3)
        ],
        0,
    )
    o72 = dot_back(o72.astype(BF16), pm[...])
    sides = []
    for shift in (0, FF):
        halves = []
        for half in range(2):
            low = shift + half * HALF_FF
            stacked = jnp.concatenate(
                [
                    b[:, p * B_STEP + low : p * B_STEP + low + HALF_FF].astype(F32)
                    for p in range(3)
                ],
                0,
            )
            halves.append(dot_back(stacked.astype(BF16), pf[...]))
        sides.append(jnp.concatenate(halves, 1))
    for xh in range(2):
        down = jnp.concatenate(
            [
                jnp.concatenate(
                    [
                        b[:, B_DOWN + p * 512 : B_DOWN + (p + 1) * 512].astype(F32),
                        b[:, B_DOWN_TAIL + p * 64 : B_DOWN_TAIL + (p + 1) * 64].astype(F32),
                    ],
                    1,
                )
                for p in range(xh * 4, xh * 4 + 4)
            ],
            0,
        )
        down = dot_back(down.astype(BF16), pm[...])
        rows = slice(xh * 36, xh * 36 + 36)
        for c in range(8):
            cols = slice(c * 72, c * 72 + 72)
            piece = down[:, cols]
            out[c * 2 + xh, :, lanes] = jnp.concatenate(
                [
                    o72[rows, cols],
                    sides[0][rows, c * 192 : c * 192 + 192],
                    sides[1][rows, c * 192 : c * 192 + 192],
                    piece[:36],
                    piece[36:72],
                    jnp.concatenate([piece[72:96], jnp.zeros((12, 72), F32)], 0),
                    jnp.zeros((36, 96), F32),
                ],
                1,
            ).astype(BF16)


def gather_first_kernel(b, pm, pf, out):
    gathered_b(b, pm, pf, out, slice(0, PACK_B))


def gather_second_kernel(c, pm, pf, out):
    gathered_b(c, pm, pf, out, slice(0, PACK_B))
    gathered_a(c[:, B_WIDTH:].astype(F32), out, slice(PACK_B, PACK))


def gather_last_kernel(a0, a1, a2, a3, a4, blocks, out):
    a = a0[...].astype(F32)
    for ref in (a1, a2, a3, a4):
        a = a + ref[...].astype(F32)
    out[:, :, PACK_A:] = blocks[...]
    gathered_a(a, out, slice(0, PACK_A))


def finish_kernel(first_ref, last_ref, vec, wq, wk, wv, wo, wg, wu, wd):
    diagonal = eye(36)

    def added(ref, low, high):
        total = ref[0, :, low:high].astype(F32)
        for i in range(1, 16):
            total = total + ref[i, :, low:high].astype(F32)
        return total

    totals = (
        added(last_ref, 0, PACK),
        jnp.concatenate([added(last_ref, PACK, PACK + PACK_A), added(first_ref, 0, PACK_B)], 1),
    )
    for layer, total in enumerate(totals):
        wq[:, layer, :] = total[:, PK_Q:PK_K]
        wk[layer] = total[:, PK_K:PK_V].T
        wv[layer] = total[:, PK_V:PK_GAIN].T
        wo[:, layer, :] = total[:, PK_O:PK_G]
        first = jnp.sum(diagonal * total[:, PK_GAIN : PK_GAIN + 1], 0, keepdims=True)
        second = jnp.sum(diagonal * total[:, PK_GAIN + 1 : PK_GAIN + 2], 0, keepdims=True)
        vec[layer : layer + 1, :] = jnp.concatenate([first, second], 1)
        wg[:, layer, :] = total[:, PK_G:PK_U]
        wu[:, layer, :] = total[:, PK_U:PK_D]
        wd[layer] = jnp.concatenate(
            [
                total[:, PK_D : PK_D + 72],
                total[:, PK_D + 72 : PK_D + 144],
                total[:24, PK_D + 144 : PK_D + 216],
            ],
            0,
        ).T


def swap_halves(tile):
    lane = lax.broadcasted_iota(jnp.int32, tile.shape, 1) % HEAD_DIM
    return jnp.where(
        lane < HEAD_DIM // 2,
        pltpu.roll(tile, 128 - HEAD_DIM // 2, 1),
        pltpu.roll(tile, HEAD_DIM // 2, 1),
    )


def place_rows(source):
    lane = lax.broadcasted_iota(jnp.int32, (192, 192), 1)
    return jnp.where(lane == source[...], 1.0, 0.0).astype(BF16)


def pre_kernel(first, source, a_in, x_ref, pm, pq, cosine, sine, a, normed_out, q_out, kv_out, gains_out, *x_out):
    a[...] = dot(place_rows(source), a_in[...]).astype(BF16)
    gains = dot_rows(a[:, 896:1024], pq[0:192, :])
    for p in range(1, 3):
        gains = gains + dot_rows(
            a[:, p * A_STEP + 896 : (p + 1) * A_STEP], pq[p * 192 : (p + 1) * 192, :]
        )
    gains = gains[64:72]
    gains_out[...] = gains
    if first:
        x = dot_rows(x_ref[:D, :], pm[...])
        x_out[0][...] = x
    else:
        x = x_ref[...]
    inverse = lax.rsqrt(jnp.mean(x * x, -1, keepdims=True) + norm_eps)
    normed = (x * inverse * gains[0:1]).astype(BF16)
    normed_out[...] = normed
    lin = dot(normed[:, :192], a[:, :A_STEP])
    for p in range(1, 3):
        lin = lin + dot(
            normed[:, p * 192 : (p + 1) * 192], a[:, p * A_STEP : (p + 1) * A_STEP]
        )
    turned = []
    for t in range(6):
        tile = lin[:, t * 128 : (t + 1) * 128]
        turned.append(tile * cosine[...] + swap_halves(tile) * sine[...])
    turned = jnp.concatenate(turned, 1)
    q_out[...] = (turned[:, :D] * score_scale).astype(BF16)
    for g in range(KV_HEADS):
        part = slice(g * HEAD_DIM, (g + 1) * HEAD_DIM)
        kv_out[:, g * PAIR : (g + 1) * PAIR] = jnp.concatenate(
            [turned[:, D:768][:, part], lin[:, 768:960][:, part]], 1
        ).astype(BF16)


def weight_back(left, b, main, tail, p):
    return dot_back(left[:, :512], b[:, main + p * 512 : main + (p + 1) * 512]) + dot_back(
        left[:, 512:], b[:, tail + p * 64 : tail + (p + 1) * 64]
    )


def fetch_b(b, held, sems):
    copies = []
    for i, (low, high) in enumerate(((0, B_DOWN), (B_DOWN, B_OUT), (B_OUT, B_WIDTH))):
        copies.append(
            pltpu.make_async_copy(b.at[:, low:high], held.at[:, low:high], sems.at[i])
        )
    return copies


def ffn_forward(o_ref, x_ref, gains, pm, b, copies, mid_out, op_out, nm_out, gate_low, up_low, hid_low):
    ffn, down, rest = copies
    op = dot(o_ref[...], pm[...]).astype(BF16)
    op_out[...] = op

    def through(left, main, tail, count):
        wide = None
        narrow = None
        for p in range(count):
            piece = left[:, p * 192 : (p + 1) * 192]
            one = dot(piece, b[:, main + p * 512 : main + (p + 1) * 512])
            two = dot(piece, b[:, tail + p * 64 : tail + (p + 1) * 64])
            wide = one if wide is None else wide + one
            narrow = two if narrow is None else narrow + two
        return jnp.concatenate([wide, narrow], 1)

    rest.wait()
    mid = x_ref[...] + through(op, B_OUT, B_OUT_TAIL, 3)
    mid_out[...] = mid
    inverse = lax.rsqrt(jnp.mean(mid * mid, -1, keepdims=True) + norm_eps)
    nm = (mid * inverse * gains[1:2, :]).astype(BF16)
    nm_out[...] = nm
    ffn.wait()
    for part in range(2):
        cols = slice(part * HALF_FF, (part + 1) * HALF_FF)
        gate, up = None, None
        for p in range(3):
            piece = nm[:, p * 192 : (p + 1) * 192]
            low = p * B_STEP + part * HALF_FF
            one = dot(piece, b[:, low : low + HALF_FF])
            two = dot(piece, b[:, low + FF : low + FF + HALF_FF])
            gate = one if gate is None else gate + one
            up = two if up is None else up + two
        gate_low[:, cols] = gate.astype(BF16)
        up_low[:, cols] = up.astype(BF16)
        hid_low[:, cols] = (gate / (1.0 + jnp.exp(-gate)) * up).astype(BF16)
    down.wait()
    return mid + through(hid_low, B_DOWN, B_DOWN_TAIL, 8)


def post_kernel(o_ref, x_ref, gains, pm, b_ref, *refs):
    mid_out, op_out, nm_out, gate_out, up_out, hid_out, x_out, b, sems = refs
    copies = fetch_b(b_ref, b, sems)
    for copy in copies[::-1]:
        copy.start()
    x_out[...] = ffn_forward(
        o_ref, x_ref, gains, pm, b, copies, mid_out, op_out, nm_out, gate_out, up_out, hid_out
    )


def norm_back(dy, v, gain):
    inverse = lax.rsqrt(jnp.mean(v * v, -1, keepdims=True) + norm_eps)
    scaled = dy * gain
    back = inverse * scaled - v * (
        inverse * inverse * inverse * jnp.mean(scaled * v, -1, keepdims=True)
    )
    return back, jnp.sum(dy * v * inverse, 0, keepdims=True)


class Sender:
    def __init__(self, db, db_out, sems):
        self.db, self.db_out, self.sems, self.sent = db, db_out, sems, []

    def send(self, low, high, source=None):
        source = self.db.at[:, low:high] if source is None else source
        self.sent.append(
            pltpu.make_async_copy(
                source, self.db_out.at[:, low:high], self.sems.at[3 + len(self.sent)]
            )
        )
        self.sent[-1].start()

    def wait(self):
        for copy in self.sent:
            copy.wait()


def ffn_backward(
    g,
    nm,
    gate_ref,
    up_ref,
    hid,
    mid,
    op,
    gains,
    pm,
    b,
    copies,
    sender,
    gm_out,
    do_out,
    dg_out,
    late=(),
    da=None,
):
    db = sender.db
    gb = g.astype(BF16)
    for p in range(8):
        piece = dot_rows(hid[:, p * 192 : (p + 1) * 192], gb)
        db[:, B_DOWN + p * 512 : B_DOWN + (p + 1) * 512] = piece[:, :512].astype(BF16)
        db[:, B_DOWN_TAIL + p * 64 : B_DOWN_TAIL + (p + 1) * 64] = piece[:, 512:].astype(BF16)
    sender.send(B_DOWN, B_OUT)
    for copy in copies[1:]:
        copy.wait()
    dh = jnp.concatenate([weight_back(gb, b, B_DOWN, B_DOWN_TAIL, p) for p in range(8)], 1)
    for copy in late[:3]:
        copy.wait()
    gate = gate_ref[...].astype(F32)
    up = up_ref[...].astype(F32)
    sig = 1.0 / (1.0 + jnp.exp(-gate))
    d_gate = (dh * up * sig * (1.0 + gate * (1.0 - sig))).astype(BF16)
    d_up = (dh * (gate * sig)).astype(BF16)
    for p in range(3):
        piece = nm[:, p * 192 : (p + 1) * 192]
        low = p * B_STEP
        db[:, low : low + FF] = dot_rows(piece, d_gate).astype(BF16)
        db[:, low + FF : low + B_STEP] = dot_rows(piece, d_up).astype(BF16)
        sender.send(low, low + B_STEP)
    for copy in copies[:1]:
        copy.wait()
    for copy in late[3:]:
        copy.wait()
    if da is not None:
        sender.send(B_WIDTH, C_WIDTH, da)
    dnm = []
    for p in range(3):
        low = p * B_STEP
        dnm.append(
            dot_back(d_gate, b[:, low : low + FF])
            + dot_back(d_up, b[:, low + FF : low + B_STEP])
        )
    back, gain_grad = norm_back(jnp.concatenate(dnm, 1), mid[...], gains[1:2, :])
    dg_out[...] = gain_grad
    gm = g + back
    gm_out[...] = gm
    gmb = gm.astype(BF16)
    dop = []
    for p in range(3):
        piece = dot_rows(op[:, p * 192 : (p + 1) * 192], gmb)
        db[:, B_OUT + p * 512 : B_OUT + (p + 1) * 512] = piece[:, :512].astype(BF16)
        db[:, B_OUT_TAIL + p * 64 : B_OUT_TAIL + (p + 1) * 64] = piece[:, 512:].astype(BF16)
        dop.append(weight_back(gmb, b, B_OUT, B_OUT_TAIL, p))
    db[:, B_OUT_TAIL + 192 : B_WIDTH] = jnp.zeros((192, 64), BF16)
    sender.send(B_OUT, B_WIDTH)
    do_out[...] = dot_back(jnp.concatenate(dop, 1).astype(BF16), pm[...]).astype(BF16)
    sender.wait()


def held_copies(refs, held, sems, first):
    copies = [
        pltpu.make_async_copy(ref, target, sems.at[first + i])
        for i, (ref, target) in enumerate(zip(refs, held))
    ]
    for copy in copies:
        copy.start()
    return copies


def mlp_back_kernel(g_ref, hid, gains, gate, up, nm, mid, op, pm, b_ref, da, *refs):
    db_out, gm_out, do_out, dg_out, b, db, da_held, *held, sems = refs
    copies = fetch_b(b_ref, b, sems)
    copies[2].start()
    copies[1].start()
    late = held_copies((gate, up, nm), held[:3], sems, 9)
    copies[0].start()
    late += held_copies((mid, op, pm, da), (*held[3:], da_held), sems, 12)
    sender = Sender(db, db_out, sems)
    ffn_backward(
        g_ref[...], held[2], held[0], held[1], hid, held[3], held[4], gains, held[5], b,
        copies, sender, gm_out, do_out, dg_out, late, da_held,
    )


def turn_kernel(o_ref, x_ref, gains, traded, pm, b_ref, *refs):
    x_out, db_out, gm_out, do_out, dg_out, b, db, mid, op, nm, gate, up, hid, sems = refs
    copies = fetch_b(b_ref, b, sems)
    for copy in copies[::-1]:
        copy.start()
    out = ffn_forward(o_ref, x_ref, gains, pm, b, copies, mid, op, nm, gate, up, hid)
    x_out[...] = dot_back(pm[...], out.astype(BF16)).astype(BF16)
    g = dot_rows(traded[D : 2 * D, :], pm[...])
    sender = Sender(db, db_out, sems)
    ffn_backward(
        g, nm, gate, up, hid, mid, op, gains, pm, b, (), sender, gm_out, do_out, dg_out
    )


def qkv_back_kernel(
    last, dq, kv0, kv1, kv2, kv3, kv4, cosine, sine, normed, gains, dg2, a_ref, x_late, gm_late, pq_late, *refs
):
    if last:
        pm_ref, source, x_out, *da_refs, da, a, x_ref, gm, pq, pm, sems = refs
        late = held_copies((a_ref, x_late, gm_late, pq_late, pm_ref), (a, x_ref, gm, pq, pm), sems, 0)
    else:
        x_out, da, a, x_ref, gm, pq, sems = refs
        late = held_copies((a_ref, x_late, gm_late, pq_late), (a, x_ref, gm, pq), sems, 0)
    dkv = kv0[...].astype(F32)
    for ref in (kv1, kv2, kv3, kv4):
        dkv = dkv + ref[...].astype(F32)
    d_key = [dkv[:, g * PAIR : g * PAIR + HEAD_DIM] for g in range(KV_HEADS)]
    d_value = [dkv[:, g * PAIR + HEAD_DIM : (g + 1) * PAIR] for g in range(KV_HEADS)]
    rot = jnp.concatenate([dq[...]] + d_key, 1)
    turned = []
    for t in range(6):
        tile = rot[:, t * 128 : (t + 1) * 128]
        turned.append(tile * cosine[...] - swap_halves(tile) * sine[...])
    dqkv = jnp.concatenate(turned + d_value + [jnp.zeros((ROWS, 64), F32)], 1).astype(BF16)
    late[0].wait()
    dn = []
    for p in range(3):
        low = p * A_STEP
        da[:, low : low + A_STEP] = dot_rows(
            normed[:, p * 192 : (p + 1) * 192], dqkv
        ).astype(BF16)
        dn.append(dot_back(dqkv, a[:, low : low + A_STEP]))
    for copy in late[1:]:
        copy.wait()
    x = x_ref[...]
    back, dg1 = norm_back(jnp.concatenate(dn, 1), x, gains[0:1, :])
    rows = lax.broadcasted_iota(jnp.int32, (64, D), 0)
    stacked = jnp.where(rows == 0, dg1, jnp.where(rows == 1, dg2[...], 0.0)).astype(BF16)
    placed = dot_back(pq[...], stacked).astype(BF16)
    for p in range(3):
        da[:, p * A_STEP + 960 : (p + 1) * A_STEP] = placed[p * 192 : (p + 1) * 192]
    out = gm[...] + back
    if last:
        x_out[...] = dot_back(pm[...], out.astype(BF16)).astype(BF16)
        placed = dot_rows(place_rows(source), da[...])
        for i, ref in enumerate(da_refs):
            ref[...] = placed[i * 24 : (i + 1) * 24].astype(BF16)
    else:
        x_out[...] = out


PAIR = 2 * HEAD_DIM
WIDE = GROUP * BLOCK
CHUNK = 256
STEPS = KEYS // CHUNK + 1
SLOTS = 2 * KV_HEADS


def load_heads(ref, scratch, run, upper):
    zero = jnp.zeros((WIDE, HEAD_DIM), BF16)
    for g in range(KV_HEADS):
        heads = jnp.concatenate(
            [
                ref[
                    run * BLOCK : (run + 1) * BLOCK,
                    (g * GROUP + h) * HEAD_DIM : (g * GROUP + h + 1) * HEAD_DIM,
                ]
                for h in range(GROUP)
            ],
            0,
        )
        both = [zero, heads] if upper else [heads, zero]
        scratch[run * KV_HEADS + g] = jnp.concatenate(both, 1)


def sort_keys(table, pieces, kvs):
    for j in range(KEYS // BLOCK):
        start = pl.multiple_of(table[2 + j] * BLOCK, BLOCK)
        kvs[pl.ds(start, BLOCK), :] = pieces[j // 2][(j % 2) * BLOCK : (j % 2 + 1) * BLOCK, :]


def set_lead(lead):
    key = lax.broadcasted_iota(jnp.int32, (CHUNK, BLOCK), 0)
    row = lax.broadcasted_iota(jnp.int32, (CHUNK, BLOCK), 1)
    lead[...] = row - key


def head_columns(h):
    return slice(h * BLOCK, (h + 1) * BLOCK)


def step_of(table, it):
    first = (table[0] + 2) // 2
    second = it >= first
    run = jnp.where(second, 1, 0)
    chunk = jnp.where(second, it - first, it)
    block = jnp.where(second, table[1], table[0])
    return run, pl.multiple_of(chunk * CHUNK, CHUNK), chunk * CHUNK - block * BLOCK


def attend_kernel(table, q_ref, *refs):
    pieces, (o_out, lse_out, kvs, qs, lead, ms, ls, acc) = refs[:8], refs[8:]
    sort_keys(table, pieces, kvs)
    load_heads(q_ref, qs, 0, False)
    load_heads(q_ref, qs, 1, False)
    set_lead(lead)
    ms[...] = jnp.full(ms.shape, masked_score, F32)
    ls[...] = jnp.zeros(ls.shape, F32)
    acc[...] = jnp.zeros(acc.shape, F32)

    def step(it, carry):
        run, start, least = step_of(table, it)
        results = []
        for g in range(KV_HEADS):
            at = run * KV_HEADS + g
            kv = kvs[pl.ds(start, CHUNK), g * PAIR : (g + 1) * PAIR]
            turned = kv.T
            for h in range(GROUP):
                part = head_columns(h)
                scores = dot_back(kv, qs[at, part, :])
                scores = jnp.where(lead[...] >= least, scores, masked_score)
                before = ms[at, :, part]
                now = jnp.maximum(before, jnp.max(scores, 0, keepdims=True))
                raised = jnp.exp(scores - now)
                shrink = jnp.exp(before - now)
                total = ls[at, :, part] * shrink + jnp.sum(raised, 0, keepdims=True)
                out = dot(turned, raised.astype(BF16))[HEAD_DIM:]
                results.append((at, part, now, total, acc[at, :, part] * shrink + out))
        for at, part, now, total, out in results:
            ms[at, :, part] = now
            ls[at, :, part] = total
            acc[at, :, part] = out
        return carry

    lax.fori_loop(0, STEPS, step, 0, unroll=STEPS)
    for run in range(2):
        for g in range(KV_HEADS):
            at = run * KV_HEADS + g
            total = ls[at]
            lse_out[at] = ms[at] + jnp.log(total)
            heads = (acc[at] / total).T
            for h in range(GROUP):
                o_out[
                    run * BLOCK : (run + 1) * BLOCK,
                    (g * GROUP + h) * HEAD_DIM : (g * GROUP + h + 1) * HEAD_DIM,
                ] = heads[h * BLOCK : (h + 1) * BLOCK].astype(BF16)


def attend_back_kernel(table, q_ref, o_ref, do_ref, lse, *refs):
    pieces = refs[:8]
    dq_out, outs, (kvs, qs, dos, lead, deltas, dkvs, dqs) = refs[8], refs[9:17], refs[17:]
    sort_keys(table, pieces, kvs)
    set_lead(lead)
    for run in range(2):
        load_heads(q_ref, qs, run, False)
        load_heads(do_ref, dos, run, True)
        rows = slice(run * BLOCK, (run + 1) * BLOCK)
        product = o_ref[rows, :].astype(F32) * do_ref[rows, :].astype(F32)
        turned = jnp.concatenate([product, jnp.zeros((BLOCK, HEAD_DIM), F32)], 1).T
        for g in range(KV_HEADS):
            deltas[run * KV_HEADS + g] = jnp.concatenate(
                [
                    jnp.sum(turned[h * HEAD_DIM : (h + 1) * HEAD_DIM], 0, keepdims=True)
                    for h in range(g * GROUP, (g + 1) * GROUP)
                ],
                1,
            )
    dkvs[...] = jnp.zeros(dkvs.shape, F32)
    dqs[...] = jnp.zeros(dqs.shape, F32)

    def step(it, carry):
        run, start, least = step_of(table, it)
        scores, d_probs, low_probs, d_scores, results = [], [], [], [], []
        for g in range(KV_HEADS):
            at = run * KV_HEADS + g
            kv = kvs[pl.ds(start, CHUNK), g * PAIR : (g + 1) * PAIR]
            scores.append(dot_back(kv, qs[at]))
            d_probs.append(dot_back(kv, dos[at]))
        ahead = jnp.concatenate([lead[...]] * GROUP, 1) >= least
        for g in range(KV_HEADS):
            at = run * KV_HEADS + g
            probs = jnp.exp(jnp.where(ahead, scores[g], masked_score) - lse[at])
            low_probs.append(probs.astype(BF16))
            d_scores.append((probs * (d_probs[g] - deltas[at])).astype(BF16))
        for g in range(KV_HEADS):
            at = run * KV_HEADS + g
            kv = kvs[pl.ds(start, CHUNK), g * PAIR : (g + 1) * PAIR]
            d_kv = dot(d_scores[g], qs[at]) + dot(low_probs[g], dos[at])
            results.append((at, d_kv, dot_rows(kv, d_scores[g])[:HEAD_DIM]))
        for g, (at, d_kv, d_q) in enumerate(results):
            dkvs[g, pl.ds(start, CHUNK), :] += d_kv
            dqs[at] += d_q
        return carry

    lax.fori_loop(0, STEPS, step, 0, unroll=STEPS)
    for run in range(2):
        for g in range(KV_HEADS):
            heads = (dqs[run * KV_HEADS + g] * score_scale).T
            for h in range(GROUP):
                dq_out[
                    run * BLOCK : (run + 1) * BLOCK,
                    (g * GROUP + h) * HEAD_DIM : (g * GROUP + h + 1) * HEAD_DIM,
                ] = heads[h * BLOCK : (h + 1) * BLOCK]
    for j in range(KEYS // BLOCK):
        start = pl.multiple_of(table[2 + j] * BLOCK, BLOCK)
        rows = slice((j % 2) * BLOCK, (j % 2 + 1) * BLOCK)
        for g in range(KV_HEADS):
            outs[j // 2][rows, g * PAIR : (g + 1) * PAIR] = dkvs[
                g, pl.ds(start, BLOCK), :
            ].astype(BF16)


def attend(table, q, kv_all):
    return call(
        attend_kernel,
        [sds((ROWS, D), BF16), sds((SLOTS, 1, WIDE), F32)],
        10,
        6.9,
        smem=(0,),
        scratch=[
            pltpu.VMEM((KEYS, KV_HEADS * PAIR), BF16),
            pltpu.VMEM((SLOTS, WIDE, PAIR), BF16),
            pltpu.VMEM((CHUNK, BLOCK), jnp.int32),
            pltpu.VMEM((SLOTS, 1, WIDE), F32),
            pltpu.VMEM((SLOTS, 1, WIDE), F32),
            pltpu.VMEM((SLOTS, HEAD_DIM, WIDE), F32),
        ],
    )(table, q, *kv_all)


def attend_back(table, q, kv_all, o, do, lse):
    return call(
        attend_back_kernel,
        [sds((ROWS, D), F32)] + [sds((ROWS, 2 * KVD), BF16)] * 8,
        13,
        11.3,
        smem=(0,),
        scratch=[
            pltpu.VMEM((KEYS, KV_HEADS * PAIR), BF16),
            pltpu.VMEM((SLOTS, WIDE, PAIR), BF16),
            pltpu.VMEM((SLOTS, WIDE, PAIR), BF16),
            pltpu.VMEM((CHUNK, BLOCK), jnp.int32),
            pltpu.VMEM((SLOTS, 1, WIDE), F32),
            pltpu.VMEM((KV_HEADS, KEYS, PAIR), F32),
            pltpu.VMEM((SLOTS, HEAD_DIM, WIDE), F32),
        ],
    )(table, q, o, do, lse, *kv_all)


def ring(shift):
    return [(i, (i + shift) % 4) for i in range(4)]


def ring_x(shift):
    pairs = []
    for x in range(4):
        to = (x + shift) % 4
        pairs.append(((x % 2) * 2 + x // 2, (to % 2) * 2 + to // 2))
    return pairs


SHIFTS = (1, -1, 2)


def from_x(value):
    return [value] + [lax.ppermute(value, ("xl", "xh"), ring_x(s)) for s in SHIFTS]


def from_ring(value, axis):
    return [value] + [lax.ppermute(value, axis, ring(s)) for s in SHIFTS]


def other_core(value):
    return lax.ppermute(value, "core", [(0, 1), (1, 0)])


def trade(value):
    return lax.ppermute(value, ("xl", "core"), [(0, 0), (1, 2), (2, 1), (3, 3)])


def place_of(distance):
    distance = distance % 4
    return distance ^ (distance >> 1)


def block_index():
    z, xl, xh = (lax.axis_index(name) for name in OUTER)
    block = jnp.arange(16, dtype=jnp.int32)
    along_x = place_of(xh * 2 + xl - (block % 2) * 2 - (block // 2) % 2)
    along_z = place_of(z - block // 4)
    return along_z * 4 + along_x, along_x * 4 + along_z


def row_source():
    y, core = lax.axis_index("y"), lax.axis_index("core")
    rows = jnp.arange(192, dtype=jnp.int32)
    owner, j = rows // 24, rows % 24
    piece = ((owner + core) % 2) * 4 + place_of(y - owner // 2)
    return (piece * 24 + j)[:, None]


def spread_a(index, blocks):
    return call(
        spread_a_kernel,
        [sds((24, A_WIDTH), BF16)] * 2,
        5,
        3.0,
        smem=(0,),
        scratch=[pltpu.VMEM((16, 36, 2 * PACK_A), BF16)],
    )(index, *blocks)


def spread_b(first, index, blocks, pm, pf):
    return call(
        functools.partial(spread_b_kernel, first),
        sds((24, B_WIDTH), BF16),
        7,
        4.3,
        smem=(0,),
        scratch=[pltpu.VMEM((16, 36, PACK_B), BF16)],
    )(index, *blocks, pm, pf)


def share(near):
    return near + [other_core(piece) for piece in near]


def return_pieces(near, far, axis):
    far = [other_core(piece) for piece in far]
    both = [(n.astype(F32) + f.astype(F32)).astype(BF16) for n, f in zip(near[1:], far[1:])]
    back = [lax.ppermute(piece, axis, ring(-s)) for piece, s in zip(both, SHIFTS)]
    return [near[0], far[0]] + back


def key_table(starts):
    z, core = lax.axis_index("z"), lax.axis_index("core")
    j = np.arange(18) - 2
    shift = np.where(j < 0, 0, np.array((0,) + SHIFTS)[(j // 2) % 4]).astype(np.int32)
    far = np.where(j < 0, 0, j // 8).astype(np.int32)
    wanted = (((z - shift) % 4) * 2 + (core + far) % 2) * 2 + (j % 2).astype(np.int32)
    match = wanted[:, None] == jnp.arange(16, dtype=jnp.int32)[None, :]
    return jnp.sum(jnp.where(match, starts[None, :], 0), 1)


def angles(places):
    half_dim = HEAD_DIM // 2
    inverse = rope_base ** (-2.0 * jnp.arange(half_dim).astype(F32) / HEAD_DIM)
    turned = places.astype(F32)[:, None] * inverse[None, :]
    cosine, sine = jnp.cos(turned), jnp.sin(turned)
    return jnp.concatenate([cosine] * 4, 1), jnp.concatenate([-sine, sine] * 2, 1)


def after(value, *others):
    return lax.optimization_barrier((value, *others))[0]


def on_device(
    tokens, positions, vectors, w_query, w_key, w_value, w_out, w_gate, w_up, w_down, cotangent
):
    pm = jnp.asarray(one_hot(feature_order()), BF16)
    pf = jnp.asarray(one_hot(hidden_order()), BF16)
    pq = jnp.asarray(gain_matrix(), BF16)
    index, z_index = block_index()
    source = row_source()
    layer_second = (1, 0, 2)
    turned = (0, 2, 1)
    pack, later = call(
        pack_kernel, [sds((36, PACK_FIRST), BF16), sds((36, PACK_B), BF16)], 8, 1.9
    )(
        vectors,
        w_query.transpose(layer_second),
        w_key.transpose(turned),
        w_value.transpose(turned),
        w_out.transpose(layer_second),
        w_gate.transpose(layer_second),
        w_up.transpose(layer_second),
        w_down.transpose(turned),
    )
    later = jnp.stack(from_ring(later, "z"))
    blocks = from_ring(after(jnp.stack(from_x(pack)), later), "z")
    a_near, a1_near = spread_a(index, blocks)
    near = from_ring(a_near, "y")
    later = from_x(after(later, a_near))
    a_near = jnp.concatenate(share(near), 0)
    blocks = [after(blocks[0], *near[1:])] + blocks[1:]
    b0 = lax.all_gather(
        spread_b(2 * PACK_A, index, blocks, pm, pf), INNER, axis=0, tiled=True
    )

    starts = jnp.broadcast_to((positions[0, ::BLOCK] // BLOCK).astype(BF16)[:, None], (16, ROWS))
    traded = jnp.concatenate([tokens[0].T, cotangent[0].T, starts], 0)
    traded = trade(after(traded, blocks[3]))
    table = key_table(traded[2 * D :, 0].astype(jnp.int32))
    places = (table[:2, None] * BLOCK + jnp.arange(BLOCK)[None, :]).reshape(ROWS)
    cosine, sine = angles(places)
    x = traded

    saved = []
    for layer in range(2):
        a, normed, q, kv, gains, *entered = call(
            functools.partial(pre_kernel, layer == 0),
            [
                sds((192, A_WIDTH), BF16),
                sds((ROWS, D), BF16),
                sds((ROWS, D), BF16),
                sds((ROWS, 2 * KVD), BF16),
                sds((8, D), F32),
            ]
            + [sds((ROWS, D), F32)] * (layer == 0),
            7,
            4.6,
        )(source, a_near, x, pm, pq, cosine, sine)
        x = entered[0] if entered else x
        near = from_ring(kv, "z")
        if layer == 0:
            a1_near = from_ring(after(a1_near, *near[1:]), "y")
            later = [after(later[0], *near[1:])] + later[1:]
            b1_near = spread_b(0, z_index, later, pm, pf)
            b1 = lax.all_gather(b1_near, INNER, axis=0, tiled=True)
        kv_all = share(near)
        o, lse = attend(table, q, kv_all)
        if layer == 0:
            a_near = jnp.concatenate(share([after(piece, o) for piece in a1_near]), 0)
        saved.append((x, a, normed, q, kv_all, gains, o, lse))
        if layer == 0:
            mid, op, nm, gate, up, hid, x = call(
                post_kernel,
                [
                    sds((ROWS, D), F32),
                    sds((ROWS, D), BF16),
                    sds((ROWS, D), BF16),
                    sds((ROWS, FF), BF16),
                    sds((ROWS, FF), BF16),
                    sds((ROWS, FF), BF16),
                    sds((ROWS, D), F32),
                ],
                5,
                7.9,
                left=(4,),
                scratch=[pltpu.VMEM((192, B_WIDTH), BF16), pltpu.SemaphoreType.DMA((3,))],
            )(o, x, gains, pm, b0)

    back_shapes = [sds((ROWS, D), F32), sds((ROWS, D), BF16), sds((1, D), F32)]
    back_scratch = [pltpu.VMEM((192, B_WIDTH), BF16)] * 2
    for layer in (1, 0):
        x, a, normed, q, kv_all, gains, o, lse = saved[layer]
        last = layer == 0
        if last:
            db, gm, do, dg2 = call(
                mlp_back_kernel,
                [sds((192, C_WIDTH), BF16)] + back_shapes,
                11,
                12.5,
                left=range(3, 11),
                left_out=(0,),
                scratch=back_scratch
                + [
                    pltpu.VMEM((192, A_WIDTH), BF16),
                    pltpu.VMEM((ROWS, FF), BF16),
                    pltpu.VMEM((ROWS, FF), BF16),
                    pltpu.VMEM((ROWS, D), BF16),
                    pltpu.VMEM((ROWS, D), F32),
                    pltpu.VMEM((ROWS, D), BF16),
                    pltpu.VMEM((D, D), BF16),
                    pltpu.SemaphoreType.DMA((16,)),
                ],
            )(grad, hid, gains, gate, up, nm, mid, op, pm, b0, da)
        else:
            output, db, gm, do, dg2 = call(
                turn_kernel,
                [sds((D, ROWS), BF16), sds((192, B_WIDTH), BF16)] + back_shapes,
                6,
                15.0,
                left=(5,),
                left_out=(1,),
                scratch=back_scratch
                + [
                    pltpu.VMEM((ROWS, D), F32),
                    pltpu.VMEM((ROWS, D), BF16),
                    pltpu.VMEM((ROWS, D), BF16),
                    pltpu.VMEM((ROWS, FF), BF16),
                    pltpu.VMEM((ROWS, FF), BF16),
                    pltpu.VMEM((ROWS, FF), BF16),
                    pltpu.SemaphoreType.DMA((8,)),
                ],
            )(o, x, gains, traded, pm, b1)
            output = trade(output)
        summed = lax.psum_scatter(db, INNER, scatter_dimension=0, tiled=True)
        dq, *pieces = attend_back(table, q, kv_all, o, do, lse)
        parts = return_pieces(pieces[:4], pieces[4:], "z")
        held = [
            pltpu.VMEM((192, A_WIDTH), BF16),
            pltpu.VMEM((ROWS, D), F32),
            pltpu.VMEM((ROWS, D), F32),
            pltpu.VMEM((D, D), BF16),
        ]
        if last:
            first = call(gather_first_kernel, sds((16, 36, PACK_B), BF16), 3, 5.0)(
                after(first, parts[1]), pm, pf
            )
            parts[0] = after(parts[0], first)
            outs = [sds((D, ROWS), BF16)] + [sds((24, A_WIDTH), BF16)] * 8
            scratch = [pltpu.VMEM((192, A_WIDTH), BF16)] + held + [pltpu.VMEM((D, D), BF16)]
        else:
            first = summed
            parts[0] = after(parts[0], output)
            outs = [sds((ROWS, D), F32), sds((192, A_WIDTH), BF16)]
            scratch = held
        grad, *pieces = call(
            functools.partial(qkv_back_kernel, last),
            outs,
            17 if last else 15,
            6.4,
            left=range(11, 16) if last else range(11, 15),
            scratch=scratch + [pltpu.SemaphoreType.DMA((5,))],
        )(
            dq,
            *parts,
            cosine,
            sine,
            normed,
            gains,
            dg2,
            a,
            x,
            gm,
            pq,
            *((pm, source) if last else ()),
        )
        da = pieces[0]
    parts = return_pieces(pieces[:4], pieces[4:], "y")
    first = lax.all_to_all(first, OUTER, 0, 0, tiled=True)
    grad = trade(grad)
    blocks = call(gather_second_kernel, sds((16, 36, PACK), BF16), 3, 5.0)(summed, pm, pf)
    blocks = call(gather_last_kernel, sds((16, 36, PACK + PACK_A), BF16), 6, 2.5)(
        *parts, after(blocks, grad)
    )
    rest = lax.all_to_all(blocks, OUTER, 0, 0, tiled=True)
    outs = call(
        finish_kernel,
        [
            sds((2, 72), F32),
            sds((36, 2, 72), F32),
            sds((2, 24, 36), F32),
            sds((2, 24, 36), F32),
            sds((36, 2, 72), F32),
            sds((36, 2, 192), F32),
            sds((36, 2, 192), F32),
            sds((2, 72, 96), F32),
        ],
        2,
        2.9,
    )(first, rest)
    order = (None, layer_second, turned, turned, layer_second, layer_second, layer_second, turned)
    outs = [out if axes is None else out.transpose(axes) for out, axes in zip(outs, order)]
    return (output.T[None], grad.astype(F32).T[None], *outs)


def solution(mesh):
    fine = Mesh(np.asarray(mesh.devices).reshape(SIZES), AXES)
    split = P(None, FSDP, CTX)
    rows = P(FSDP, CTX, None)
    return jax.shard_map(
        on_device,
        mesh=fine,
        in_specs=(rows, P(FSDP, None), P(None, FSDP)) + (split,) * 7 + (rows,),
        out_specs=(rows, rows, P(None, FSDP)) + (split,) * 7,
        check_vma=False,
    )
```

```python
import functools

import jax
import jax.numpy as jnp
import numpy as np
from jax import lax
from jax.experimental import pallas as pl
from jax.experimental.pallas import tpu as pltpu
from jax.sharding import Mesh
from jax.sharding import PartitionSpec as P

D = 576
HEADS = 9
KV_HEADS = 3
HEAD_DIM = 64
GROUP = HEADS // KV_HEADS
FF = 1536
ROWS = 256
BLOCK = 128
KEYS = 2048
KVD = KV_HEADS * HEAD_DIM
HALF_FF = FF // 2

rope_base = 10000.0
norm_eps = 1e-05
masked_score = -1e30
score_scale = HEAD_DIM ** (-0.5)

F32 = jnp.float32
BF16 = jnp.bfloat16

AXES = ("z", "xl", "xh", "y", "core")
SIZES = (4, 2, 2, 4, 2)
CTX = ("z", "xl")
FSDP = ("xh", "y", "core")
INNER = ("y", "core")
OUTER = ("z", "xl", "xh")

PACK = 896
PACK_A = 128
PACK_B = PACK - PACK_A
PACK_FIRST = PACK + PACK_A
PK_Q, PK_K, PK_V, PK_GAIN = 0, 72, 96, 120
PK_O, PK_G, PK_U, PK_D = 128, 200, 392, 584

A_STEP = 1024
A_WIDTH = 3 * A_STEP
B_STEP = 2 * FF
B_DOWN = 3 * B_STEP
B_OUT = B_DOWN + 8 * 512
B_DOWN_TAIL = B_OUT + 3 * 512
B_OUT_TAIL = B_DOWN_TAIL + 8 * 64
B_WIDTH = B_OUT_TAIL + 256

C_WIDTH = B_WIDTH + A_WIDTH

BYTES_PER_MICRO = 3.4e6
FLOPS_PER_MICRO = 1e9


def feature_order():
    n = np.arange(D)
    owner, i = n // 36, n % 36
    xh, yc = owner // 8, owner % 8
    local = xh * 36 + i
    return (local // 24) * 192 + yc * 24 + local % 24


def hidden_order():
    n = np.arange(HALF_FF)
    yc, i = n // 96, n % 96
    return (i // 24) * 192 + yc * 24 + i % 24


def one_hot(places):
    size = len(places)
    out = np.zeros((size, size), np.float32)
    out[np.arange(size), places] = 1.0
    return out


def gain_matrix():
    n = np.arange(D)
    yc, local = n // 72, n % 72
    gathered = (local // 24) * 192 + yc * 24 + local % 24
    out = np.zeros((D, D), np.float32)
    out[gathered, feature_order()] = 1.0
    return out


def dot(left, right):
    return lax.dot_general(left, right, (((1,), (0,)), ((), ())), preferred_element_type=F32)


def dot_rows(left, right):
    return lax.dot_general(left, right, (((0,), (0,)), ((), ())), preferred_element_type=F32)


def dot_back(left, right):
    return lax.dot_general(left, right, (((1,), (1,)), ((), ())), preferred_element_type=F32)


def call(kernel, out_shape, n_in, micros, smem=(), left=(), left_out=(), scratch=(), grant=56):
    def spec(i, left):
        return pl.BlockSpec(
            memory_space=pltpu.SMEM if i in smem else pl.ANY if i in left else pltpu.VMEM
        )

    in_specs = [spec(i, left) for i in range(n_in)]
    many = isinstance(out_shape, (list, tuple))
    return pl.pallas_call(
        kernel,
        out_shape=out_shape,
        in_specs=in_specs,
        out_specs=[
            pl.BlockSpec(memory_space=pl.ANY if i in left_out else pltpu.VMEM)
            for i in range(len(out_shape))
        ]
        if many
        else pl.BlockSpec(memory_space=pltpu.VMEM),
        scratch_shapes=list(scratch),
        compiler_params=pltpu.CompilerParams(vmem_limit_bytes=grant << 20),
        cost_estimate=pl.CostEstimate(
            flops=int(micros * FLOPS_PER_MICRO),
            bytes_accessed=int(micros * BYTES_PER_MICRO),
            transcendentals=0,
        ),
    )


def sds(shape, dtype):
    return jax.ShapeDtypeStruct(shape, dtype)


def eye(size):
    rows = lax.broadcasted_iota(jnp.int32, (size, size), 0)
    cols = lax.broadcasted_iota(jnp.int32, (size, size), 1)
    return jnp.where(rows == cols, 1.0, 0.0).astype(F32)


def pack_kernel(vec, wq, wk, wv, wo, wg, wu, wd, out, later):
    diagonal = eye(36)
    for layer in range(2):
        gains = vec[layer : layer + 1, :].astype(F32)
        first = jnp.sum(diagonal * gains[:, :36], 1, keepdims=True)
        second = jnp.sum(diagonal * gains[:, 36:72], 1, keepdims=True)
        down = wd[layer].astype(F32).T
        block = jnp.concatenate(
            [
                wq[...].astype(F32)[:, layer],
                wk[layer].astype(F32).T,
                wv[layer].astype(F32).T,
                first,
                second,
                jnp.zeros((36, 6), F32),
                wo[...].astype(F32)[:, layer],
                wg[...].astype(F32)[:, layer],
                wu[...].astype(F32)[:, layer],
                down[:36],
                down[36:72],
                jnp.concatenate([down[72:96], jnp.zeros((12, 72), F32)], 0),
                jnp.zeros((36, 96), F32),
            ],
            1,
        ).astype(BF16)
        out[:, layer * PACK_A : (layer + 1) * PACK_A] = block[:, :PACK_A]
        if layer == 0:
            out[:, 2 * PACK_A :] = block[:, PACK_A:]
        else:
            later[...] = block[:, PACK_A:]


def part_of(index, blocks, c, xh, low, high):
    return blocks[index[c * 2 + xh], :, low:high].astype(F32)


def wide_of(index, blocks, low, high):
    halves = [
        jnp.concatenate([part_of(index, blocks, c, xh, low, high) for c in range(8)], 1)
        for xh in range(2)
    ]
    return jnp.concatenate(halves, 0)


def spread_a_kernel(index, r0, r1, r2, r3, out, blocks):
    for i, piece in enumerate((r0, r1, r2, r3)):
        blocks[4 * i : 4 * i + 4] = piece[:, :, : 2 * PACK_A]
    part = functools.partial(part_of, index, blocks)
    wide = functools.partial(wide_of, index, blocks)
    for layer in range(2):
        low = layer * PACK_A
        gains = []
        for xh in range(2):
            both = part(0, xh, low + PK_GAIN, low + PK_GAIN + 2)
            gains.append(jnp.concatenate([both[:, :1], both[:, 1:]], 0))
        a = jnp.concatenate(
            [
                wide(low + PK_Q, low + PK_K),
                wide(low + PK_K, low + PK_V),
                wide(low + PK_V, low + PK_GAIN),
            ]
            + gains
            + [jnp.zeros((72, 62), F32)],
            1,
        )
        for p in range(3):
            at = layer * A_WIDTH + p * A_STEP
            out[:, at : at + A_STEP] = a[24 * p : 24 * p + 24].astype(BF16)


def spread_b_kernel(first, index, r0, r1, r2, r3, pm, pf, b_out, blocks):
    for i, piece in enumerate((r0, r1, r2, r3)):
        blocks[4 * i : 4 * i + 4] = piece[:, :, first : first + PACK_B]
    part = functools.partial(part_of, index, blocks)
    wide = functools.partial(wide_of, index, blocks)
    out = dot(wide(0, PK_G - PK_O).astype(BF16), pm[...])
    for p in range(3):
        piece = out[24 * p : 24 * p + 24].astype(BF16)
        b_out[:, B_OUT + p * 512 : B_OUT + (p + 1) * 512] = piece[:, :512]
        b_out[:, B_OUT_TAIL + p * 64 : B_OUT_TAIL + (p + 1) * 64] = piece[:, 512:]
    b_out[:, B_OUT_TAIL + 192 :] = jnp.zeros((24, 64), BF16)
    for shift, low, high in ((0, PK_G - PK_O, PK_U - PK_O), (FF, PK_U - PK_O, PK_D - PK_O)):
        natural = wide(low, high).astype(BF16)
        for half in range(2):
            placed = dot(natural[:, half * HALF_FF : (half + 1) * HALF_FF], pf[...])
            for p in range(3):
                start = p * B_STEP + shift + half * HALF_FF
                b_out[:, start : start + HALF_FF] = placed[24 * p : 24 * p + 24].astype(BF16)
    down_at = PK_D - PK_O
    for xh in range(2):
        pieces = []
        for c in range(8):
            pieces.append(
                jnp.concatenate(
                    [
                        part(c, xh, down_at, down_at + 72),
                        part(c, xh, down_at + 72, down_at + 144),
                        part(c, xh, down_at + 144, down_at + 216)[:24],
                    ],
                    0,
                )
            )
        down = dot(jnp.concatenate(pieces, 1).astype(BF16), pm[...])
        for i in range(4):
            p = xh * 4 + i
            piece = down[24 * i : 24 * i + 24].astype(BF16)
            b_out[:, B_DOWN + p * 512 : B_DOWN + (p + 1) * 512] = piece[:, :512]
            b_out[:, B_DOWN_TAIL + p * 64 : B_DOWN_TAIL + (p + 1) * 64] = piece[:, 512:]


def gathered_a(a, out, lanes):
    a72 = jnp.concatenate([a[:, p * A_STEP : (p + 1) * A_STEP] for p in range(3)], 0)
    for xh in range(2):
        rows = slice(xh * 36, xh * 36 + 36)
        gain = a72[:, 960 + xh : 961 + xh]
        for c in range(8):
            out[c * 2 + xh, :, lanes] = jnp.concatenate(
                [
                    a72[rows, c * 72 : c * 72 + 72],
                    a72[rows, 576 + c * 24 : 600 + c * 24],
                    a72[rows, 768 + c * 24 : 792 + c * 24],
                    gain[:36],
                    gain[36:72],
                    jnp.zeros((36, 6), F32),
                ],
                1,
            ).astype(BF16)


def gathered_b(b, pm, pf, out, lanes):
    o72 = jnp.concatenate(
        [
            jnp.concatenate(
                [
                    b[:, B_OUT + p * 512 : B_OUT + (p + 1) * 512].astype(F32),
                    b[:, B_OUT_TAIL + p * 64 : B_OUT_TAIL + (p + 1) * 64].astype(F32),
                ],
                1,
            )
            for p in range(3)
        ],
        0,
    )
    o72 = dot_back(o72.astype(BF16), pm[...])
    sides = []
    for shift in (0, FF):
        halves = []
        for half in range(2):
            low = shift + half * HALF_FF
            stacked = jnp.concatenate(
                [
                    b[:, p * B_STEP + low : p * B_STEP + low + HALF_FF].astype(F32)
                    for p in range(3)
                ],
                0,
            )
            halves.append(dot_back(stacked.astype(BF16), pf[...]))
        sides.append(jnp.concatenate(halves, 1))
    for xh in range(2):
        down = jnp.concatenate(
            [
                jnp.concatenate(
                    [
                        b[:, B_DOWN + p * 512 : B_DOWN + (p + 1) * 512].astype(F32),
                        b[:, B_DOWN_TAIL + p * 64 : B_DOWN_TAIL + (p + 1) * 64].astype(F32),
                    ],
                    1,
                )
                for p in range(xh * 4, xh * 4 + 4)
            ],
            0,
        )
        down = dot_back(down.astype(BF16), pm[...])
        rows = slice(xh * 36, xh * 36 + 36)
        for c in range(8):
            cols = slice(c * 72, c * 72 + 72)
            piece = down[:, cols]
            out[c * 2 + xh, :, lanes] = jnp.concatenate(
                [
                    o72[rows, cols],
                    sides[0][rows, c * 192 : c * 192 + 192],
                    sides[1][rows, c * 192 : c * 192 + 192],
                    piece[:36],
                    piece[36:72],
                    jnp.concatenate([piece[72:96], jnp.zeros((12, 72), F32)], 0),
                    jnp.zeros((36, 96), F32),
                ],
                1,
            ).astype(BF16)


def gather_first_kernel(b, pm, pf, out):
    gathered_b(b, pm, pf, out, slice(0, PACK_B))


def gather_second_kernel(c, pm, pf, out):
    gathered_b(c, pm, pf, out, slice(0, PACK_B))
    gathered_a(c[:, B_WIDTH:].astype(F32), out, slice(PACK_B, PACK))


def gather_last_kernel(a0, a1, a2, a3, a4, blocks, out):
    a = a0[...].astype(F32)
    for ref in (a1, a2, a3, a4):
        a = a + ref[...].astype(F32)
    out[:, :, PACK_A:] = blocks[...]
    gathered_a(a, out, slice(0, PACK_A))


def finish_kernel(first_ref, last_ref, vec, wq, wk, wv, wo, wg, wu, wd):
    diagonal = eye(36)

    def added(ref, low, high):
        total = ref[0, :, low:high].astype(F32)
        for i in range(1, 16):
            total = total + ref[i, :, low:high].astype(F32)
        return total

    totals = (
        added(last_ref, 0, PACK),
        jnp.concatenate([added(last_ref, PACK, PACK + PACK_A), added(first_ref, 0, PACK_B)], 1),
    )
    for layer, total in enumerate(totals):
        wq[:, layer, :] = total[:, PK_Q:PK_K]
        wk[layer] = total[:, PK_K:PK_V].T
        wv[layer] = total[:, PK_V:PK_GAIN].T
        wo[:, layer, :] = total[:, PK_O:PK_G]
        first = jnp.sum(diagonal * total[:, PK_GAIN : PK_GAIN + 1], 0, keepdims=True)
        second = jnp.sum(diagonal * total[:, PK_GAIN + 1 : PK_GAIN + 2], 0, keepdims=True)
        vec[layer : layer + 1, :] = jnp.concatenate([first, second], 1)
        wg[:, layer, :] = total[:, PK_G:PK_U]
        wu[:, layer, :] = total[:, PK_U:PK_D]
        wd[layer] = jnp.concatenate(
            [
                total[:, PK_D : PK_D + 72],
                total[:, PK_D + 72 : PK_D + 144],
                total[:24, PK_D + 144 : PK_D + 216],
            ],
            0,
        ).T


def swap_halves(tile):
    lane = lax.broadcasted_iota(jnp.int32, tile.shape, 1) % HEAD_DIM
    return jnp.where(
        lane < HEAD_DIM // 2,
        pltpu.roll(tile, 128 - HEAD_DIM // 2, 1),
        pltpu.roll(tile, HEAD_DIM // 2, 1),
    )


def place_rows(source):
    lane = lax.broadcasted_iota(jnp.int32, (192, 192), 1)
    return jnp.where(lane == source[...], 1.0, 0.0).astype(BF16)


def pre_kernel(first, source, a_in, x_ref, pm, pq, cosine, sine, a, normed_out, q_out, kv_out, gains_out, *x_out):
    a[...] = dot(place_rows(source), a_in[...]).astype(BF16)
    gains = dot_rows(a[:, 896:1024], pq[0:192, :])
    for p in range(1, 3):
        gains = gains + dot_rows(
            a[:, p * A_STEP + 896 : (p + 1) * A_STEP], pq[p * 192 : (p + 1) * 192, :]
        )
    gains = gains[64:72]
    gains_out[...] = gains
    if first:
        x = dot_rows(x_ref[:D, :], pm[...])
        x_out[0][...] = x
    else:
        x = x_ref[...]
    inverse = lax.rsqrt(jnp.mean(x * x, -1, keepdims=True) + norm_eps)
    normed = (x * inverse * gains[0:1]).astype(BF16)
    normed_out[...] = normed
    lin = dot(normed[:, :192], a[:, :A_STEP])
    for p in range(1, 3):
        lin = lin + dot(
            normed[:, p * 192 : (p + 1) * 192], a[:, p * A_STEP : (p + 1) * A_STEP]
        )
    turned = []
    for t in range(6):
        tile = lin[:, t * 128 : (t + 1) * 128]
        turned.append(tile * cosine[...] + swap_halves(tile) * sine[...])
    turned = jnp.concatenate(turned, 1)
    q_out[...] = (turned[:, :D] * score_scale).astype(BF16)
    for g in range(KV_HEADS):
        part = slice(g * HEAD_DIM, (g + 1) * HEAD_DIM)
        kv_out[:, g * PAIR : (g + 1) * PAIR] = jnp.concatenate(
            [turned[:, D:768][:, part], lin[:, 768:960][:, part]], 1
        ).astype(BF16)


def weight_back(left, b, main, tail, p):
    return dot_back(left[:, :512], b[:, main + p * 512 : main + (p + 1) * 512]) + dot_back(
        left[:, 512:], b[:, tail + p * 64 : tail + (p + 1) * 64]
    )


def fetch_b(b, held, sems):
    copies = []
    for i, (low, high) in enumerate(((0, B_DOWN), (B_DOWN, B_OUT), (B_OUT, B_WIDTH))):
        copies.append(
            pltpu.make_async_copy(b.at[:, low:high], held.at[:, low:high], sems.at[i])
        )
    return copies


def ffn_forward(o_ref, x_ref, gains, pm, b, copies, mid_out, op_out, nm_out, gate_low, up_low, hid_low):
    ffn, down, rest = copies
    op = dot(o_ref[...], pm[...]).astype(BF16)
    op_out[...] = op

    def through(left, main, tail, count):
        wide = None
        narrow = None
        for p in range(count):
            piece = left[:, p * 192 : (p + 1) * 192]
            one = dot(piece, b[:, main + p * 512 : main + (p + 1) * 512])
            two = dot(piece, b[:, tail + p * 64 : tail + (p + 1) * 64])
            wide = one if wide is None else wide + one
            narrow = two if narrow is None else narrow + two
        return jnp.concatenate([wide, narrow], 1)

    rest.wait()
    mid = x_ref[...] + through(op, B_OUT, B_OUT_TAIL, 3)
    mid_out[...] = mid
    inverse = lax.rsqrt(jnp.mean(mid * mid, -1, keepdims=True) + norm_eps)
    nm = (mid * inverse * gains[1:2, :]).astype(BF16)
    nm_out[...] = nm
    ffn.wait()
    for part in range(2):
        cols = slice(part * HALF_FF, (part + 1) * HALF_FF)
        gate, up = None, None
        for p in range(3):
            piece = nm[:, p * 192 : (p + 1) * 192]
            low = p * B_STEP + part * HALF_FF
            one = dot(piece, b[:, low : low + HALF_FF])
            two = dot(piece, b[:, low + FF : low + FF + HALF_FF])
            gate = one if gate is None else gate + one
            up = two if up is None else up + two
        gate_low[:, cols] = gate.astype(BF16)
        up_low[:, cols] = up.astype(BF16)
        hid_low[:, cols] = (gate / (1.0 + jnp.exp(-gate)) * up).astype(BF16)
    down.wait()
    return mid + through(hid_low, B_DOWN, B_DOWN_TAIL, 8)


def middle_kernel(o_ref, x_ref, gains, pm, cosine, sine, source, b_ref, a_late, pq_late, *refs):
    kept, (x_out, a, normed, q, kv, gains_out, b, a_in, pq, sems) = refs[:6], refs[6:]
    copies = fetch_b(b_ref, b, sems)
    for copy in copies[::-1]:
        copy.start()
    late = held_copies((a_late, pq_late), (a_in, pq), sems, 3)
    x_out[...] = ffn_forward(o_ref, x_ref, gains, pm, b, copies, *kept)
    for copy in late:
        copy.wait()
    pre_kernel(False, source, a_in, x_out, pm, pq, cosine, sine, a, normed, q, kv, gains_out)


def norm_back(dy, v, gain):
    inverse = lax.rsqrt(jnp.mean(v * v, -1, keepdims=True) + norm_eps)
    scaled = dy * gain
    back = inverse * scaled - v * (
        inverse * inverse * inverse * jnp.mean(scaled * v, -1, keepdims=True)
    )
    return back, jnp.sum(dy * v * inverse, 0, keepdims=True)


class Sender:
    def __init__(self, db, db_out, sems):
        self.db, self.db_out, self.sems, self.sent = db, db_out, sems, []

    def send(self, low, high, source=None):
        source = self.db.at[:, low:high] if source is None else source
        self.sent.append(
            pltpu.make_async_copy(
                source, self.db_out.at[:, low:high], self.sems.at[3 + len(self.sent)]
            )
        )
        self.sent[-1].start()

    def wait(self):
        for copy in self.sent:
            copy.wait()


def ffn_backward(
    g,
    nm,
    gate_ref,
    up_ref,
    hid,
    mid,
    op,
    gains,
    pm,
    b,
    copies,
    sender,
    gm_out,
    do_out,
    dg_out,
    late=(),
):
    db = sender.db
    gb = g.astype(BF16)
    for p in range(8):
        piece = dot_rows(hid[:, p * 192 : (p + 1) * 192], gb)
        db[:, B_DOWN + p * 512 : B_DOWN + (p + 1) * 512] = piece[:, :512].astype(BF16)
        db[:, B_DOWN_TAIL + p * 64 : B_DOWN_TAIL + (p + 1) * 64] = piece[:, 512:].astype(BF16)
    sender.send(B_DOWN, B_OUT)
    for copy in copies[1:]:
        copy.wait()
    dh = jnp.concatenate([weight_back(gb, b, B_DOWN, B_DOWN_TAIL, p) for p in range(8)], 1)
    for copy in late[:3]:
        copy.wait()
    gate = gate_ref[...].astype(F32)
    up = up_ref[...].astype(F32)
    sig = 1.0 / (1.0 + jnp.exp(-gate))
    d_gate = (dh * up * sig * (1.0 + gate * (1.0 - sig))).astype(BF16)
    d_up = (dh * (gate * sig)).astype(BF16)
    for p in range(3):
        piece = nm[:, p * 192 : (p + 1) * 192]
        low = p * B_STEP
        db[:, low : low + FF] = dot_rows(piece, d_gate).astype(BF16)
        db[:, low + FF : low + B_STEP] = dot_rows(piece, d_up).astype(BF16)
        sender.send(low, low + B_STEP)
    for copy in copies[:1]:
        copy.wait()
    for copy in late[3:]:
        copy.wait()
    dnm = []
    for p in range(3):
        low = p * B_STEP
        dnm.append(
            dot_back(d_gate, b[:, low : low + FF])
            + dot_back(d_up, b[:, low + FF : low + B_STEP])
        )
    back, gain_grad = norm_back(jnp.concatenate(dnm, 1), mid[...], gains[1:2, :])
    dg_out[...] = gain_grad
    gm = g + back
    gm_out[...] = gm
    gmb = gm.astype(BF16)
    dop = []
    for p in range(3):
        piece = dot_rows(op[:, p * 192 : (p + 1) * 192], gmb)
        db[:, B_OUT + p * 512 : B_OUT + (p + 1) * 512] = piece[:, :512].astype(BF16)
        db[:, B_OUT_TAIL + p * 64 : B_OUT_TAIL + (p + 1) * 64] = piece[:, 512:].astype(BF16)
        dop.append(weight_back(gmb, b, B_OUT, B_OUT_TAIL, p))
    db[:, B_OUT_TAIL + 192 : B_WIDTH] = jnp.zeros((192, 64), BF16)
    sender.send(B_OUT, B_WIDTH)
    do_out[...] = dot_back(jnp.concatenate(dop, 1).astype(BF16), pm[...]).astype(BF16)
    sender.wait()


def held_copies(refs, held, sems, first):
    copies = [
        pltpu.make_async_copy(ref, target, sems.at[first + i])
        for i, (ref, target) in enumerate(zip(refs, held))
    ]
    for copy in copies:
        copy.start()
    return copies


def turn_kernel(o_ref, x_ref, gains, traded, pm, b_ref, *refs):
    x_out, db_out, gm_out, do_out, dg_out, b, db, mid, op, nm, gate, up, hid, sems = refs
    copies = fetch_b(b_ref, b, sems)
    for copy in copies[::-1]:
        copy.start()
    out = ffn_forward(o_ref, x_ref, gains, pm, b, copies, mid, op, nm, gate, up, hid)
    x_out[...] = dot_back(pm[...], out.astype(BF16)).astype(BF16)
    g = dot_rows(traded[D : 2 * D, :], pm[...])
    sender = Sender(db, db_out, sems)
    ffn_backward(
        g, nm, gate, up, hid, mid, op, gains, pm, b, (), sender, gm_out, do_out, dg_out
    )


def qkv_back_kernel(
    last, dq, kv0, kv1, kv2, kv3, kv4, cosine, sine, normed, gains, dg2, a_ref, x_late, gm_late, pq_late, *refs,
    started=None,
):
    if last:
        pm_ref, source, x_out, *da_refs, da, a, x_ref, gm, pq, pm, sems = refs
        late = held_copies((a_ref, x_late, gm_late, pq_late, pm_ref), (a, x_ref, gm, pq, pm), sems, 0)
    else:
        x_out, da, a, x_ref, gm, pq, sems = refs
        late = held_copies((a_ref, x_late, gm_late, pq_late), (a, x_ref, gm, pq), sems, 0)
        started()
    dkv = kv0[...].astype(F32)
    for ref in (kv1, kv2, kv3, kv4):
        dkv = dkv + ref[...].astype(F32)
    d_key = [dkv[:, g * PAIR : g * PAIR + HEAD_DIM] for g in range(KV_HEADS)]
    d_value = [dkv[:, g * PAIR + HEAD_DIM : (g + 1) * PAIR] for g in range(KV_HEADS)]
    rot = jnp.concatenate([dq[...]] + d_key, 1)
    turned = []
    for t in range(6):
        tile = rot[:, t * 128 : (t + 1) * 128]
        turned.append(tile * cosine[...] - swap_halves(tile) * sine[...])
    dqkv = jnp.concatenate(turned + d_value + [jnp.zeros((ROWS, 64), F32)], 1).astype(BF16)
    late[0].wait()
    dn = []
    for p in range(3):
        low = p * A_STEP
        da[:, low : low + A_STEP] = dot_rows(
            normed[:, p * 192 : (p + 1) * 192], dqkv
        ).astype(BF16)
        dn.append(dot_back(dqkv, a[:, low : low + A_STEP]))
    for copy in late[1:]:
        copy.wait()
    x = x_ref[...]
    back, dg1 = norm_back(jnp.concatenate(dn, 1), x, gains[0:1, :])
    rows = lax.broadcasted_iota(jnp.int32, (64, D), 0)
    stacked = jnp.where(rows == 0, dg1, jnp.where(rows == 1, dg2[...], 0.0)).astype(BF16)
    placed = dot_back(pq[...], stacked).astype(BF16)
    for p in range(3):
        da[:, p * A_STEP + 960 : (p + 1) * A_STEP] = placed[p * 192 : (p + 1) * 192]
    out = gm[...] + back
    if last:
        x_out[...] = dot_back(pm[...], out.astype(BF16)).astype(BF16)
        placed = dot_rows(place_rows(source), da[...])
        for i, ref in enumerate(da_refs):
            ref[...] = placed[i * 24 : (i + 1) * 24].astype(BF16)
    else:
        x_out[...] = out


def back_kernel(*args):
    qkv_args, (gains, hid, gate, up, nm, mid, op, pm, b_ref), refs = args[:15], args[15:24], args[24:]
    db_out, gm_out, do_out, dg_out, grad, da, a, x, gm, pq, *held, b, db, qkv_sems, sems = refs
    copies = fetch_b(b_ref, b, sems)
    late = []

    def started():
        late.extend(held_copies((hid,), held[:1], sems, 9))
        copies[2].start()
        copies[1].start()
        late.extend(held_copies((gate, up, nm), held[1:4], sems, 10))
        copies[0].start()
        late.extend(held_copies((mid, op, pm), held[4:], sems, 13))

    qkv_back_kernel(False, *qkv_args, grad, da, a, x, gm, pq, qkv_sems, started=started)
    sender = Sender(db, db_out, sems)
    sender.send(B_WIDTH, C_WIDTH, da)
    late[0].wait()
    hid, gate, up, nm, mid, op, pm = held
    ffn_backward(
        grad[...], nm, gate, up, hid, mid, op, gains, pm, b,
        copies, sender, gm_out, do_out, dg_out, late[1:],
    )


PAIR = 2 * HEAD_DIM
WIDE = GROUP * BLOCK
CHUNK = 256
STEPS = KEYS // CHUNK + 1
SLOTS = 2 * KV_HEADS


def load_heads(ref, scratch, run, upper):
    zero = jnp.zeros((WIDE, HEAD_DIM), BF16)
    for g in range(KV_HEADS):
        heads = jnp.concatenate(
            [
                ref[
                    run * BLOCK : (run + 1) * BLOCK,
                    (g * GROUP + h) * HEAD_DIM : (g * GROUP + h + 1) * HEAD_DIM,
                ]
                for h in range(GROUP)
            ],
            0,
        )
        both = [zero, heads] if upper else [heads, zero]
        scratch[run * KV_HEADS + g] = jnp.concatenate(both, 1)


def sort_keys(table, pieces, kvs):
    for j in range(KEYS // BLOCK):
        start = pl.multiple_of(table[2 + j] * BLOCK, BLOCK)
        kvs[pl.ds(start, BLOCK), :] = pieces[j // 2][(j % 2) * BLOCK : (j % 2 + 1) * BLOCK, :]


def set_lead(lead):
    key = lax.broadcasted_iota(jnp.int32, (CHUNK, BLOCK), 0)
    row = lax.broadcasted_iota(jnp.int32, (CHUNK, BLOCK), 1)
    lead[...] = row - key


def head_columns(h):
    return slice(h * BLOCK, (h + 1) * BLOCK)


def step_of(table, it):
    first = (table[0] + 2) // 2
    second = it >= first
    run = jnp.where(second, 1, 0)
    chunk = jnp.where(second, it - first, it)
    block = jnp.where(second, table[1], table[0])
    return run, pl.multiple_of(chunk * CHUNK, CHUNK), chunk * CHUNK - block * BLOCK


def attend_kernel(table, q_ref, *refs):
    pieces, (o_out, lse_out, kvs, qs, lead, ms, ls, acc) = refs[:8], refs[8:]
    sort_keys(table, pieces, kvs)
    load_heads(q_ref, qs, 0, False)
    load_heads(q_ref, qs, 1, False)
    set_lead(lead)
    ms[...] = jnp.full(ms.shape, masked_score, F32)
    ls[...] = jnp.zeros(ls.shape, F32)
    acc[...] = jnp.zeros(acc.shape, F32)

    def step(it, carry):
        run, start, least = step_of(table, it)
        results = []
        for g in range(KV_HEADS):
            at = run * KV_HEADS + g
            kv = kvs[pl.ds(start, CHUNK), g * PAIR : (g + 1) * PAIR]
            turned = kv.T
            for h in range(GROUP):
                part = head_columns(h)
                scores = dot_back(kv, qs[at, part, :])
                scores = jnp.where(lead[...] >= least, scores, masked_score)
                before = ms[at, :, part]
                now = jnp.maximum(before, jnp.max(scores, 0, keepdims=True))
                raised = jnp.exp(scores - now)
                shrink = jnp.exp(before - now)
                total = ls[at, :, part] * shrink + jnp.sum(raised, 0, keepdims=True)
                out = dot(turned, raised.astype(BF16))[HEAD_DIM:]
                results.append((at, part, now, total, acc[at, :, part] * shrink + out))
        for at, part, now, total, out in results:
            ms[at, :, part] = now
            ls[at, :, part] = total
            acc[at, :, part] = out
        return carry

    lax.fori_loop(0, STEPS, step, 0, unroll=STEPS)
    for run in range(2):
        for g in range(KV_HEADS):
            at = run * KV_HEADS + g
            total = ls[at]
            lse_out[at] = ms[at] + jnp.log(total)
            heads = (acc[at] / total).T
            for h in range(GROUP):
                o_out[
                    run * BLOCK : (run + 1) * BLOCK,
                    (g * GROUP + h) * HEAD_DIM : (g * GROUP + h + 1) * HEAD_DIM,
                ] = heads[h * BLOCK : (h + 1) * BLOCK].astype(BF16)


def attend_back_kernel(table, q_ref, o_ref, do_ref, lse, *refs):
    pieces = refs[:8]
    dq_out, outs, (kvs, qs, dos, lead, deltas, dkvs, dqs) = refs[8], refs[9:17], refs[17:]
    sort_keys(table, pieces, kvs)
    set_lead(lead)
    for run in range(2):
        load_heads(q_ref, qs, run, False)
        load_heads(do_ref, dos, run, True)
        rows = slice(run * BLOCK, (run + 1) * BLOCK)
        product = o_ref[rows, :].astype(F32) * do_ref[rows, :].astype(F32)
        turned = jnp.concatenate([product, jnp.zeros((BLOCK, HEAD_DIM), F32)], 1).T
        for g in range(KV_HEADS):
            deltas[run * KV_HEADS + g] = jnp.concatenate(
                [
                    jnp.sum(turned[h * HEAD_DIM : (h + 1) * HEAD_DIM], 0, keepdims=True)
                    for h in range(g * GROUP, (g + 1) * GROUP)
                ],
                1,
            )
    dkvs[...] = jnp.zeros(dkvs.shape, F32)
    dqs[...] = jnp.zeros(dqs.shape, F32)

    def step(it, carry):
        run, start, least = step_of(table, it)
        scores, d_probs, low_probs, d_scores, results = [], [], [], [], []
        for g in range(KV_HEADS):
            at = run * KV_HEADS + g
            kv = kvs[pl.ds(start, CHUNK), g * PAIR : (g + 1) * PAIR]
            scores.append(dot_back(kv, qs[at]))
            d_probs.append(dot_back(kv, dos[at]))
        ahead = jnp.concatenate([lead[...]] * GROUP, 1) >= least
        for g in range(KV_HEADS):
            at = run * KV_HEADS + g
            probs = jnp.exp(jnp.where(ahead, scores[g], masked_score) - lse[at])
            low_probs.append(probs.astype(BF16))
            d_scores.append((probs * (d_probs[g] - deltas[at])).astype(BF16))
        for g in range(KV_HEADS):
            at = run * KV_HEADS + g
            kv = kvs[pl.ds(start, CHUNK), g * PAIR : (g + 1) * PAIR]
            d_kv = dot(d_scores[g], qs[at]) + dot(low_probs[g], dos[at])
            results.append((at, d_kv, dot_rows(kv, d_scores[g])[:HEAD_DIM]))
        for g, (at, d_kv, d_q) in enumerate(results):
            dkvs[g, pl.ds(start, CHUNK), :] += d_kv
            dqs[at] += d_q
        return carry

    lax.fori_loop(0, STEPS, step, 0, unroll=STEPS)
    for run in range(2):
        for g in range(KV_HEADS):
            heads = (dqs[run * KV_HEADS + g] * score_scale).T
            for h in range(GROUP):
                dq_out[
                    run * BLOCK : (run + 1) * BLOCK,
                    (g * GROUP + h) * HEAD_DIM : (g * GROUP + h + 1) * HEAD_DIM,
                ] = heads[h * BLOCK : (h + 1) * BLOCK]
    for j in range(KEYS // BLOCK):
        start = pl.multiple_of(table[2 + j] * BLOCK, BLOCK)
        rows = slice((j % 2) * BLOCK, (j % 2 + 1) * BLOCK)
        for g in range(KV_HEADS):
            outs[j // 2][rows, g * PAIR : (g + 1) * PAIR] = dkvs[
                g, pl.ds(start, BLOCK), :
            ].astype(BF16)


def attend(table, q, kv_all):
    return call(
        attend_kernel,
        [sds((ROWS, D), BF16), sds((SLOTS, 1, WIDE), F32)],
        10,
        6.9,
        grant=16,
        smem=(0,),
        scratch=[
            pltpu.VMEM((KEYS, KV_HEADS * PAIR), BF16),
            pltpu.VMEM((SLOTS, WIDE, PAIR), BF16),
            pltpu.VMEM((CHUNK, BLOCK), jnp.int32),
            pltpu.VMEM((SLOTS, 1, WIDE), F32),
            pltpu.VMEM((SLOTS, 1, WIDE), F32),
            pltpu.VMEM((SLOTS, HEAD_DIM, WIDE), F32),
        ],
    )(table, q, *kv_all)


def attend_back(table, q, kv_all, o, do, lse):
    return call(
        attend_back_kernel,
        [sds((ROWS, D), F32)] + [sds((ROWS, 2 * KVD), BF16)] * 8,
        13,
        11.3,
        smem=(0,),
        scratch=[
            pltpu.VMEM((KEYS, KV_HEADS * PAIR), BF16),
            pltpu.VMEM((SLOTS, WIDE, PAIR), BF16),
            pltpu.VMEM((SLOTS, WIDE, PAIR), BF16),
            pltpu.VMEM((CHUNK, BLOCK), jnp.int32),
            pltpu.VMEM((SLOTS, 1, WIDE), F32),
            pltpu.VMEM((KV_HEADS, KEYS, PAIR), F32),
            pltpu.VMEM((SLOTS, HEAD_DIM, WIDE), F32),
        ],
    )(table, q, o, do, lse, *kv_all)


def ring(shift):
    return [(i, (i + shift) % 4) for i in range(4)]


def ring_x(shift):
    pairs = []
    for x in range(4):
        to = (x + shift) % 4
        pairs.append(((x % 2) * 2 + x // 2, (to % 2) * 2 + to // 2))
    return pairs


SHIFTS = (1, -1, 2)


def from_x(value):
    return [value] + [lax.ppermute(value, ("xl", "xh"), ring_x(s)) for s in SHIFTS]


def from_ring(value, axis):
    return [value] + [lax.ppermute(value, axis, ring(s)) for s in SHIFTS]


def other_core(value):
    return lax.ppermute(value, "core", [(0, 1), (1, 0)])


def trade(value):
    return lax.ppermute(value, ("xl", "core"), [(0, 0), (1, 2), (2, 1), (3, 3)])


def place_of(distance):
    distance = distance % 4
    return distance ^ (distance >> 1)


def block_index():
    z, xl, xh = (lax.axis_index(name) for name in OUTER)
    block = jnp.arange(16, dtype=jnp.int32)
    along_x = place_of(xh * 2 + xl - (block % 2) * 2 - (block // 2) % 2)
    along_z = place_of(z - block // 4)
    return along_z * 4 + along_x, along_x * 4 + along_z


def row_source():
    y, core = lax.axis_index("y"), lax.axis_index("core")
    rows = jnp.arange(192, dtype=jnp.int32)
    owner, j = rows // 24, rows % 24
    piece = ((owner + core) % 2) * 4 + place_of(y - owner // 2)
    return (piece * 24 + j)[:, None]


def spread_a(index, blocks):
    return call(
        spread_a_kernel,
        sds((24, 2 * A_WIDTH), BF16),
        5,
        3.0,
        smem=(0,),
        scratch=[pltpu.VMEM((16, 36, 2 * PACK_A), BF16)],
        grant=16,
    )(index, *blocks)


def spread_b(first, index, blocks, pm, pf):
    return call(
        functools.partial(spread_b_kernel, first),
        sds((24, B_WIDTH), BF16),
        7,
        4.3,
        smem=(0,),
        scratch=[pltpu.VMEM((16, 36, PACK_B), BF16)],
        grant=16,
    )(index, *blocks, pm, pf)


def share(near):
    return near + [other_core(piece) for piece in near]


def return_pieces(near, far, axis):
    far = [other_core(piece) for piece in far]
    both = [(n.astype(F32) + f.astype(F32)).astype(BF16) for n, f in zip(near[1:], far[1:])]
    back = [lax.ppermute(piece, axis, ring(-s)) for piece, s in zip(both, SHIFTS)]
    return [near[0], far[0]] + back


def key_table(starts):
    z, core = lax.axis_index("z"), lax.axis_index("core")
    j = np.arange(18) - 2
    shift = np.where(j < 0, 0, np.array((0,) + SHIFTS)[(j // 2) % 4]).astype(np.int32)
    far = np.where(j < 0, 0, j // 8).astype(np.int32)
    wanted = (((z - shift) % 4) * 2 + (core + far) % 2) * 2 + (j % 2).astype(np.int32)
    match = wanted[:, None] == jnp.arange(16, dtype=jnp.int32)[None, :]
    return jnp.sum(jnp.where(match, starts[None, :], 0), 1)


def angles(places):
    half_dim = HEAD_DIM // 2
    inverse = rope_base ** (-2.0 * jnp.arange(half_dim).astype(F32) / HEAD_DIM)
    turned = places.astype(F32)[:, None] * inverse[None, :]
    cosine, sine = jnp.cos(turned), jnp.sin(turned)
    return jnp.concatenate([cosine] * 4, 1), jnp.concatenate([-sine, sine] * 2, 1)


def after(value, *others):
    return lax.optimization_barrier((value, *others))[0]


def on_device(
    tokens, positions, vectors, w_query, w_key, w_value, w_out, w_gate, w_up, w_down, cotangent
):
    pm = jnp.asarray(one_hot(feature_order()), BF16)
    pf = jnp.asarray(one_hot(hidden_order()), BF16)
    pq = jnp.asarray(gain_matrix(), BF16)
    index, z_index = block_index()
    source = row_source()
    layer_second = (1, 0, 2)
    turned = (0, 2, 1)
    pack, later = call(
        pack_kernel, [sds((36, PACK_FIRST), BF16), sds((36, PACK_B), BF16)], 8, 1.9
    )(
        vectors,
        w_query.transpose(layer_second),
        w_key.transpose(turned),
        w_value.transpose(turned),
        w_out.transpose(layer_second),
        w_gate.transpose(layer_second),
        w_up.transpose(layer_second),
        w_down.transpose(turned),
    )
    later = jnp.stack(from_ring(later, "z"))
    blocks = from_ring(after(jnp.stack(from_x(pack)), later), "z")
    a_near = spread_a(index, blocks)
    near = from_ring(a_near, "y")
    later = from_x(after(later, a_near))
    both = share(near)
    a_near, a1_near = (
        jnp.concatenate([piece[:, low : low + A_WIDTH] for piece in both], 0)
        for low in (0, A_WIDTH)
    )
    blocks = [after(blocks[0], *near[1:])] + blocks[1:]
    b0 = lax.all_gather(
        spread_b(2 * PACK_A, index, blocks, pm, pf), INNER, axis=0, tiled=True
    )

    starts = jnp.broadcast_to((positions[0, ::BLOCK] // BLOCK).astype(BF16)[:, None], (16, ROWS))
    traded = jnp.concatenate([tokens[0].T, cotangent[0].T, starts], 0)
    traded = trade(after(traded, blocks[3]))
    table = key_table(traded[2 * D :, 0].astype(jnp.int32))
    places = (table[:2, None] * BLOCK + jnp.arange(BLOCK)[None, :]).reshape(ROWS)
    cosine, sine = angles(places)
    x = traded

    pre_shapes = [
        sds((192, A_WIDTH), BF16),
        sds((ROWS, D), BF16),
        sds((ROWS, D), BF16),
        sds((ROWS, 2 * KVD), BF16),
        sds((8, D), F32),
    ]
    a, normed, q, kv, gains, x = call(
        functools.partial(pre_kernel, True), pre_shapes + [sds((ROWS, D), F32)], 7, 5.0, grant=16
    )(source, a_near, traded, pm, pq, cosine, sine)
    near = from_ring(kv, "z")
    later = [after(later[0], *near[1:])] + later[1:]
    b1 = lax.all_gather(spread_b(0, z_index, later, pm, pf), INNER, axis=0, tiled=True)
    kv_all = share(near)
    o, lse = attend(table, q, kv_all)
    first_layer = (x, a, normed, q, kv_all, gains, o, lse)

    *kept, x, a, normed, q, kv, gains = call(
        middle_kernel,
        [
            sds((ROWS, D), F32),
            sds((ROWS, D), BF16),
            sds((ROWS, D), BF16),
            sds((ROWS, FF), BF16),
            sds((ROWS, FF), BF16),
            sds((ROWS, FF), BF16),
            sds((ROWS, D), F32),
        ]
        + pre_shapes,
        10,
        10.0,
        left=(7, 8, 9),
        scratch=[
            pltpu.VMEM((192, B_WIDTH), BF16),
            pltpu.VMEM((192, A_WIDTH), BF16),
            pltpu.VMEM((D, D), BF16),
            pltpu.SemaphoreType.DMA((5,)),
        ],
    )(o, x, gains, pm, cosine, sine, source, b0, a1_near, pq)
    kv_all = share(from_ring(kv, "z"))
    o, lse = attend(table, q, kv_all)

    back_shapes = [sds((ROWS, D), F32), sds((ROWS, D), BF16), sds((1, D), F32)]
    back_scratch = [pltpu.VMEM((192, B_WIDTH), BF16)] * 2
    ffn_scratch = [
        pltpu.VMEM((ROWS, FF), BF16),
        pltpu.VMEM((ROWS, FF), BF16),
        pltpu.VMEM((ROWS, FF), BF16),
        pltpu.VMEM((ROWS, D), BF16),
        pltpu.VMEM((ROWS, D), F32),
        pltpu.VMEM((ROWS, D), BF16),
    ]
    output, db, gm, do, dg2 = call(
        turn_kernel,
        [sds((D, ROWS), BF16), sds((192, B_WIDTH), BF16)] + back_shapes,
        6,
        17.0,
        left=(5,),
        left_out=(1,),
        scratch=back_scratch
        + [
            pltpu.VMEM((ROWS, D), F32),
            pltpu.VMEM((ROWS, D), BF16),
            pltpu.VMEM((ROWS, D), BF16),
            pltpu.VMEM((ROWS, FF), BF16),
            pltpu.VMEM((ROWS, FF), BF16),
            pltpu.VMEM((ROWS, FF), BF16),
            pltpu.SemaphoreType.DMA((8,)),
        ],
    )(o, x, gains, traded, pm, b1)
    output = trade(output)
    first = lax.psum_scatter(db, INNER, scatter_dimension=0, tiled=True)
    dq, *pieces = attend_back(table, q, kv_all, o, do, lse)
    parts = return_pieces(pieces[:4], pieces[4:], "z")
    parts[0] = after(parts[0], output)
    held = [
        pltpu.VMEM((192, A_WIDTH), BF16),
        pltpu.VMEM((ROWS, D), F32),
        pltpu.VMEM((ROWS, D), F32),
        pltpu.VMEM((D, D), BF16),
    ]
    second_layer = (dq, *parts, cosine, sine, normed, gains, dg2, a, x, gm, pq)

    x, a, normed, q, kv_all, gains, o, lse = first_layer
    mid, op, nm, gate, up, hid = kept
    db, gm, do, dg2 = call(
        back_kernel,
        [sds((192, C_WIDTH), BF16)] + back_shapes,
        24,
        16.0,
        left=(*range(11, 15), *range(16, 24)),
        left_out=(0,),
        scratch=[pltpu.VMEM((ROWS, D), F32), pltpu.VMEM((192, A_WIDTH), BF16)]
        + held
        + ffn_scratch
        + [pltpu.VMEM((D, D), BF16)]
        + back_scratch
        + [pltpu.SemaphoreType.DMA((4,)), pltpu.SemaphoreType.DMA((16,))],
    )(*second_layer, gains, hid, gate, up, nm, mid, op, pm, b0)
    summed = lax.psum_scatter(db, INNER, scatter_dimension=0, tiled=True)
    dq, *pieces = attend_back(table, q, kv_all, o, do, lse)
    parts = return_pieces(pieces[:4], pieces[4:], "z")
    first = call(gather_first_kernel, sds((16, 36, PACK_B), BF16), 3, 5.0, grant=16)(
        after(first, parts[1]), pm, pf
    )
    parts[0] = after(parts[0], first)
    grad, *pieces = call(
        functools.partial(qkv_back_kernel, True),
        [sds((D, ROWS), BF16)] + [sds((24, A_WIDTH), BF16)] * 8,
        17,
        6.4,
        grant=20,
        left=range(11, 16),
        scratch=[pltpu.VMEM((192, A_WIDTH), BF16)]
        + held
        + [pltpu.VMEM((D, D), BF16), pltpu.SemaphoreType.DMA((5,))],
    )(dq, *parts, cosine, sine, normed, gains, dg2, a, x, gm, pq, pm, source)
    parts = return_pieces(pieces[:4], pieces[4:], "y")
    first = lax.all_to_all(first, OUTER, 0, 0, tiled=True)
    grad = trade(grad)
    blocks = call(gather_second_kernel, sds((16, 36, PACK), BF16), 3, 5.0, grant=16)(summed, pm, pf)
    blocks = call(gather_last_kernel, sds((16, 36, PACK + PACK_A), BF16), 6, 2.5, grant=16)(
        *parts, blocks
    )
    rest = lax.all_to_all(after(blocks, grad), OUTER, 0, 0, tiled=True)
    outs = call(
        finish_kernel,
        [
            sds((2, 72), F32),
            sds((36, 2, 72), F32),
            sds((2, 24, 36), F32),
            sds((2, 24, 36), F32),
            sds((36, 2, 72), F32),
            sds((36, 2, 192), F32),
            sds((36, 2, 192), F32),
            sds((2, 72, 96), F32),
        ],
        2,
        2.9,
        grant=16,
    )(first, rest)
    order = (None, layer_second, turned, turned, layer_second, layer_second, layer_second, turned)
    outs = [out if axes is None else out.transpose(axes) for out, axes in zip(outs, order)]
    return (output.T[None], grad.astype(F32).T[None], *outs)


def solution(mesh):
    fine = Mesh(np.asarray(mesh.devices).reshape(SIZES), AXES)
    split = P(None, FSDP, CTX)
    rows = P(FSDP, CTX, None)
    return jax.shard_map(
        on_device,
        mesh=fine,
        in_specs=(rows, P(FSDP, None), P(None, FSDP)) + (split,) * 7 + (rows,),
        out_specs=(rows, rows, P(None, FSDP)) + (split,) * 7,
        check_vma=False,
    )
```

```python
import functools

import jax
import jax.numpy as jnp
import numpy as np
from jax import lax
from jax.experimental import pallas as pl
from jax.experimental.pallas import tpu as pltpu
from jax.sharding import Mesh
from jax.sharding import PartitionSpec as P

D = 576
HEADS = 9
KV_HEADS = 3
HEAD_DIM = 64
GROUP = HEADS // KV_HEADS
FF = 1536
ROWS = 256
BLOCK = 128
KEYS = 2048
KVD = KV_HEADS * HEAD_DIM
HALF_FF = FF // 2

rope_base = 10000.0
norm_eps = 1e-05
masked_score = -1e30
score_scale = HEAD_DIM ** (-0.5)

F32 = jnp.float32
BF16 = jnp.bfloat16

AXES = ("z", "xl", "xh", "y", "core")
SIZES = (4, 2, 2, 4, 2)
CTX = ("z", "xl")
FSDP = ("xh", "y", "core")
INNER = ("y", "core")
OUTER = ("z", "xl", "xh")

PACK = 896
PACK_A = 128
PACK_B = PACK - PACK_A
PACK_FIRST = PACK + PACK_A
PK_Q, PK_K, PK_V, PK_GAIN = 0, 72, 96, 120
PK_O, PK_G, PK_U, PK_D = 128, 200, 392, 584

A_STEP = 1024
A_WIDTH = 3 * A_STEP
B_STEP = 2 * FF
B_DOWN = 3 * B_STEP
B_OUT = B_DOWN + 8 * 512
B_DOWN_TAIL = B_OUT + 3 * 512
B_OUT_TAIL = B_DOWN_TAIL + 8 * 64
B_WIDTH = B_OUT_TAIL + 256

C_WIDTH = B_WIDTH + A_WIDTH

BYTES_PER_MICRO = 3.4e6
FLOPS_PER_MICRO = 1e9


def feature_order():
    n = np.arange(D)
    owner, i = n // 36, n % 36
    xh, yc = owner // 8, owner % 8
    local = xh * 36 + i
    return (local // 24) * 192 + yc * 24 + local % 24


def hidden_order():
    n = np.arange(HALF_FF)
    yc, i = n // 96, n % 96
    return (i // 24) * 192 + yc * 24 + i % 24


def one_hot(places):
    size = len(places)
    out = np.zeros((size, size), np.float32)
    out[np.arange(size), places] = 1.0
    return out


def gain_matrix():
    n = np.arange(D)
    yc, local = n // 72, n % 72
    gathered = (local // 24) * 192 + yc * 24 + local % 24
    out = np.zeros((D, D), np.float32)
    out[gathered, feature_order()] = 1.0
    return out


def dot(left, right):
    return lax.dot_general(left, right, (((1,), (0,)), ((), ())), preferred_element_type=F32)


def dot_rows(left, right):
    return lax.dot_general(left, right, (((0,), (0,)), ((), ())), preferred_element_type=F32)


def dot_back(left, right):
    return lax.dot_general(left, right, (((1,), (1,)), ((), ())), preferred_element_type=F32)


def call(kernel, out_shape, n_in, micros, smem=(), left=(), left_out=(), scratch=(), grant=56):
    def spec(i, left):
        return pl.BlockSpec(
            memory_space=pltpu.SMEM if i in smem else pl.ANY if i in left else pltpu.VMEM
        )

    in_specs = [spec(i, left) for i in range(n_in)]
    many = isinstance(out_shape, (list, tuple))
    return pl.pallas_call(
        kernel,
        out_shape=out_shape,
        in_specs=in_specs,
        out_specs=[
            pl.BlockSpec(memory_space=pl.ANY if i in left_out else pltpu.VMEM)
            for i in range(len(out_shape))
        ]
        if many
        else pl.BlockSpec(memory_space=pltpu.VMEM),
        scratch_shapes=list(scratch),
        compiler_params=pltpu.CompilerParams(vmem_limit_bytes=grant << 20),
        cost_estimate=pl.CostEstimate(
            flops=int(micros * FLOPS_PER_MICRO),
            bytes_accessed=int(micros * BYTES_PER_MICRO),
            transcendentals=0,
        ),
    )


def sds(shape, dtype):
    return jax.ShapeDtypeStruct(shape, dtype)


def eye(size):
    rows = lax.broadcasted_iota(jnp.int32, (size, size), 0)
    cols = lax.broadcasted_iota(jnp.int32, (size, size), 1)
    return jnp.where(rows == cols, 1.0, 0.0).astype(F32)


def pack_kernel(vec, wq, wk, wv, wo, wg, wu, wd, out, later):
    diagonal = eye(36)
    for layer in range(2):
        gains = vec[layer : layer + 1, :].astype(F32)
        first = jnp.sum(diagonal * gains[:, :36], 1, keepdims=True)
        second = jnp.sum(diagonal * gains[:, 36:72], 1, keepdims=True)
        down = wd[layer].astype(F32).T
        block = jnp.concatenate(
            [
                wq[...].astype(F32)[:, layer],
                wk[layer].astype(F32).T,
                wv[layer].astype(F32).T,
                first,
                second,
                jnp.zeros((36, 6), F32),
                wo[...].astype(F32)[:, layer],
                wg[...].astype(F32)[:, layer],
                wu[...].astype(F32)[:, layer],
                down[:36],
                down[36:72],
                jnp.concatenate([down[72:96], jnp.zeros((12, 72), F32)], 0),
                jnp.zeros((36, 96), F32),
            ],
            1,
        ).astype(BF16)
        out[:, layer * PACK_A : (layer + 1) * PACK_A] = block[:, :PACK_A]
        if layer == 0:
            out[:, 2 * PACK_A :] = block[:, PACK_A:]
        else:
            later[...] = block[:, PACK_A:]


def part_of(index, blocks, c, xh, low, high):
    return blocks[index[c * 2 + xh], :, low:high].astype(F32)


def wide_of(index, blocks, low, high):
    halves = [
        jnp.concatenate([part_of(index, blocks, c, xh, low, high) for c in range(8)], 1)
        for xh in range(2)
    ]
    return jnp.concatenate(halves, 0)


def spread_a_kernel(index, r0, r1, r2, r3, out, blocks):
    for i, piece in enumerate((r0, r1, r2, r3)):
        blocks[4 * i : 4 * i + 4] = piece[:, :, : 2 * PACK_A]
    part = functools.partial(part_of, index, blocks)
    wide = functools.partial(wide_of, index, blocks)
    for layer in range(2):
        low = layer * PACK_A
        gains = []
        for xh in range(2):
            both = part(0, xh, low + PK_GAIN, low + PK_GAIN + 2)
            gains.append(jnp.concatenate([both[:, :1], both[:, 1:]], 0))
        a = jnp.concatenate(
            [
                wide(low + PK_Q, low + PK_K),
                wide(low + PK_K, low + PK_V),
                wide(low + PK_V, low + PK_GAIN),
            ]
            + gains
            + [jnp.zeros((72, 62), F32)],
            1,
        )
        for p in range(3):
            at = layer * A_WIDTH + p * A_STEP
            out[:, at : at + A_STEP] = a[24 * p : 24 * p + 24].astype(BF16)


def spread_b_kernel(first, index, r0, r1, r2, r3, pm, pf, b_out, blocks):
    for i, piece in enumerate((r0, r1, r2, r3)):
        blocks[4 * i : 4 * i + 4] = piece[:, :, first : first + PACK_B]
    part = functools.partial(part_of, index, blocks)
    wide = functools.partial(wide_of, index, blocks)
    out = dot(wide(0, PK_G - PK_O).astype(BF16), pm[...])
    for p in range(3):
        piece = out[24 * p : 24 * p + 24].astype(BF16)
        b_out[:, B_OUT + p * 512 : B_OUT + (p + 1) * 512] = piece[:, :512]
        b_out[:, B_OUT_TAIL + p * 64 : B_OUT_TAIL + (p + 1) * 64] = piece[:, 512:]
    b_out[:, B_OUT_TAIL + 192 :] = jnp.zeros((24, 64), BF16)
    for shift, low, high in ((0, PK_G - PK_O, PK_U - PK_O), (FF, PK_U - PK_O, PK_D - PK_O)):
        natural = wide(low, high).astype(BF16)
        for half in range(2):
            placed = dot(natural[:, half * HALF_FF : (half + 1) * HALF_FF], pf[...])
            for p in range(3):
                start = p * B_STEP + shift + half * HALF_FF
                b_out[:, start : start + HALF_FF] = placed[24 * p : 24 * p + 24].astype(BF16)
    down_at = PK_D - PK_O
    for xh in range(2):
        pieces = []
        for c in range(8):
            pieces.append(
                jnp.concatenate(
                    [
                        part(c, xh, down_at, down_at + 72),
                        part(c, xh, down_at + 72, down_at + 144),
                        part(c, xh, down_at + 144, down_at + 216)[:24],
                    ],
                    0,
                )
            )
        down = dot(jnp.concatenate(pieces, 1).astype(BF16), pm[...])
        for i in range(4):
            p = xh * 4 + i
            piece = down[24 * i : 24 * i + 24].astype(BF16)
            b_out[:, B_DOWN + p * 512 : B_DOWN + (p + 1) * 512] = piece[:, :512]
            b_out[:, B_DOWN_TAIL + p * 64 : B_DOWN_TAIL + (p + 1) * 64] = piece[:, 512:]


def gathered_a(a, out, lanes):
    a72 = jnp.concatenate([a[:, p * A_STEP : (p + 1) * A_STEP] for p in range(3)], 0)
    for xh in range(2):
        rows = slice(xh * 36, xh * 36 + 36)
        gain = a72[:, 960 + xh : 961 + xh]
        for c in range(8):
            out[c * 2 + xh, :, lanes] = jnp.concatenate(
                [
                    a72[rows, c * 72 : c * 72 + 72],
                    a72[rows, 576 + c * 24 : 600 + c * 24],
                    a72[rows, 768 + c * 24 : 792 + c * 24],
                    gain[:36],
                    gain[36:72],
                    jnp.zeros((36, 6), F32),
                ],
                1,
            ).astype(BF16)


def gathered_b(b, pm, pf, out, lanes):
    o72 = jnp.concatenate(
        [
            jnp.concatenate(
                [
                    b[:, B_OUT + p * 512 : B_OUT + (p + 1) * 512].astype(F32),
                    b[:, B_OUT_TAIL + p * 64 : B_OUT_TAIL + (p + 1) * 64].astype(F32),
                ],
                1,
            )
            for p in range(3)
        ],
        0,
    )
    o72 = dot_back(o72.astype(BF16), pm[...])
    sides = []
    for shift in (0, FF):
        halves = []
        for half in range(2):
            low = shift + half * HALF_FF
            stacked = jnp.concatenate(
                [
                    b[:, p * B_STEP + low : p * B_STEP + low + HALF_FF].astype(F32)
                    for p in range(3)
                ],
                0,
            )
            halves.append(dot_back(stacked.astype(BF16), pf[...]))
        sides.append(jnp.concatenate(halves, 1))
    for xh in range(2):
        down = jnp.concatenate(
            [
                jnp.concatenate(
                    [
                        b[:, B_DOWN + p * 512 : B_DOWN + (p + 1) * 512].astype(F32),
                        b[:, B_DOWN_TAIL + p * 64 : B_DOWN_TAIL + (p + 1) * 64].astype(F32),
                    ],
                    1,
                )
                for p in range(xh * 4, xh * 4 + 4)
            ],
            0,
        )
        down = dot_back(down.astype(BF16), pm[...])
        rows = slice(xh * 36, xh * 36 + 36)
        for c in range(8):
            cols = slice(c * 72, c * 72 + 72)
            piece = down[:, cols]
            out[c * 2 + xh, :, lanes] = jnp.concatenate(
                [
                    o72[rows, cols],
                    sides[0][rows, c * 192 : c * 192 + 192],
                    sides[1][rows, c * 192 : c * 192 + 192],
                    piece[:36],
                    piece[36:72],
                    jnp.concatenate([piece[72:96], jnp.zeros((12, 72), F32)], 0),
                    jnp.zeros((36, 96), F32),
                ],
                1,
            ).astype(BF16)


def gather_first_kernel(b, pm, pf, out):
    gathered_b(b, pm, pf, out, slice(0, PACK_B))


def gather_second_kernel(c, pm, pf, out):
    gathered_b(c, pm, pf, out, slice(0, PACK_B))
    gathered_a(c[:, B_WIDTH:].astype(F32), out, slice(PACK_B, PACK))


def gather_last_kernel(a0, a1, a2, a3, a4, blocks, out):
    a = a0[...].astype(F32)
    for ref in (a1, a2, a3, a4):
        a = a + ref[...].astype(F32)
    out[:, :, PACK_A:] = blocks[...]
    gathered_a(a, out, slice(0, PACK_A))


def finish_kernel(first_ref, last_ref, vec, wq, wk, wv, wo, wg, wu, wd):
    diagonal = eye(36)

    def added(ref, low, high):
        total = ref[0, :, low:high].astype(F32)
        for i in range(1, 16):
            total = total + ref[i, :, low:high].astype(F32)
        return total

    totals = (
        added(last_ref, 0, PACK),
        jnp.concatenate([added(last_ref, PACK, PACK + PACK_A), added(first_ref, 0, PACK_B)], 1),
    )
    for layer, total in enumerate(totals):
        wq[:, layer, :] = total[:, PK_Q:PK_K]
        wk[layer] = total[:, PK_K:PK_V].T
        wv[layer] = total[:, PK_V:PK_GAIN].T
        wo[:, layer, :] = total[:, PK_O:PK_G]
        first = jnp.sum(diagonal * total[:, PK_GAIN : PK_GAIN + 1], 0, keepdims=True)
        second = jnp.sum(diagonal * total[:, PK_GAIN + 1 : PK_GAIN + 2], 0, keepdims=True)
        vec[layer : layer + 1, :] = jnp.concatenate([first, second], 1)
        wg[:, layer, :] = total[:, PK_G:PK_U]
        wu[:, layer, :] = total[:, PK_U:PK_D]
        wd[layer] = jnp.concatenate(
            [
                total[:, PK_D : PK_D + 72],
                total[:, PK_D + 72 : PK_D + 144],
                total[:24, PK_D + 144 : PK_D + 216],
            ],
            0,
        ).T


def keep_kernel(value, out):
    out[...] = value[...]


def swap_halves(tile):
    lane = lax.broadcasted_iota(jnp.int32, tile.shape, 1) % HEAD_DIM
    return jnp.where(
        lane < HEAD_DIM // 2,
        pltpu.roll(tile, 128 - HEAD_DIM // 2, 1),
        pltpu.roll(tile, HEAD_DIM // 2, 1),
    )


def place_rows(source):
    lane = lax.broadcasted_iota(jnp.int32, (192, 192), 1)
    return jnp.where(lane == source[...], 1.0, 0.0).astype(BF16)


def pre_kernel(first, source, a_in, x_ref, pm, pq, cosine, sine, a, normed_out, q_out, kv_out, gains_out, *x_out):
    a[...] = dot(place_rows(source), a_in[...]).astype(BF16)
    gains = dot_rows(a[:, 896:1024], pq[0:192, :])
    for p in range(1, 3):
        gains = gains + dot_rows(
            a[:, p * A_STEP + 896 : (p + 1) * A_STEP], pq[p * 192 : (p + 1) * 192, :]
        )
    gains = gains[64:72]
    gains_out[...] = gains
    if first:
        x = dot_rows(x_ref[:D, :], pm[...])
        x_out[0][...] = x
    else:
        x = x_ref[...]
    inverse = lax.rsqrt(jnp.mean(x * x, -1, keepdims=True) + norm_eps)
    normed = (x * inverse * gains[0:1]).astype(BF16)
    normed_out[...] = normed
    lin = dot(normed[:, :192], a[:, :A_STEP])
    for p in range(1, 3):
        lin = lin + dot(
            normed[:, p * 192 : (p + 1) * 192], a[:, p * A_STEP : (p + 1) * A_STEP]
        )
    turned = []
    for t in range(6):
        tile = lin[:, t * 128 : (t + 1) * 128]
        turned.append(tile * cosine[...] + swap_halves(tile) * sine[...])
    turned = jnp.concatenate(turned, 1)
    q_out[...] = (turned[:, :D] * score_scale).astype(BF16)
    for g in range(KV_HEADS):
        part = slice(g * HEAD_DIM, (g + 1) * HEAD_DIM)
        kv_out[:, g * PAIR : (g + 1) * PAIR] = jnp.concatenate(
            [turned[:, D:768][:, part], lin[:, 768:960][:, part]], 1
        ).astype(BF16)


def weight_back(left, b, main, tail, p):
    return dot_back(left[:, :512], b[:, main + p * 512 : main + (p + 1) * 512]) + dot_back(
        left[:, 512:], b[:, tail + p * 64 : tail + (p + 1) * 64]
    )


def fetch_b(b, held, sems):
    copies = []
    for i, (low, high) in enumerate(((0, B_DOWN), (B_DOWN, B_OUT), (B_OUT, B_WIDTH))):
        copies.append(
            pltpu.make_async_copy(b.at[:, low:high], held.at[:, low:high], sems.at[i])
        )
    return copies


def ffn_forward(o_ref, x_ref, gains, pm, b, copies, mid_out, op_out, nm_out, gate_low, up_low, hid_low):
    ffn, down, rest = copies
    op = dot(o_ref[...], pm[...]).astype(BF16)
    op_out[...] = op

    def through(left, main, tail, count):
        wide = None
        narrow = None
        for p in range(count):
            piece = left[:, p * 192 : (p + 1) * 192]
            one = dot(piece, b[:, main + p * 512 : main + (p + 1) * 512])
            two = dot(piece, b[:, tail + p * 64 : tail + (p + 1) * 64])
            wide = one if wide is None else wide + one
            narrow = two if narrow is None else narrow + two
        return jnp.concatenate([wide, narrow], 1)

    rest.wait()
    mid = x_ref[...] + through(op, B_OUT, B_OUT_TAIL, 3)
    mid_out[...] = mid
    inverse = lax.rsqrt(jnp.mean(mid * mid, -1, keepdims=True) + norm_eps)
    nm = (mid * inverse * gains[1:2, :]).astype(BF16)
    nm_out[...] = nm
    ffn.wait()
    for part in range(2):
        cols = slice(part * HALF_FF, (part + 1) * HALF_FF)
        gate, up = None, None
        for p in range(3):
            piece = nm[:, p * 192 : (p + 1) * 192]
            low = p * B_STEP + part * HALF_FF
            one = dot(piece, b[:, low : low + HALF_FF])
            two = dot(piece, b[:, low + FF : low + FF + HALF_FF])
            gate = one if gate is None else gate + one
            up = two if up is None else up + two
        gate_low[:, cols] = gate.astype(BF16)
        up_low[:, cols] = up.astype(BF16)
        hid_low[:, cols] = (gate / (1.0 + jnp.exp(-gate)) * up).astype(BF16)
    down.wait()
    return mid + through(hid_low, B_DOWN, B_DOWN_TAIL, 8)


def middle_kernel(o_ref, x_ref, gains, pm, cosine, sine, source, b_ref, a_late, pq_late, *refs):
    kept, (x_out, a, normed, q, kv, gains_out, b, a_in, pq, sems) = refs[:6], refs[6:]
    copies = fetch_b(b_ref, b, sems)
    for copy in copies[::-1]:
        copy.start()
    late = held_copies((a_late, pq_late), (a_in, pq), sems, 3)
    x_out[...] = ffn_forward(o_ref, x_ref, gains, pm, b, copies, *kept)
    for copy in late:
        copy.wait()
    pre_kernel(False, source, a_in, x_out, pm, pq, cosine, sine, a, normed, q, kv, gains_out)


def norm_back(dy, v, gain):
    inverse = lax.rsqrt(jnp.mean(v * v, -1, keepdims=True) + norm_eps)
    scaled = dy * gain
    back = inverse * scaled - v * (
        inverse * inverse * inverse * jnp.mean(scaled * v, -1, keepdims=True)
    )
    return back, jnp.sum(dy * v * inverse, 0, keepdims=True)


class Sender:
    def __init__(self, db, db_out, sems):
        self.db, self.db_out, self.sems, self.sent = db, db_out, sems, []

    def send(self, low, high, source=None):
        source = self.db.at[:, low:high] if source is None else source
        self.sent.append(
            pltpu.make_async_copy(
                source, self.db_out.at[:, low:high], self.sems.at[3 + len(self.sent)]
            )
        )
        self.sent[-1].start()

    def wait(self):
        for copy in self.sent:
            copy.wait()


def ffn_backward(
    g,
    nm,
    gate_ref,
    up_ref,
    hid,
    mid,
    op,
    gains,
    pm,
    b,
    copies,
    sender,
    gm_out,
    do_out,
    dg_out,
    late=(),
):
    db = sender.db
    gb = g.astype(BF16)
    for p in range(8):
        piece = dot_rows(hid[:, p * 192 : (p + 1) * 192], gb)
        db[:, B_DOWN + p * 512 : B_DOWN + (p + 1) * 512] = piece[:, :512].astype(BF16)
        db[:, B_DOWN_TAIL + p * 64 : B_DOWN_TAIL + (p + 1) * 64] = piece[:, 512:].astype(BF16)
    sender.send(B_DOWN, B_OUT)
    for copy in copies[1:]:
        copy.wait()
    dh = jnp.concatenate([weight_back(gb, b, B_DOWN, B_DOWN_TAIL, p) for p in range(8)], 1)
    for copy in late[:3]:
        copy.wait()
    gate = gate_ref[...].astype(F32)
    up = up_ref[...].astype(F32)
    sig = 1.0 / (1.0 + jnp.exp(-gate))
    d_gate = (dh * up * sig * (1.0 + gate * (1.0 - sig))).astype(BF16)
    d_up = (dh * (gate * sig)).astype(BF16)
    for p in range(3):
        piece = nm[:, p * 192 : (p + 1) * 192]
        low = p * B_STEP
        db[:, low : low + FF] = dot_rows(piece, d_gate).astype(BF16)
        db[:, low + FF : low + B_STEP] = dot_rows(piece, d_up).astype(BF16)
        sender.send(low, low + B_STEP)
    for copy in copies[:1]:
        copy.wait()
    for copy in late[3:]:
        copy.wait()
    dnm = []
    for p in range(3):
        low = p * B_STEP
        dnm.append(
            dot_back(d_gate, b[:, low : low + FF])
            + dot_back(d_up, b[:, low + FF : low + B_STEP])
        )
    back, gain_grad = norm_back(jnp.concatenate(dnm, 1), mid[...], gains[1:2, :])
    dg_out[...] = gain_grad
    gm = g + back
    gm_out[...] = gm
    gmb = gm.astype(BF16)
    dop = []
    for p in range(3):
        piece = dot_rows(op[:, p * 192 : (p + 1) * 192], gmb)
        db[:, B_OUT + p * 512 : B_OUT + (p + 1) * 512] = piece[:, :512].astype(BF16)
        db[:, B_OUT_TAIL + p * 64 : B_OUT_TAIL + (p + 1) * 64] = piece[:, 512:].astype(BF16)
        dop.append(weight_back(gmb, b, B_OUT, B_OUT_TAIL, p))
    db[:, B_OUT_TAIL + 192 : B_WIDTH] = jnp.zeros((192, 64), BF16)
    sender.send(B_OUT, B_WIDTH)
    do_out[...] = dot_back(jnp.concatenate(dop, 1).astype(BF16), pm[...]).astype(BF16)
    sender.wait()


def held_copies(refs, held, sems, first):
    copies = [
        pltpu.make_async_copy(ref, target, sems.at[first + i])
        for i, (ref, target) in enumerate(zip(refs, held))
    ]
    for copy in copies:
        copy.start()
    return copies


def turn_kernel(o_ref, x_ref, gains, traded, pm, b_ref, *refs):
    x_out, db_out, gm_out, do_out, dg_out, b, db, mid, op, nm, gate, up, hid, sems = refs
    copies = fetch_b(b_ref, b, sems)
    for copy in copies[::-1]:
        copy.start()
    out = ffn_forward(o_ref, x_ref, gains, pm, b, copies, mid, op, nm, gate, up, hid)
    x_out[...] = dot_back(pm[...], out.astype(BF16)).astype(BF16)
    g = dot_rows(traded[D : 2 * D, :], pm[...])
    sender = Sender(db, db_out, sems)
    ffn_backward(
        g, nm, gate, up, hid, mid, op, gains, pm, b, (), sender, gm_out, do_out, dg_out
    )


def qkv_back_kernel(
    last, dq, kv0, kv1, kv2, kv3, kv4, cosine, sine, normed, gains, dg2, a_ref, x_late, gm_late, pq_late, *refs,
    started=None,
):
    if last:
        pm_ref, source, x_out, *da_refs, da, a, x_ref, gm, pq, pm, sems = refs
        late = held_copies((a_ref, x_late, gm_late, pq_late, pm_ref), (a, x_ref, gm, pq, pm), sems, 0)
    else:
        x_out, da, a, x_ref, gm, pq, sems = refs
        late = held_copies((a_ref, x_late, gm_late, pq_late), (a, x_ref, gm, pq), sems, 0)
        started()
    dkv = kv0[...].astype(F32)
    for ref in (kv1, kv2, kv3, kv4):
        dkv = dkv + ref[...].astype(F32)
    d_key = [dkv[:, g * PAIR : g * PAIR + HEAD_DIM] for g in range(KV_HEADS)]
    d_value = [dkv[:, g * PAIR + HEAD_DIM : (g + 1) * PAIR] for g in range(KV_HEADS)]
    rot = jnp.concatenate([dq[...]] + d_key, 1)
    turned = []
    for t in range(6):
        tile = rot[:, t * 128 : (t + 1) * 128]
        turned.append(tile * cosine[...] - swap_halves(tile) * sine[...])
    dqkv = jnp.concatenate(turned + d_value + [jnp.zeros((ROWS, 64), F32)], 1).astype(BF16)
    late[0].wait()
    dn = []
    for p in range(3):
        low = p * A_STEP
        da[:, low : low + A_STEP] = dot_rows(
            normed[:, p * 192 : (p + 1) * 192], dqkv
        ).astype(BF16)
        dn.append(dot_back(dqkv, a[:, low : low + A_STEP]))
    for copy in late[1:]:
        copy.wait()
    x = x_ref[...]
    back, dg1 = norm_back(jnp.concatenate(dn, 1), x, gains[0:1, :])
    rows = lax.broadcasted_iota(jnp.int32, (64, D), 0)
    stacked = jnp.where(rows == 0, dg1, jnp.where(rows == 1, dg2[...], 0.0)).astype(BF16)
    placed = dot_back(pq[...], stacked).astype(BF16)
    for p in range(3):
        da[:, p * A_STEP + 960 : (p + 1) * A_STEP] = placed[p * 192 : (p + 1) * 192]
    out = gm[...] + back
    if last:
        x_out[...] = dot_back(pm[...], out.astype(BF16)).astype(BF16)
        placed = dot_rows(place_rows(source), da[...])
        for i, ref in enumerate(da_refs):
            ref[...] = placed[i * 24 : (i + 1) * 24].astype(BF16)
    else:
        x_out[...] = out


def back_kernel(*args):
    qkv_args, (gains, hid, gate, up, nm, mid, op, pm, b_ref), refs = args[:15], args[15:24], args[24:]
    db_out, gm_out, do_out, dg_out, grad, da, a, x, gm, pq, *held, b, db, qkv_sems, sems = refs
    copies = fetch_b(b_ref, b, sems)
    late = []

    def started():
        late.extend(held_copies((hid,), held[:1], sems, 9))
        copies[2].start()
        copies[1].start()
        late.extend(held_copies((gate, up, nm), held[1:4], sems, 10))
        copies[0].start()
        late.extend(held_copies((mid, op, pm), held[4:], sems, 13))

    qkv_back_kernel(False, *qkv_args, grad, da, a, x, gm, pq, qkv_sems, started=started)
    sender = Sender(db, db_out, sems)
    sender.send(B_WIDTH, C_WIDTH, da)
    late[0].wait()
    hid, gate, up, nm, mid, op, pm = held
    ffn_backward(
        grad[...], nm, gate, up, hid, mid, op, gains, pm, b,
        copies, sender, gm_out, do_out, dg_out, late[1:],
    )


PAIR = 2 * HEAD_DIM
WIDE = GROUP * BLOCK
CHUNK = 256
STEPS = KEYS // CHUNK + 1
SLOTS = 2 * KV_HEADS


def load_heads(ref, scratch, run, upper):
    zero = jnp.zeros((WIDE, HEAD_DIM), BF16)
    for g in range(KV_HEADS):
        heads = jnp.concatenate(
            [
                ref[
                    run * BLOCK : (run + 1) * BLOCK,
                    (g * GROUP + h) * HEAD_DIM : (g * GROUP + h + 1) * HEAD_DIM,
                ]
                for h in range(GROUP)
            ],
            0,
        )
        both = [zero, heads] if upper else [heads, zero]
        scratch[run * KV_HEADS + g] = jnp.concatenate(both, 1)


def sort_keys(table, pieces, kvs):
    for j in range(KEYS // BLOCK):
        start = pl.multiple_of(table[2 + j] * BLOCK, BLOCK)
        kvs[pl.ds(start, BLOCK), :] = pieces[j // 2][(j % 2) * BLOCK : (j % 2 + 1) * BLOCK, :]


def set_lead(lead):
    key = lax.broadcasted_iota(jnp.int32, (CHUNK, BLOCK), 0)
    row = lax.broadcasted_iota(jnp.int32, (CHUNK, BLOCK), 1)
    lead[...] = row - key


def head_columns(h):
    return slice(h * BLOCK, (h + 1) * BLOCK)


def step_of(table, it):
    first = (table[0] + 2) // 2
    second = it >= first
    run = jnp.where(second, 1, 0)
    chunk = jnp.where(second, it - first, it)
    block = jnp.where(second, table[1], table[0])
    return run, pl.multiple_of(chunk * CHUNK, CHUNK), chunk * CHUNK - block * BLOCK


def attend_kernel(table, q_ref, *refs):
    pieces, (o_out, lse_out, kvs, qs, lead, ms, ls, acc) = refs[:8], refs[8:]
    sort_keys(table, pieces, kvs)
    load_heads(q_ref, qs, 0, False)
    load_heads(q_ref, qs, 1, False)
    set_lead(lead)
    ms[...] = jnp.full(ms.shape, masked_score, F32)
    ls[...] = jnp.zeros(ls.shape, F32)
    acc[...] = jnp.zeros(acc.shape, F32)

    def step(it, carry):
        run, start, least = step_of(table, it)
        results = []
        for g in range(KV_HEADS):
            at = run * KV_HEADS + g
            kv = kvs[pl.ds(start, CHUNK), g * PAIR : (g + 1) * PAIR]
            turned = kv.T
            for h in range(GROUP):
                part = head_columns(h)
                scores = dot_back(kv, qs[at, part, :])
                scores = jnp.where(lead[...] >= least, scores, masked_score)
                before = ms[at, :, part]
                now = jnp.maximum(before, jnp.max(scores, 0, keepdims=True))
                raised = jnp.exp(scores - now)
                shrink = jnp.exp(before - now)
                total = ls[at, :, part] * shrink + jnp.sum(raised, 0, keepdims=True)
                out = dot(turned, raised.astype(BF16))[HEAD_DIM:]
                results.append((at, part, now, total, acc[at, :, part] * shrink + out))
        for at, part, now, total, out in results:
            ms[at, :, part] = now
            ls[at, :, part] = total
            acc[at, :, part] = out
        return carry

    lax.fori_loop(0, STEPS, step, 0, unroll=STEPS)
    for run in range(2):
        for g in range(KV_HEADS):
            at = run * KV_HEADS + g
            total = ls[at]
            lse_out[at] = ms[at] + jnp.log(total)
            heads = (acc[at] / total).T
            for h in range(GROUP):
                o_out[
                    run * BLOCK : (run + 1) * BLOCK,
                    (g * GROUP + h) * HEAD_DIM : (g * GROUP + h + 1) * HEAD_DIM,
                ] = heads[h * BLOCK : (h + 1) * BLOCK].astype(BF16)


def attend_back_kernel(table, q_ref, o_ref, do_ref, lse, *refs):
    pieces = refs[:8]
    dq_out, outs, (kvs, qs, dos, lead, deltas, dkvs, dqs) = refs[8], refs[9:17], refs[17:]
    sort_keys(table, pieces, kvs)
    set_lead(lead)
    for run in range(2):
        load_heads(q_ref, qs, run, False)
        load_heads(do_ref, dos, run, True)
        rows = slice(run * BLOCK, (run + 1) * BLOCK)
        product = o_ref[rows, :].astype(F32) * do_ref[rows, :].astype(F32)
        turned = jnp.concatenate([product, jnp.zeros((BLOCK, HEAD_DIM), F32)], 1).T
        for g in range(KV_HEADS):
            deltas[run * KV_HEADS + g] = jnp.concatenate(
                [
                    jnp.sum(turned[h * HEAD_DIM : (h + 1) * HEAD_DIM], 0, keepdims=True)
                    for h in range(g * GROUP, (g + 1) * GROUP)
                ],
                1,
            )
    dkvs[...] = jnp.zeros(dkvs.shape, F32)
    dqs[...] = jnp.zeros(dqs.shape, F32)

    def step(it, carry):
        run, start, least = step_of(table, it)
        scores, d_probs, low_probs, d_scores, results = [], [], [], [], []
        for g in range(KV_HEADS):
            at = run * KV_HEADS + g
            kv = kvs[pl.ds(start, CHUNK), g * PAIR : (g + 1) * PAIR]
            scores.append(dot_back(kv, qs[at]))
            d_probs.append(dot_back(kv, dos[at]))
        ahead = jnp.concatenate([lead[...]] * GROUP, 1) >= least
        for g in range(KV_HEADS):
            at = run * KV_HEADS + g
            probs = jnp.exp(jnp.where(ahead, scores[g], masked_score) - lse[at])
            low_probs.append(probs.astype(BF16))
            d_scores.append((probs * (d_probs[g] - deltas[at])).astype(BF16))
        for g in range(KV_HEADS):
            at = run * KV_HEADS + g
            kv = kvs[pl.ds(start, CHUNK), g * PAIR : (g + 1) * PAIR]
            d_kv = dot(d_scores[g], qs[at]) + dot(low_probs[g], dos[at])
            results.append((at, d_kv, dot_rows(kv, d_scores[g])[:HEAD_DIM]))
        for g, (at, d_kv, d_q) in enumerate(results):
            dkvs[g, pl.ds(start, CHUNK), :] += d_kv
            dqs[at] += d_q
        return carry

    lax.fori_loop(0, STEPS, step, 0, unroll=STEPS)
    for run in range(2):
        for g in range(KV_HEADS):
            heads = (dqs[run * KV_HEADS + g] * score_scale).T
            for h in range(GROUP):
                dq_out[
                    run * BLOCK : (run + 1) * BLOCK,
                    (g * GROUP + h) * HEAD_DIM : (g * GROUP + h + 1) * HEAD_DIM,
                ] = heads[h * BLOCK : (h + 1) * BLOCK]
    for j in range(KEYS // BLOCK):
        start = pl.multiple_of(table[2 + j] * BLOCK, BLOCK)
        rows = slice((j % 2) * BLOCK, (j % 2 + 1) * BLOCK)
        for g in range(KV_HEADS):
            outs[j // 2][rows, g * PAIR : (g + 1) * PAIR] = dkvs[
                g, pl.ds(start, BLOCK), :
            ].astype(BF16)


def attend(table, q, kv_all):
    return call(
        attend_kernel,
        [sds((ROWS, D), BF16), sds((SLOTS, 1, WIDE), F32)],
        10,
        6.9,
        grant=16,
        smem=(0,),
        scratch=[
            pltpu.VMEM((KEYS, KV_HEADS * PAIR), BF16),
            pltpu.VMEM((SLOTS, WIDE, PAIR), BF16),
            pltpu.VMEM((CHUNK, BLOCK), jnp.int32),
            pltpu.VMEM((SLOTS, 1, WIDE), F32),
            pltpu.VMEM((SLOTS, 1, WIDE), F32),
            pltpu.VMEM((SLOTS, HEAD_DIM, WIDE), F32),
        ],
    )(table, q, *kv_all)


def attend_back(table, q, kv_all, o, do, lse):
    return call(
        attend_back_kernel,
        [sds((ROWS, D), F32)] + [sds((ROWS, 2 * KVD), BF16)] * 8,
        13,
        11.3,
        smem=(0,),
        scratch=[
            pltpu.VMEM((KEYS, KV_HEADS * PAIR), BF16),
            pltpu.VMEM((SLOTS, WIDE, PAIR), BF16),
            pltpu.VMEM((SLOTS, WIDE, PAIR), BF16),
            pltpu.VMEM((CHUNK, BLOCK), jnp.int32),
            pltpu.VMEM((SLOTS, 1, WIDE), F32),
            pltpu.VMEM((KV_HEADS, KEYS, PAIR), F32),
            pltpu.VMEM((SLOTS, HEAD_DIM, WIDE), F32),
        ],
    )(table, q, o, do, lse, *kv_all)


def ring(shift):
    return [(i, (i + shift) % 4) for i in range(4)]


def ring_x(shift):
    pairs = []
    for x in range(4):
        to = (x + shift) % 4
        pairs.append(((x % 2) * 2 + x // 2, (to % 2) * 2 + to // 2))
    return pairs


SHIFTS = (1, -1, 2)


def from_x(value):
    return [value] + [lax.ppermute(value, ("xl", "xh"), ring_x(s)) for s in SHIFTS]


def from_ring(value, axis):
    return [value] + [lax.ppermute(value, axis, ring(s)) for s in SHIFTS]


def other_core(value):
    return lax.ppermute(value, "core", [(0, 1), (1, 0)])


def trade(value):
    return lax.ppermute(value, ("xl", "core"), [(0, 0), (1, 2), (2, 1), (3, 3)])


def place_of(distance):
    distance = distance % 4
    return distance ^ (distance >> 1)


def block_index():
    z, xl, xh = (lax.axis_index(name) for name in OUTER)
    block = jnp.arange(16, dtype=jnp.int32)
    along_x = place_of(xh * 2 + xl - (block % 2) * 2 - (block // 2) % 2)
    along_z = place_of(z - block // 4)
    return along_z * 4 + along_x, along_x * 4 + along_z


def row_source():
    y, core = lax.axis_index("y"), lax.axis_index("core")
    rows = jnp.arange(192, dtype=jnp.int32)
    owner, j = rows // 24, rows % 24
    piece = ((owner + core) % 2) * 4 + place_of(y - owner // 2)
    return (piece * 24 + j)[:, None]


def spread_a(index, blocks):
    return call(
        spread_a_kernel,
        sds((24, 2 * A_WIDTH), BF16),
        5,
        3.0,
        smem=(0,),
        scratch=[pltpu.VMEM((16, 36, 2 * PACK_A), BF16)],
        grant=16,
    )(index, *blocks)


def spread_b(first, index, blocks, pm, pf):
    return call(
        functools.partial(spread_b_kernel, first),
        sds((24, B_WIDTH), BF16),
        7,
        4.3,
        smem=(0,),
        scratch=[pltpu.VMEM((16, 36, PACK_B), BF16)],
        grant=16,
    )(index, *blocks, pm, pf)


def share(near):
    return near + [other_core(piece) for piece in near]


def return_pieces(near, far, axis):
    far = [other_core(piece) for piece in far]
    both = [(n.astype(F32) + f.astype(F32)).astype(BF16) for n, f in zip(near[1:], far[1:])]
    back = [lax.ppermute(piece, axis, ring(-s)) for piece, s in zip(both, SHIFTS)]
    return [near[0], far[0]] + back


def key_table(starts):
    z, core = lax.axis_index("z"), lax.axis_index("core")
    j = np.arange(18) - 2
    shift = np.where(j < 0, 0, np.array((0,) + SHIFTS)[(j // 2) % 4]).astype(np.int32)
    far = np.where(j < 0, 0, j // 8).astype(np.int32)
    wanted = (((z - shift) % 4) * 2 + (core + far) % 2) * 2 + (j % 2).astype(np.int32)
    match = wanted[:, None] == jnp.arange(16, dtype=jnp.int32)[None, :]
    return jnp.sum(jnp.where(match, starts[None, :], 0), 1)


def angles(places):
    half_dim = HEAD_DIM // 2
    inverse = rope_base ** (-2.0 * jnp.arange(half_dim).astype(F32) / HEAD_DIM)
    turned = places.astype(F32)[:, None] * inverse[None, :]
    cosine, sine = jnp.cos(turned), jnp.sin(turned)
    return jnp.concatenate([cosine] * 4, 1), jnp.concatenate([-sine, sine] * 2, 1)


def after(value, *others):
    return lax.optimization_barrier((value, *others))[0]


def on_device(
    tokens, positions, vectors, w_query, w_key, w_value, w_out, w_gate, w_up, w_down, cotangent
):
    pm = jnp.asarray(one_hot(feature_order()), BF16)
    pf = jnp.asarray(one_hot(hidden_order()), BF16)
    pq = jnp.asarray(gain_matrix(), BF16)
    index, z_index = block_index()
    source = row_source()
    layer_second = (1, 0, 2)
    turned = (0, 2, 1)
    pack, later = call(
        pack_kernel, [sds((36, PACK_FIRST), BF16), sds((36, PACK_B), BF16)], 8, 1.9
    )(
        vectors,
        w_query.transpose(layer_second),
        w_key.transpose(turned),
        w_value.transpose(turned),
        w_out.transpose(layer_second),
        w_gate.transpose(layer_second),
        w_up.transpose(layer_second),
        w_down.transpose(turned),
    )
    later = jnp.stack(from_ring(later, "z"))
    blocks = from_ring(after(jnp.stack(from_x(pack)), later), "z")
    a_near = spread_a(index, blocks)
    near = from_ring(a_near, "y")
    later = from_x(after(later, a_near))
    both = share(near)
    a_near, a1_near = (
        jnp.concatenate([piece[:, low : low + A_WIDTH] for piece in both], 0)
        for low in (0, A_WIDTH)
    )
    blocks = [after(blocks[0], *near[1:])] + blocks[1:]
    b0 = lax.all_gather(
        spread_b(2 * PACK_A, index, blocks, pm, pf), INNER, axis=0, tiled=True
    )

    starts = jnp.broadcast_to((positions[0, ::BLOCK] // BLOCK).astype(BF16)[:, None], (16, ROWS))
    traded = jnp.concatenate([tokens[0].T, cotangent[0].T, starts], 0)
    traded = trade(after(traded, blocks[3]))
    table = key_table(traded[2 * D :, 0].astype(jnp.int32))
    places = (table[:2, None] * BLOCK + jnp.arange(BLOCK)[None, :]).reshape(ROWS)
    cosine, sine = angles(places)
    x = traded

    pre_shapes = [
        sds((192, A_WIDTH), BF16),
        sds((ROWS, D), BF16),
        sds((ROWS, D), BF16),
        sds((ROWS, 2 * KVD), BF16),
        sds((8, D), F32),
    ]
    a, normed, q, kv, gains, x = call(
        functools.partial(pre_kernel, True), pre_shapes + [sds((ROWS, D), F32)], 7, 5.0, grant=16
    )(source, a_near, traded, pm, pq, cosine, sine)
    near = from_ring(kv, "z")
    later = [after(later[0], *near[1:])] + later[1:]
    b1 = lax.all_gather(spread_b(0, z_index, later, pm, pf), INNER, axis=0, tiled=True)
    kv_all = share(near)
    o, lse = attend(table, q, kv_all)
    first_layer = (x, a, normed, q, kv_all, gains, o, lse)

    *kept, x, a, normed, q, kv, gains = call(
        middle_kernel,
        [
            sds((ROWS, D), F32),
            sds((ROWS, D), BF16),
            sds((ROWS, D), BF16),
            sds((ROWS, FF), BF16),
            sds((ROWS, FF), BF16),
            sds((ROWS, FF), BF16),
            sds((ROWS, D), F32),
        ]
        + pre_shapes,
        10,
        10.0,
        left=(7, 8, 9),
        scratch=[
            pltpu.VMEM((192, B_WIDTH), BF16),
            pltpu.VMEM((192, A_WIDTH), BF16),
            pltpu.VMEM((D, D), BF16),
            pltpu.SemaphoreType.DMA((5,)),
        ],
    )(o, x, gains, pm, cosine, sine, source, b0, a1_near, pq)
    kv_all = share(from_ring(kv, "z"))
    o, lse = attend(table, q, kv_all)

    back_shapes = [sds((ROWS, D), F32), sds((ROWS, D), BF16), sds((1, D), F32)]
    back_scratch = [pltpu.VMEM((192, B_WIDTH), BF16)] * 2
    ffn_scratch = [
        pltpu.VMEM((ROWS, FF), BF16),
        pltpu.VMEM((ROWS, FF), BF16),
        pltpu.VMEM((ROWS, FF), BF16),
        pltpu.VMEM((ROWS, D), BF16),
        pltpu.VMEM((ROWS, D), F32),
        pltpu.VMEM((ROWS, D), BF16),
    ]
    output, db, gm, do, dg2 = call(
        turn_kernel,
        [sds((D, ROWS), BF16), sds((192, B_WIDTH), BF16)] + back_shapes,
        6,
        17.0,
        left=(5,),
        left_out=(1,),
        scratch=back_scratch
        + [
            pltpu.VMEM((ROWS, D), F32),
            pltpu.VMEM((ROWS, D), BF16),
            pltpu.VMEM((ROWS, D), BF16),
            pltpu.VMEM((ROWS, FF), BF16),
            pltpu.VMEM((ROWS, FF), BF16),
            pltpu.VMEM((ROWS, FF), BF16),
            pltpu.SemaphoreType.DMA((8,)),
        ],
    )(o, x, gains, traded, pm, b1)
    output = trade(output)
    first = lax.psum_scatter(db, INNER, scatter_dimension=0, tiled=True)
    dq, *pieces = attend_back(table, q, kv_all, o, do, lse)
    parts = return_pieces(pieces[:4], pieces[4:], "z")
    parts[0] = after(parts[0], output)
    held = [
        pltpu.VMEM((192, A_WIDTH), BF16),
        pltpu.VMEM((ROWS, D), F32),
        pltpu.VMEM((ROWS, D), F32),
        pltpu.VMEM((D, D), BF16),
    ]
    second_layer = (dq, *parts, cosine, sine, normed, gains, dg2, a, x, gm, pq)

    x, a, normed, q, kv_all, gains, o, lse = first_layer
    mid, op, nm, gate, up, hid = kept
    db, gm, do, dg2 = call(
        back_kernel,
        [sds((192, C_WIDTH), BF16)] + back_shapes,
        24,
        16.0,
        left=(*range(11, 15), *range(16, 24)),
        left_out=(0,),
        scratch=[pltpu.VMEM((ROWS, D), F32), pltpu.VMEM((192, A_WIDTH), BF16)]
        + held
        + ffn_scratch
        + [pltpu.VMEM((D, D), BF16)]
        + back_scratch
        + [pltpu.SemaphoreType.DMA((4,)), pltpu.SemaphoreType.DMA((16,))],
    )(*second_layer, gains, hid, gate, up, nm, mid, op, pm, b0)
    summed = lax.psum_scatter(db, INNER, scatter_dimension=0, tiled=True)
    dq, *pieces = attend_back(table, q, kv_all, o, do, lse)
    parts = return_pieces(pieces[:4], pieces[4:], "z")
    first = call(gather_first_kernel, sds((16, 36, PACK_B), BF16), 3, 5.0, grant=16)(
        after(first, parts[1]), pm, pf
    )
    parts[0] = after(parts[0], first)
    grad, *pieces = call(
        functools.partial(qkv_back_kernel, True),
        [sds((D, ROWS), BF16)] + [sds((24, A_WIDTH), BF16)] * 8,
        17,
        6.4,
        grant=20,
        left=range(11, 16),
        scratch=[pltpu.VMEM((192, A_WIDTH), BF16)]
        + held
        + [pltpu.VMEM((D, D), BF16), pltpu.SemaphoreType.DMA((5,))],
    )(dq, *parts, cosine, sine, normed, gains, dg2, a, x, gm, pq, pm, source)
    parts = return_pieces(pieces[:4], pieces[4:], "y")
    first = lax.all_to_all(first, OUTER, 0, 0, tiled=True)
    grad = trade(grad)
    blocks = call(gather_second_kernel, sds((16, 36, PACK), BF16), 3, 5.0, grant=16)(summed, pm, pf)
    blocks = call(gather_last_kernel, sds((16, 36, PACK + PACK_A), BF16), 6, 2.5, grant=16)(
        *parts, blocks
    )
    rest = lax.all_to_all(after(blocks, grad), OUTER, 0, 0, tiled=True)
    outs = call(
        finish_kernel,
        [
            sds((2, 72), F32),
            sds((36, 2, 72), F32),
            sds((2, 24, 36), F32),
            sds((2, 24, 36), F32),
            sds((36, 2, 72), F32),
            sds((36, 2, 192), F32),
            sds((36, 2, 192), F32),
            sds((2, 72, 96), F32),
        ],
        2,
        2.9,
        grant=16,
    )(first, rest)
    order = (None, layer_second, turned, turned, layer_second, layer_second, layer_second, turned)
    outs = [out if axes is None else out.transpose(axes) for out, axes in zip(outs, order)]
    output = call(keep_kernel, sds((D, ROWS), BF16), 1, 1.0)(output)
    return (output.T[None], grad.astype(F32).T[None], *outs)


def solution(mesh):
    fine = Mesh(np.asarray(mesh.devices).reshape(SIZES), AXES)
    split = P(None, FSDP, CTX)
    rows = P(FSDP, CTX, None)
    return jax.shard_map(
        on_device,
        mesh=fine,
        in_specs=(rows, P(FSDP, None), P(None, FSDP)) + (split,) * 7 + (rows,),
        out_specs=(rows, rows, P(None, FSDP)) + (split,) * 7,
        check_vma=False,
    )
```

```python
import functools

import jax
import jax.numpy as jnp
import numpy as np
from jax import lax
from jax.experimental import pallas as pl
from jax.experimental.pallas import tpu as pltpu
from jax.sharding import Mesh
from jax.sharding import PartitionSpec as P

D = 576
HEADS = 9
KV_HEADS = 3
HEAD_DIM = 64
GROUP = HEADS // KV_HEADS
FF = 1536
ROWS = 256
BLOCK = 128
KEYS = 2048
KVD = KV_HEADS * HEAD_DIM
HALF_FF = FF // 2

rope_base = 10000.0
norm_eps = 1e-05
masked_score = -1e30
score_scale = HEAD_DIM ** (-0.5)

F32 = jnp.float32
BF16 = jnp.bfloat16

AXES = ("z", "xl", "xh", "y", "core")
SIZES = (4, 2, 2, 4, 2)
CTX = ("z", "xl")
FSDP = ("xh", "y", "core")
INNER = ("y", "core")
OUTER = ("z", "xl", "xh")

PACK = 896
PACK_A = 128
PACK_B = PACK - PACK_A
PACK_FIRST = PACK + PACK_A
PK_Q, PK_K, PK_V, PK_GAIN = 0, 72, 96, 120
PK_O, PK_G, PK_U, PK_D = 128, 200, 392, 584

A_STEP = 1024
A_WIDTH = 3 * A_STEP
B_STEP = 2 * FF
B_DOWN = 3 * B_STEP
B_OUT = B_DOWN + 8 * 512
B_DOWN_TAIL = B_OUT + 3 * 512
B_OUT_TAIL = B_DOWN_TAIL + 8 * 64
B_WIDTH = B_OUT_TAIL + 256

C_WIDTH = B_WIDTH + A_WIDTH

BYTES_PER_MICRO = 3.4e6
FLOPS_PER_MICRO = 1e9


def feature_order():
    n = np.arange(D)
    owner, i = n // 36, n % 36
    xh, yc = owner // 8, owner % 8
    local = xh * 36 + i
    return (local // 24) * 192 + yc * 24 + local % 24


def hidden_order():
    n = np.arange(HALF_FF)
    yc, i = n // 96, n % 96
    return (i // 24) * 192 + yc * 24 + i % 24


def one_hot(places):
    size = len(places)
    out = np.zeros((size, size), np.float32)
    out[np.arange(size), places] = 1.0
    return out


def gain_matrix():
    n = np.arange(D)
    yc, local = n // 72, n % 72
    gathered = (local // 24) * 192 + yc * 24 + local % 24
    out = np.zeros((D, D), np.float32)
    out[gathered, feature_order()] = 1.0
    return out


def dot(left, right):
    return lax.dot_general(left, right, (((1,), (0,)), ((), ())), preferred_element_type=F32)


def dot_rows(left, right):
    return lax.dot_general(left, right, (((0,), (0,)), ((), ())), preferred_element_type=F32)


def dot_back(left, right):
    return lax.dot_general(left, right, (((1,), (1,)), ((), ())), preferred_element_type=F32)


def call(kernel, out_shape, n_in, micros, smem=(), left=(), left_out=(), scratch=(), grant=56):
    def spec(i, left):
        return pl.BlockSpec(
            memory_space=pltpu.SMEM if i in smem else pl.ANY if i in left else pltpu.VMEM
        )

    in_specs = [spec(i, left) for i in range(n_in)]
    many = isinstance(out_shape, (list, tuple))
    return pl.pallas_call(
        kernel,
        out_shape=out_shape,
        in_specs=in_specs,
        out_specs=[
            pl.BlockSpec(memory_space=pl.ANY if i in left_out else pltpu.VMEM)
            for i in range(len(out_shape))
        ]
        if many
        else pl.BlockSpec(memory_space=pltpu.VMEM),
        scratch_shapes=list(scratch),
        compiler_params=pltpu.CompilerParams(vmem_limit_bytes=grant << 20),
        cost_estimate=pl.CostEstimate(
            flops=int(micros * FLOPS_PER_MICRO),
            bytes_accessed=int(micros * BYTES_PER_MICRO),
            transcendentals=0,
        ),
    )


def sds(shape, dtype):
    return jax.ShapeDtypeStruct(shape, dtype)


def eye(size):
    rows = lax.broadcasted_iota(jnp.int32, (size, size), 0)
    cols = lax.broadcasted_iota(jnp.int32, (size, size), 1)
    return jnp.where(rows == cols, 1.0, 0.0).astype(F32)


def pack_kernel(vec, wq, wk, wv, wo, wg, wu, wd, out, later):
    diagonal = eye(36)
    for layer in range(2):
        gains = vec[layer : layer + 1, :].astype(F32)
        first = jnp.sum(diagonal * gains[:, :36], 1, keepdims=True)
        second = jnp.sum(diagonal * gains[:, 36:72], 1, keepdims=True)
        down = wd[layer].astype(F32).T
        block = jnp.concatenate(
            [
                wq[...].astype(F32)[:, layer],
                wk[layer].astype(F32).T,
                wv[layer].astype(F32).T,
                first,
                second,
                jnp.zeros((36, 6), F32),
                wo[...].astype(F32)[:, layer],
                wg[...].astype(F32)[:, layer],
                wu[...].astype(F32)[:, layer],
                down[:36],
                down[36:72],
                jnp.concatenate([down[72:96], jnp.zeros((12, 72), F32)], 0),
                jnp.zeros((36, 96), F32),
            ],
            1,
        ).astype(BF16)
        out[:, layer * PACK_A : (layer + 1) * PACK_A] = block[:, :PACK_A]
        if layer == 0:
            out[:, 2 * PACK_A :] = block[:, PACK_A:]
        else:
            later[...] = block[:, PACK_A:]


def part_of(index, blocks, c, xh, low, high):
    return blocks[index[c * 2 + xh], :, low:high].astype(F32)


def wide_of(index, blocks, low, high):
    halves = [
        jnp.concatenate([part_of(index, blocks, c, xh, low, high) for c in range(8)], 1)
        for xh in range(2)
    ]
    return jnp.concatenate(halves, 0)


def spread_a_kernel(index, r0, r1, r2, r3, out, blocks):
    for i, piece in enumerate((r0, r1, r2, r3)):
        blocks[4 * i : 4 * i + 4] = piece[:, :, : 2 * PACK_A]
    part = functools.partial(part_of, index, blocks)
    wide = functools.partial(wide_of, index, blocks)
    for layer in range(2):
        low = layer * PACK_A
        gains = []
        for xh in range(2):
            both = part(0, xh, low + PK_GAIN, low + PK_GAIN + 2)
            gains.append(jnp.concatenate([both[:, :1], both[:, 1:]], 0))
        a = jnp.concatenate(
            [
                wide(low + PK_Q, low + PK_K),
                wide(low + PK_K, low + PK_V),
                wide(low + PK_V, low + PK_GAIN),
            ]
            + gains
            + [jnp.zeros((72, 62), F32)],
            1,
        )
        for p in range(3):
            at = layer * A_WIDTH + p * A_STEP
            out[:, at : at + A_STEP] = a[24 * p : 24 * p + 24].astype(BF16)


def spread_b_kernel(first, index, r0, r1, r2, r3, pm, pf, b_out, blocks):
    for i, piece in enumerate((r0, r1, r2, r3)):
        blocks[4 * i : 4 * i + 4] = piece[:, :, first : first + PACK_B]
    part = functools.partial(part_of, index, blocks)
    wide = functools.partial(wide_of, index, blocks)
    out = dot(wide(0, PK_G - PK_O).astype(BF16), pm[...])
    for p in range(3):
        piece = out[24 * p : 24 * p + 24].astype(BF16)
        b_out[:, B_OUT + p * 512 : B_OUT + (p + 1) * 512] = piece[:, :512]
        b_out[:, B_OUT_TAIL + p * 64 : B_OUT_TAIL + (p + 1) * 64] = piece[:, 512:]
    b_out[:, B_OUT_TAIL + 192 :] = jnp.zeros((24, 64), BF16)
    for shift, low, high in ((0, PK_G - PK_O, PK_U - PK_O), (FF, PK_U - PK_O, PK_D - PK_O)):
        natural = wide(low, high).astype(BF16)
        for half in range(2):
            placed = dot(natural[:, half * HALF_FF : (half + 1) * HALF_FF], pf[...])
            for p in range(3):
                start = p * B_STEP + shift + half * HALF_FF
                b_out[:, start : start + HALF_FF] = placed[24 * p : 24 * p + 24].astype(BF16)
    down_at = PK_D - PK_O
    for xh in range(2):
        pieces = []
        for c in range(8):
            pieces.append(
                jnp.concatenate(
                    [
                        part(c, xh, down_at, down_at + 72),
                        part(c, xh, down_at + 72, down_at + 144),
                        part(c, xh, down_at + 144, down_at + 216)[:24],
                    ],
                    0,
                )
            )
        down = dot(jnp.concatenate(pieces, 1).astype(BF16), pm[...])
        for i in range(4):
            p = xh * 4 + i
            piece = down[24 * i : 24 * i + 24].astype(BF16)
            b_out[:, B_DOWN + p * 512 : B_DOWN + (p + 1) * 512] = piece[:, :512]
            b_out[:, B_DOWN_TAIL + p * 64 : B_DOWN_TAIL + (p + 1) * 64] = piece[:, 512:]


def gathered_a(a, out, lanes):
    a72 = jnp.concatenate([a[:, p * A_STEP : (p + 1) * A_STEP] for p in range(3)], 0)
    for xh in range(2):
        rows = slice(xh * 36, xh * 36 + 36)
        gain = a72[:, 960 + xh : 961 + xh]
        for c in range(8):
            out[c * 2 + xh, :, lanes] = jnp.concatenate(
                [
                    a72[rows, c * 72 : c * 72 + 72],
                    a72[rows, 576 + c * 24 : 600 + c * 24],
                    a72[rows, 768 + c * 24 : 792 + c * 24],
                    gain[:36],
                    gain[36:72],
                    jnp.zeros((36, 6), F32),
                ],
                1,
            ).astype(BF16)


def gathered_b(b, pm, pf, out, lanes):
    o72 = jnp.concatenate(
        [
            jnp.concatenate(
                [
                    b[:, B_OUT + p * 512 : B_OUT + (p + 1) * 512].astype(F32),
                    b[:, B_OUT_TAIL + p * 64 : B_OUT_TAIL + (p + 1) * 64].astype(F32),
                ],
                1,
            )
            for p in range(3)
        ],
        0,
    )
    o72 = dot_back(o72.astype(BF16), pm[...])
    sides = []
    for shift in (0, FF):
        halves = []
        for half in range(2):
            low = shift + half * HALF_FF
            stacked = jnp.concatenate(
                [
                    b[:, p * B_STEP + low : p * B_STEP + low + HALF_FF].astype(F32)
                    for p in range(3)
                ],
                0,
            )
            halves.append(dot_back(stacked.astype(BF16), pf[...]))
        sides.append(jnp.concatenate(halves, 1))
    for xh in range(2):
        down = jnp.concatenate(
            [
                jnp.concatenate(
                    [
                        b[:, B_DOWN + p * 512 : B_DOWN + (p + 1) * 512].astype(F32),
                        b[:, B_DOWN_TAIL + p * 64 : B_DOWN_TAIL + (p + 1) * 64].astype(F32),
                    ],
                    1,
                )
                for p in range(xh * 4, xh * 4 + 4)
            ],
            0,
        )
        down = dot_back(down.astype(BF16), pm[...])
        rows = slice(xh * 36, xh * 36 + 36)
        for c in range(8):
            cols = slice(c * 72, c * 72 + 72)
            piece = down[:, cols]
            out[c * 2 + xh, :, lanes] = jnp.concatenate(
                [
                    o72[rows, cols],
                    sides[0][rows, c * 192 : c * 192 + 192],
                    sides[1][rows, c * 192 : c * 192 + 192],
                    piece[:36],
                    piece[36:72],
                    jnp.concatenate([piece[72:96], jnp.zeros((12, 72), F32)], 0),
                    jnp.zeros((36, 96), F32),
                ],
                1,
            ).astype(BF16)


def gather_first_kernel(b, pm, pf, out):
    gathered_b(b, pm, pf, out, slice(0, PACK_B))


def gather_second_kernel(c, pm, pf, out):
    gathered_b(c, pm, pf, out, slice(0, PACK_B))
    gathered_a(c[:, B_WIDTH:].astype(F32), out, slice(PACK_B, PACK))


def gather_last_kernel(a0, a1, a2, a3, a4, blocks, out):
    a = a0[...].astype(F32)
    for ref in (a1, a2, a3, a4):
        a = a + ref[...].astype(F32)
    out[:, :, PACK_A:] = blocks[...]
    gathered_a(a, out, slice(0, PACK_A))


def finish_kernel(first_ref, last_ref, vec, wq, wk, wv, wo, wg, wu, wd):
    diagonal = eye(36)

    def added(ref, low, high):
        total = ref[0, :, low:high].astype(F32)
        for i in range(1, 16):
            total = total + ref[i, :, low:high].astype(F32)
        return total

    totals = (
        added(last_ref, 0, PACK),
        jnp.concatenate([added(last_ref, PACK, PACK + PACK_A), added(first_ref, 0, PACK_B)], 1),
    )
    for layer, total in enumerate(totals):
        wq[:, layer, :] = total[:, PK_Q:PK_K]
        wk[layer] = total[:, PK_K:PK_V].T
        wv[layer] = total[:, PK_V:PK_GAIN].T
        wo[:, layer, :] = total[:, PK_O:PK_G]
        first = jnp.sum(diagonal * total[:, PK_GAIN : PK_GAIN + 1], 0, keepdims=True)
        second = jnp.sum(diagonal * total[:, PK_GAIN + 1 : PK_GAIN + 2], 0, keepdims=True)
        vec[layer : layer + 1, :] = jnp.concatenate([first, second], 1)
        wg[:, layer, :] = total[:, PK_G:PK_U]
        wu[:, layer, :] = total[:, PK_U:PK_D]
        wd[layer] = jnp.concatenate(
            [
                total[:, PK_D : PK_D + 72],
                total[:, PK_D + 72 : PK_D + 144],
                total[:24, PK_D + 144 : PK_D + 216],
            ],
            0,
        ).T


def keep_kernel(value, out):
    out[...] = value[...]


def swap_halves(tile):
    lane = lax.broadcasted_iota(jnp.int32, tile.shape, 1) % HEAD_DIM
    return jnp.where(
        lane < HEAD_DIM // 2,
        pltpu.roll(tile, 128 - HEAD_DIM // 2, 1),
        pltpu.roll(tile, HEAD_DIM // 2, 1),
    )


def place_rows(source):
    lane = lax.broadcasted_iota(jnp.int32, (192, 192), 1)
    return jnp.where(lane == source[...], 1.0, 0.0).astype(BF16)


def pre_kernel(first, source, a_in, x_ref, pm, pq, cosine, sine, a, normed_out, q_out, kv_out, gains_out, *x_out):
    a[...] = dot(place_rows(source), a_in[...]).astype(BF16)
    gains = dot_rows(a[:, 896:1024], pq[0:192, :])
    for p in range(1, 3):
        gains = gains + dot_rows(
            a[:, p * A_STEP + 896 : (p + 1) * A_STEP], pq[p * 192 : (p + 1) * 192, :]
        )
    gains = gains[64:72]
    gains_out[...] = gains
    if first:
        x = dot_rows(x_ref[:D, :], pm[...])
        x_out[0][...] = x
    else:
        x = x_ref[...]
    inverse = lax.rsqrt(jnp.mean(x * x, -1, keepdims=True) + norm_eps)
    normed = (x * inverse * gains[0:1]).astype(BF16)
    normed_out[...] = normed
    lin = dot(normed[:, :192], a[:, :A_STEP])
    for p in range(1, 3):
        lin = lin + dot(
            normed[:, p * 192 : (p + 1) * 192], a[:, p * A_STEP : (p + 1) * A_STEP]
        )
    turned = []
    for t in range(6):
        tile = lin[:, t * 128 : (t + 1) * 128]
        turned.append(tile * cosine[...] + swap_halves(tile) * sine[...])
    turned = jnp.concatenate(turned, 1)
    q_out[...] = (turned[:, :D] * score_scale).astype(BF16)
    for g in range(KV_HEADS):
        part = slice(g * HEAD_DIM, (g + 1) * HEAD_DIM)
        kv_out[:, g * PAIR : (g + 1) * PAIR] = jnp.concatenate(
            [turned[:, D:768][:, part], lin[:, 768:960][:, part]], 1
        ).astype(BF16)


def weight_back(left, b, main, tail, p):
    return dot_back(left[:, :512], b[:, main + p * 512 : main + (p + 1) * 512]) + dot_back(
        left[:, 512:], b[:, tail + p * 64 : tail + (p + 1) * 64]
    )


def fetch_b(b, held, sems):
    copies = []
    for i, (low, high) in enumerate(((0, B_DOWN), (B_DOWN, B_OUT), (B_OUT, B_WIDTH))):
        copies.append(
            pltpu.make_async_copy(b.at[:, low:high], held.at[:, low:high], sems.at[i])
        )
    return copies


def ffn_forward(o_ref, x_ref, gains, pm, b, copies, mid_out, op_out, nm_out, gate_low, up_low, hid_low):
    ffn, down, rest = copies
    op = dot(o_ref[...], pm[...]).astype(BF16)
    op_out[...] = op

    def through(left, main, tail, count):
        wide = None
        narrow = None
        for p in range(count):
            piece = left[:, p * 192 : (p + 1) * 192]
            one = dot(piece, b[:, main + p * 512 : main + (p + 1) * 512])
            two = dot(piece, b[:, tail + p * 64 : tail + (p + 1) * 64])
            wide = one if wide is None else wide + one
            narrow = two if narrow is None else narrow + two
        return jnp.concatenate([wide, narrow], 1)

    rest.wait()
    mid = x_ref[...] + through(op, B_OUT, B_OUT_TAIL, 3)
    mid_out[...] = mid
    inverse = lax.rsqrt(jnp.mean(mid * mid, -1, keepdims=True) + norm_eps)
    nm = (mid * inverse * gains[1:2, :]).astype(BF16)
    nm_out[...] = nm
    ffn.wait()
    for part in range(2):
        cols = slice(part * HALF_FF, (part + 1) * HALF_FF)
        gate, up = None, None
        for p in range(3):
            piece = nm[:, p * 192 : (p + 1) * 192]
            low = p * B_STEP + part * HALF_FF
            one = dot(piece, b[:, low : low + HALF_FF])
            two = dot(piece, b[:, low + FF : low + FF + HALF_FF])
            gate = one if gate is None else gate + one
            up = two if up is None else up + two
        gate_low[:, cols] = gate.astype(BF16)
        up_low[:, cols] = up.astype(BF16)
        hid_low[:, cols] = (gate / (1.0 + jnp.exp(-gate)) * up).astype(BF16)
    down.wait()
    return mid + through(hid_low, B_DOWN, B_DOWN_TAIL, 8)


def middle_kernel(o_ref, x_ref, gains, pm, cosine, sine, source, b_ref, a_late, pq_late, *refs):
    kept, (x_out, a, normed, q, kv, gains_out, b, a_in, pq), held = refs[:6], refs[6:15], refs[15:21]
    sems = refs[21]
    copies = fetch_b(b_ref, b, sems)
    for copy in copies[::-1]:
        copy.start()
    late = held_copies((a_late, pq_late), (a_in, pq), sems, 3)
    x_out[...] = ffn_forward(o_ref, x_ref, gains, pm, b, copies, *held)
    for copy in late:
        copy.wait()
    sent = held_copies(held, kept, sems, 5)
    pre_kernel(False, source, a_in, x_out, pm, pq, cosine, sine, a, normed, q, kv, gains_out)
    for copy in sent:
        copy.wait()


def norm_back(dy, v, gain):
    inverse = lax.rsqrt(jnp.mean(v * v, -1, keepdims=True) + norm_eps)
    scaled = dy * gain
    back = inverse * scaled - v * (
        inverse * inverse * inverse * jnp.mean(scaled * v, -1, keepdims=True)
    )
    return back, jnp.sum(dy * v * inverse, 0, keepdims=True)


class Sender:
    def __init__(self, db, db_out, sems):
        self.db, self.db_out, self.sems, self.sent = db, db_out, sems, []

    def send(self, low, high, source=None):
        source = self.db.at[:, low:high] if source is None else source
        self.sent.append(
            pltpu.make_async_copy(
                source, self.db_out.at[:, low:high], self.sems.at[3 + len(self.sent)]
            )
        )
        self.sent[-1].start()

    def wait(self):
        for copy in self.sent:
            copy.wait()


def ffn_backward(
    g,
    nm,
    gate_ref,
    up_ref,
    hid,
    mid,
    op,
    gains,
    pm,
    b,
    copies,
    sender,
    gm_out,
    do_out,
    dg_out,
    late=(),
):
    db = sender.db
    gb = g.astype(BF16)
    for p in range(8):
        piece = dot_rows(hid[:, p * 192 : (p + 1) * 192], gb)
        db[:, B_DOWN + p * 512 : B_DOWN + (p + 1) * 512] = piece[:, :512].astype(BF16)
        db[:, B_DOWN_TAIL + p * 64 : B_DOWN_TAIL + (p + 1) * 64] = piece[:, 512:].astype(BF16)
    sender.send(B_DOWN, B_OUT)
    for copy in copies[1:]:
        copy.wait()
    dh = jnp.concatenate([weight_back(gb, b, B_DOWN, B_DOWN_TAIL, p) for p in range(8)], 1)
    for copy in late[:3]:
        copy.wait()
    gate = gate_ref[...].astype(F32)
    up = up_ref[...].astype(F32)
    sig = 1.0 / (1.0 + jnp.exp(-gate))
    d_gate = (dh * up * sig * (1.0 + gate * (1.0 - sig))).astype(BF16)
    d_up = (dh * (gate * sig)).astype(BF16)
    for p in range(3):
        piece = nm[:, p * 192 : (p + 1) * 192]
        low = p * B_STEP
        db[:, low : low + FF] = dot_rows(piece, d_gate).astype(BF16)
        db[:, low + FF : low + B_STEP] = dot_rows(piece, d_up).astype(BF16)
        sender.send(low, low + B_STEP)
    for copy in copies[:1]:
        copy.wait()
    for copy in late[3:]:
        copy.wait()
    dnm = []
    for p in range(3):
        low = p * B_STEP
        dnm.append(
            dot_back(d_gate, b[:, low : low + FF])
            + dot_back(d_up, b[:, low + FF : low + B_STEP])
        )
    back, gain_grad = norm_back(jnp.concatenate(dnm, 1), mid[...], gains[1:2, :])
    dg_out[...] = gain_grad
    gm = g + back
    gm_out[...] = gm
    gmb = gm.astype(BF16)
    dop = []
    for p in range(3):
        piece = dot_rows(op[:, p * 192 : (p + 1) * 192], gmb)
        db[:, B_OUT + p * 512 : B_OUT + (p + 1) * 512] = piece[:, :512].astype(BF16)
        db[:, B_OUT_TAIL + p * 64 : B_OUT_TAIL + (p + 1) * 64] = piece[:, 512:].astype(BF16)
        dop.append(weight_back(gmb, b, B_OUT, B_OUT_TAIL, p))
    db[:, B_OUT_TAIL + 192 : B_WIDTH] = jnp.zeros((192, 64), BF16)
    sender.send(B_OUT, B_WIDTH)
    do_out[...] = dot_back(jnp.concatenate(dop, 1).astype(BF16), pm[...]).astype(BF16)
    sender.wait()


def held_copies(refs, held, sems, first):
    copies = [
        pltpu.make_async_copy(ref, target, sems.at[first + i])
        for i, (ref, target) in enumerate(zip(refs, held))
    ]
    for copy in copies:
        copy.start()
    return copies


def turn_kernel(o_ref, x_ref, gains, traded, pm, b_ref, *refs):
    x_out, db_out, gm_out, do_out, dg_out, b, db, mid, op, nm, gate, up, hid, sems = refs
    copies = fetch_b(b_ref, b, sems)
    for copy in copies[::-1]:
        copy.start()
    out = ffn_forward(o_ref, x_ref, gains, pm, b, copies, mid, op, nm, gate, up, hid)
    x_out[...] = dot_back(pm[...], out.astype(BF16)).astype(BF16)
    g = dot_rows(traded[D : 2 * D, :], pm[...])
    sender = Sender(db, db_out, sems)
    ffn_backward(
        g, nm, gate, up, hid, mid, op, gains, pm, b, (), sender, gm_out, do_out, dg_out
    )


def qkv_back_kernel(
    last, dq, kv0, kv1, kv2, kv3, kv4, cosine, sine, normed, gains, dg2, a_ref, x_late, gm_late, pq_late, *refs,
    started=None,
):
    if last:
        pm_ref, source, x_out, *da_refs, da, a, x_ref, gm, pq, pm, sems = refs
        late = held_copies((a_ref, x_late, gm_late, pq_late, pm_ref), (a, x_ref, gm, pq, pm), sems, 0)
    else:
        x_out, da, a, x_ref, gm, pq, sems = refs
        late = held_copies((a_ref, x_late, gm_late, pq_late), (a, x_ref, gm, pq), sems, 0)
        started()
    dkv = kv0[...].astype(F32)
    for ref in (kv1, kv2, kv3, kv4):
        dkv = dkv + ref[...].astype(F32)
    d_key = [dkv[:, g * PAIR : g * PAIR + HEAD_DIM] for g in range(KV_HEADS)]
    d_value = [dkv[:, g * PAIR + HEAD_DIM : (g + 1) * PAIR] for g in range(KV_HEADS)]
    rot = jnp.concatenate([dq[...]] + d_key, 1)
    turned = []
    for t in range(6):
        tile = rot[:, t * 128 : (t + 1) * 128]
        turned.append(tile * cosine[...] - swap_halves(tile) * sine[...])
    dqkv = jnp.concatenate(turned + d_value + [jnp.zeros((ROWS, 64), F32)], 1).astype(BF16)
    late[0].wait()
    dn = []
    for p in range(3):
        low = p * A_STEP
        da[:, low : low + A_STEP] = dot_rows(
            normed[:, p * 192 : (p + 1) * 192], dqkv
        ).astype(BF16)
        dn.append(dot_back(dqkv, a[:, low : low + A_STEP]))
    for copy in late[1:]:
        copy.wait()
    x = x_ref[...]
    back, dg1 = norm_back(jnp.concatenate(dn, 1), x, gains[0:1, :])
    rows = lax.broadcasted_iota(jnp.int32, (64, D), 0)
    stacked = jnp.where(rows == 0, dg1, jnp.where(rows == 1, dg2[...], 0.0)).astype(BF16)
    placed = dot_back(pq[...], stacked).astype(BF16)
    for p in range(3):
        da[:, p * A_STEP + 960 : (p + 1) * A_STEP] = placed[p * 192 : (p + 1) * 192]
    out = gm[...] + back
    if last:
        x_out[...] = dot_back(pm[...], out.astype(BF16)).astype(BF16)
        placed = dot_rows(place_rows(source), da[...])
        for i, ref in enumerate(da_refs):
            ref[...] = placed[i * 24 : (i + 1) * 24].astype(BF16)
    else:
        x_out[...] = out


def back_kernel(*args):
    qkv_args, (gains, hid, gate, up, nm, mid, op, pm, b_ref), refs = args[:15], args[15:24], args[24:]
    db_out, gm_out, do_out, dg_out, grad, da, a, x, gm, pq, *held, b, db, qkv_sems, sems = refs
    copies = fetch_b(b_ref, b, sems)
    late = []

    def started():
        late.extend(held_copies((hid,), held[:1], sems, 9))
        copies[2].start()
        copies[1].start()
        late.extend(held_copies((gate, up, nm), held[1:4], sems, 10))
        copies[0].start()
        late.extend(held_copies((mid, op, pm), held[4:], sems, 13))

    qkv_back_kernel(False, *qkv_args, grad, da, a, x, gm, pq, qkv_sems, started=started)
    sender = Sender(db, db_out, sems)
    sender.send(B_WIDTH, C_WIDTH, da)
    late[0].wait()
    hid, gate, up, nm, mid, op, pm = held
    ffn_backward(
        grad[...], nm, gate, up, hid, mid, op, gains, pm, b,
        copies, sender, gm_out, do_out, dg_out, late[1:],
    )


PAIR = 2 * HEAD_DIM
WIDE = GROUP * BLOCK
CHUNK = 256
STEPS = KEYS // CHUNK + 1
SLOTS = 2 * KV_HEADS


def load_heads(ref, scratch, run, upper):
    zero = jnp.zeros((WIDE, HEAD_DIM), BF16)
    for g in range(KV_HEADS):
        heads = jnp.concatenate(
            [
                ref[
                    run * BLOCK : (run + 1) * BLOCK,
                    (g * GROUP + h) * HEAD_DIM : (g * GROUP + h + 1) * HEAD_DIM,
                ]
                for h in range(GROUP)
            ],
            0,
        )
        both = [zero, heads] if upper else [heads, zero]
        scratch[run * KV_HEADS + g] = jnp.concatenate(both, 1)


def sort_keys(table, pieces, kvs):
    for j in range(KEYS // BLOCK):
        start = pl.multiple_of(table[2 + j] * BLOCK, BLOCK)
        kvs[pl.ds(start, BLOCK), :] = pieces[j // 2][(j % 2) * BLOCK : (j % 2 + 1) * BLOCK, :]


def set_lead(lead):
    key = lax.broadcasted_iota(jnp.int32, (CHUNK, BLOCK), 0)
    row = lax.broadcasted_iota(jnp.int32, (CHUNK, BLOCK), 1)
    lead[...] = row - key


def head_columns(h):
    return slice(h * BLOCK, (h + 1) * BLOCK)


def step_of(table, it):
    first = (table[0] + 2) // 2
    second = it >= first
    run = jnp.where(second, 1, 0)
    chunk = jnp.where(second, it - first, it)
    block = jnp.where(second, table[1], table[0])
    return run, pl.multiple_of(chunk * CHUNK, CHUNK), chunk * CHUNK - block * BLOCK


def attend_kernel(table, q_ref, *refs):
    pieces, (o_out, lse_out, kvs, qs, lead, ms, ls, acc) = refs[:8], refs[8:]
    sort_keys(table, pieces, kvs)
    load_heads(q_ref, qs, 0, False)
    load_heads(q_ref, qs, 1, False)
    set_lead(lead)
    ms[...] = jnp.full(ms.shape, masked_score, F32)
    ls[...] = jnp.zeros(ls.shape, F32)
    acc[...] = jnp.zeros(acc.shape, F32)

    def step(it, carry):
        run, start, least = step_of(table, it)
        results = []
        for g in range(KV_HEADS):
            at = run * KV_HEADS + g
            kv = kvs[pl.ds(start, CHUNK), g * PAIR : (g + 1) * PAIR]
            turned = kv.T
            for h in range(GROUP):
                part = head_columns(h)
                scores = dot_back(kv, qs[at, part, :])
                scores = jnp.where(lead[...] >= least, scores, masked_score)
                before = ms[at, :, part]
                now = jnp.maximum(before, jnp.max(scores, 0, keepdims=True))
                raised = jnp.exp(scores - now)
                shrink = jnp.exp(before - now)
                total = ls[at, :, part] * shrink + jnp.sum(raised, 0, keepdims=True)
                out = dot(turned, raised.astype(BF16))[HEAD_DIM:]
                results.append((at, part, now, total, acc[at, :, part] * shrink + out))
        for at, part, now, total, out in results:
            ms[at, :, part] = now
            ls[at, :, part] = total
            acc[at, :, part] = out
        return carry

    lax.fori_loop(0, STEPS, step, 0, unroll=STEPS)
    for run in range(2):
        for g in range(KV_HEADS):
            at = run * KV_HEADS + g
            total = ls[at]
            lse_out[at] = ms[at] + jnp.log(total)
            heads = (acc[at] / total).T
            for h in range(GROUP):
                o_out[
                    run * BLOCK : (run + 1) * BLOCK,
                    (g * GROUP + h) * HEAD_DIM : (g * GROUP + h + 1) * HEAD_DIM,
                ] = heads[h * BLOCK : (h + 1) * BLOCK].astype(BF16)


def attend_back_kernel(table, q_ref, o_ref, do_ref, lse, *refs):
    pieces = refs[:8]
    dq_out, outs, (kvs, qs, dos, lead, deltas, dkvs, dqs) = refs[8], refs[9:17], refs[17:]
    sort_keys(table, pieces, kvs)
    set_lead(lead)
    for run in range(2):
        load_heads(q_ref, qs, run, False)
        load_heads(do_ref, dos, run, True)
        rows = slice(run * BLOCK, (run + 1) * BLOCK)
        product = o_ref[rows, :].astype(F32) * do_ref[rows, :].astype(F32)
        turned = jnp.concatenate([product, jnp.zeros((BLOCK, HEAD_DIM), F32)], 1).T
        for g in range(KV_HEADS):
            deltas[run * KV_HEADS + g] = jnp.concatenate(
                [
                    jnp.sum(turned[h * HEAD_DIM : (h + 1) * HEAD_DIM], 0, keepdims=True)
                    for h in range(g * GROUP, (g + 1) * GROUP)
                ],
                1,
            )
    dkvs[...] = jnp.zeros(dkvs.shape, F32)
    dqs[...] = jnp.zeros(dqs.shape, F32)

    def step(it, carry):
        run, start, least = step_of(table, it)
        scores, d_probs, low_probs, d_scores, results = [], [], [], [], []
        for g in range(KV_HEADS):
            at = run * KV_HEADS + g
            kv = kvs[pl.ds(start, CHUNK), g * PAIR : (g + 1) * PAIR]
            scores.append(dot_back(kv, qs[at]))
            d_probs.append(dot_back(kv, dos[at]))
        ahead = jnp.concatenate([lead[...]] * GROUP, 1) >= least
        for g in range(KV_HEADS):
            at = run * KV_HEADS + g
            probs = jnp.exp(jnp.where(ahead, scores[g], masked_score) - lse[at])
            low_probs.append(probs.astype(BF16))
            d_scores.append((probs * (d_probs[g] - deltas[at])).astype(BF16))
        for g in range(KV_HEADS):
            at = run * KV_HEADS + g
            kv = kvs[pl.ds(start, CHUNK), g * PAIR : (g + 1) * PAIR]
            d_kv = dot(d_scores[g], qs[at]) + dot(low_probs[g], dos[at])
            results.append((at, d_kv, dot_rows(kv, d_scores[g])[:HEAD_DIM]))
        for g, (at, d_kv, d_q) in enumerate(results):
            dkvs[g, pl.ds(start, CHUNK), :] += d_kv
            dqs[at] += d_q
        return carry

    lax.fori_loop(0, STEPS, step, 0, unroll=STEPS)
    for run in range(2):
        for g in range(KV_HEADS):
            heads = (dqs[run * KV_HEADS + g] * score_scale).T
            for h in range(GROUP):
                dq_out[
                    run * BLOCK : (run + 1) * BLOCK,
                    (g * GROUP + h) * HEAD_DIM : (g * GROUP + h + 1) * HEAD_DIM,
                ] = heads[h * BLOCK : (h + 1) * BLOCK]
    for j in range(KEYS // BLOCK):
        start = pl.multiple_of(table[2 + j] * BLOCK, BLOCK)
        rows = slice((j % 2) * BLOCK, (j % 2 + 1) * BLOCK)
        for g in range(KV_HEADS):
            outs[j // 2][rows, g * PAIR : (g + 1) * PAIR] = dkvs[
                g, pl.ds(start, BLOCK), :
            ].astype(BF16)


def attend(table, q, kv_all):
    return call(
        attend_kernel,
        [sds((ROWS, D), BF16), sds((SLOTS, 1, WIDE), F32)],
        10,
        6.9,
        grant=16,
        smem=(0,),
        scratch=[
            pltpu.VMEM((KEYS, KV_HEADS * PAIR), BF16),
            pltpu.VMEM((SLOTS, WIDE, PAIR), BF16),
            pltpu.VMEM((CHUNK, BLOCK), jnp.int32),
            pltpu.VMEM((SLOTS, 1, WIDE), F32),
            pltpu.VMEM((SLOTS, 1, WIDE), F32),
            pltpu.VMEM((SLOTS, HEAD_DIM, WIDE), F32),
        ],
    )(table, q, *kv_all)


def attend_back(table, q, kv_all, o, do, lse):
    return call(
        attend_back_kernel,
        [sds((ROWS, D), F32)] + [sds((ROWS, 2 * KVD), BF16)] * 8,
        13,
        11.3,
        smem=(0,),
        scratch=[
            pltpu.VMEM((KEYS, KV_HEADS * PAIR), BF16),
            pltpu.VMEM((SLOTS, WIDE, PAIR), BF16),
            pltpu.VMEM((SLOTS, WIDE, PAIR), BF16),
            pltpu.VMEM((CHUNK, BLOCK), jnp.int32),
            pltpu.VMEM((SLOTS, 1, WIDE), F32),
            pltpu.VMEM((KV_HEADS, KEYS, PAIR), F32),
            pltpu.VMEM((SLOTS, HEAD_DIM, WIDE), F32),
        ],
    )(table, q, o, do, lse, *kv_all)


def ring(shift):
    return [(i, (i + shift) % 4) for i in range(4)]


def ring_x(shift):
    pairs = []
    for x in range(4):
        to = (x + shift) % 4
        pairs.append(((x % 2) * 2 + x // 2, (to % 2) * 2 + to // 2))
    return pairs


SHIFTS = (1, -1, 2)


def from_x(value):
    return [value] + [lax.ppermute(value, ("xl", "xh"), ring_x(s)) for s in SHIFTS]


def from_ring(value, axis):
    return [value] + [lax.ppermute(value, axis, ring(s)) for s in SHIFTS]


def other_core(value):
    return lax.ppermute(value, "core", [(0, 1), (1, 0)])


def trade(value):
    return lax.ppermute(value, ("xl", "core"), [(0, 0), (1, 2), (2, 1), (3, 3)])


def place_of(distance):
    distance = distance % 4
    return distance ^ (distance >> 1)


def block_index():
    z, xl, xh = (lax.axis_index(name) for name in OUTER)
    block = jnp.arange(16, dtype=jnp.int32)
    along_x = place_of(xh * 2 + xl - (block % 2) * 2 - (block // 2) % 2)
    along_z = place_of(z - block // 4)
    return along_z * 4 + along_x, along_x * 4 + along_z


def row_source():
    y, core = lax.axis_index("y"), lax.axis_index("core")
    rows = jnp.arange(192, dtype=jnp.int32)
    owner, j = rows // 24, rows % 24
    piece = ((owner + core) % 2) * 4 + place_of(y - owner // 2)
    return (piece * 24 + j)[:, None]


def spread_a(index, blocks):
    return call(
        spread_a_kernel,
        sds((24, 2 * A_WIDTH), BF16),
        5,
        3.0,
        smem=(0,),
        scratch=[pltpu.VMEM((16, 36, 2 * PACK_A), BF16)],
        grant=16,
    )(index, *blocks)


def spread_b(first, index, blocks, pm, pf):
    return call(
        functools.partial(spread_b_kernel, first),
        sds((24, B_WIDTH), BF16),
        7,
        4.3,
        smem=(0,),
        scratch=[pltpu.VMEM((16, 36, PACK_B), BF16)],
        grant=16,
    )(index, *blocks, pm, pf)


def share(near):
    return near + [other_core(piece) for piece in near]


def return_pieces(near, far, axis):
    far = [other_core(piece) for piece in far]
    both = [(n.astype(F32) + f.astype(F32)).astype(BF16) for n, f in zip(near[1:], far[1:])]
    back = [lax.ppermute(piece, axis, ring(-s)) for piece, s in zip(both, SHIFTS)]
    return [near[0], far[0]] + back


def key_table(starts):
    z, core = lax.axis_index("z"), lax.axis_index("core")
    j = np.arange(18) - 2
    shift = np.where(j < 0, 0, np.array((0,) + SHIFTS)[(j // 2) % 4]).astype(np.int32)
    far = np.where(j < 0, 0, j // 8).astype(np.int32)
    wanted = (((z - shift) % 4) * 2 + (core + far) % 2) * 2 + (j % 2).astype(np.int32)
    match = wanted[:, None] == jnp.arange(16, dtype=jnp.int32)[None, :]
    return jnp.sum(jnp.where(match, starts[None, :], 0), 1)


def angles(places):
    half_dim = HEAD_DIM // 2
    inverse = rope_base ** (-2.0 * jnp.arange(half_dim).astype(F32) / HEAD_DIM)
    turned = places.astype(F32)[:, None] * inverse[None, :]
    cosine, sine = jnp.cos(turned), jnp.sin(turned)
    return jnp.concatenate([cosine] * 4, 1), jnp.concatenate([-sine, sine] * 2, 1)


def after(value, *others):
    return lax.optimization_barrier((value, *others))[0]


def on_device(
    tokens, positions, vectors, w_query, w_key, w_value, w_out, w_gate, w_up, w_down, cotangent
):
    pm = jnp.asarray(one_hot(feature_order()), BF16)
    pf = jnp.asarray(one_hot(hidden_order()), BF16)
    pq = jnp.asarray(gain_matrix(), BF16)
    index, z_index = block_index()
    source = row_source()
    layer_second = (1, 0, 2)
    turned = (0, 2, 1)
    pack, later = call(
        pack_kernel, [sds((36, PACK_FIRST), BF16), sds((36, PACK_B), BF16)], 8, 1.9
    )(
        vectors,
        w_query.transpose(layer_second),
        w_key.transpose(turned),
        w_value.transpose(turned),
        w_out.transpose(layer_second),
        w_gate.transpose(layer_second),
        w_up.transpose(layer_second),
        w_down.transpose(turned),
    )
    later = jnp.stack(from_ring(later, "z"))
    blocks = from_ring(after(jnp.stack(from_x(pack)), later), "z")
    a_near = spread_a(index, blocks)
    near = from_ring(a_near, "y")
    later = from_x(after(later, a_near))
    both = share(near)
    a_near, a1_near = (
        jnp.concatenate([piece[:, low : low + A_WIDTH] for piece in both], 0)
        for low in (0, A_WIDTH)
    )
    blocks = [after(blocks[0], *near[1:])] + blocks[1:]
    b0 = lax.all_gather(
        spread_b(2 * PACK_A, index, blocks, pm, pf), INNER, axis=0, tiled=True
    )

    starts = jnp.broadcast_to((positions[0, ::BLOCK] // BLOCK).astype(BF16)[:, None], (16, ROWS))
    traded = jnp.concatenate([tokens[0].T, cotangent[0].T, starts], 0)
    traded = trade(after(traded, blocks[3]))
    table = key_table(traded[2 * D :, 0].astype(jnp.int32))
    places = (table[:2, None] * BLOCK + jnp.arange(BLOCK)[None, :]).reshape(ROWS)
    cosine, sine = angles(places)
    x = traded

    pre_shapes = [
        sds((192, A_WIDTH), BF16),
        sds((ROWS, D), BF16),
        sds((ROWS, D), BF16),
        sds((ROWS, 2 * KVD), BF16),
        sds((8, D), F32),
    ]
    a, normed, q, kv, gains, x = call(
        functools.partial(pre_kernel, True), pre_shapes + [sds((ROWS, D), F32)], 7, 5.0, grant=16
    )(source, a_near, traded, pm, pq, cosine, sine)
    near = from_ring(kv, "z")
    later = [after(later[0], *near[1:])] + later[1:]
    b1 = lax.all_gather(spread_b(0, z_index, later, pm, pf), INNER, axis=0, tiled=True)
    kv_all = share(near)
    o, lse = attend(table, q, kv_all)
    first_layer = (x, a, normed, q, kv_all, gains, o, lse)

    *kept, x, a, normed, q, kv, gains = call(
        middle_kernel,
        [
            sds((ROWS, D), F32),
            sds((ROWS, D), BF16),
            sds((ROWS, D), BF16),
            sds((ROWS, FF), BF16),
            sds((ROWS, FF), BF16),
            sds((ROWS, FF), BF16),
            sds((ROWS, D), F32),
        ]
        + pre_shapes,
        10,
        10.0,
        left=(7, 8, 9),
        left_out=range(6),
        scratch=[
            pltpu.VMEM((192, B_WIDTH), BF16),
            pltpu.VMEM((192, A_WIDTH), BF16),
            pltpu.VMEM((D, D), BF16),
            pltpu.VMEM((ROWS, D), F32),
            pltpu.VMEM((ROWS, D), BF16),
            pltpu.VMEM((ROWS, D), BF16),
            pltpu.VMEM((ROWS, FF), BF16),
            pltpu.VMEM((ROWS, FF), BF16),
            pltpu.VMEM((ROWS, FF), BF16),
            pltpu.SemaphoreType.DMA((11,)),
        ],
    )(o, x, gains, pm, cosine, sine, source, b0, a1_near, pq)
    kv_all = share(from_ring(kv, "z"))
    o, lse = attend(table, q, kv_all)

    back_shapes = [sds((ROWS, D), F32), sds((ROWS, D), BF16), sds((1, D), F32)]
    back_scratch = [pltpu.VMEM((192, B_WIDTH), BF16)] * 2
    ffn_scratch = [
        pltpu.VMEM((ROWS, FF), BF16),
        pltpu.VMEM((ROWS, FF), BF16),
        pltpu.VMEM((ROWS, FF), BF16),
        pltpu.VMEM((ROWS, D), BF16),
        pltpu.VMEM((ROWS, D), F32),
        pltpu.VMEM((ROWS, D), BF16),
    ]
    output, db, gm, do, dg2 = call(
        turn_kernel,
        [sds((D, ROWS), BF16), sds((192, B_WIDTH), BF16)] + back_shapes,
        6,
        17.0,
        left=(5,),
        left_out=(1,),
        scratch=back_scratch
        + [
            pltpu.VMEM((ROWS, D), F32),
            pltpu.VMEM((ROWS, D), BF16),
            pltpu.VMEM((ROWS, D), BF16),
            pltpu.VMEM((ROWS, FF), BF16),
            pltpu.VMEM((ROWS, FF), BF16),
            pltpu.VMEM((ROWS, FF), BF16),
            pltpu.SemaphoreType.DMA((8,)),
        ],
    )(o, x, gains, traded, pm, b1)
    output = trade(output)
    first = lax.psum_scatter(db, INNER, scatter_dimension=0, tiled=True)
    dq, *pieces = attend_back(table, q, kv_all, o, do, lse)
    parts = return_pieces(pieces[:4], pieces[4:], "z")
    parts[0] = after(parts[0], output)
    held = [
        pltpu.VMEM((192, A_WIDTH), BF16),
        pltpu.VMEM((ROWS, D), F32),
        pltpu.VMEM((ROWS, D), F32),
        pltpu.VMEM((D, D), BF16),
    ]
    second_layer = (dq, *parts, cosine, sine, normed, gains, dg2, a, x, gm, pq)

    x, a, normed, q, kv_all, gains, o, lse = first_layer
    mid, op, nm, gate, up, hid = kept
    db, gm, do, dg2 = call(
        back_kernel,
        [sds((192, C_WIDTH), BF16)] + back_shapes,
        24,
        16.0,
        left=(*range(11, 15), *range(16, 24)),
        left_out=(0,),
        scratch=[pltpu.VMEM((ROWS, D), F32), pltpu.VMEM((192, A_WIDTH), BF16)]
        + held
        + ffn_scratch
        + [pltpu.VMEM((D, D), BF16)]
        + back_scratch
        + [pltpu.SemaphoreType.DMA((4,)), pltpu.SemaphoreType.DMA((16,))],
    )(*second_layer, gains, hid, gate, up, nm, mid, op, pm, b0)
    summed = lax.psum_scatter(db, INNER, scatter_dimension=0, tiled=True)
    dq, *pieces = attend_back(table, q, kv_all, o, do, lse)
    parts = return_pieces(pieces[:4], pieces[4:], "z")
    first = call(gather_first_kernel, sds((16, 36, PACK_B), BF16), 3, 5.0, grant=16)(
        after(first, parts[1]), pm, pf
    )
    parts[0] = after(parts[0], first)
    grad, *pieces = call(
        functools.partial(qkv_back_kernel, True),
        [sds((D, ROWS), BF16)] + [sds((24, A_WIDTH), BF16)] * 8,
        17,
        6.4,
        grant=20,
        left=range(11, 16),
        scratch=[pltpu.VMEM((192, A_WIDTH), BF16)]
        + held
        + [pltpu.VMEM((D, D), BF16), pltpu.SemaphoreType.DMA((5,))],
    )(dq, *parts, cosine, sine, normed, gains, dg2, a, x, gm, pq, pm, source)
    parts = return_pieces(pieces[:4], pieces[4:], "y")
    first = lax.all_to_all(first, OUTER, 0, 0, tiled=True)
    grad = trade(grad)
    blocks = call(gather_second_kernel, sds((16, 36, PACK), BF16), 3, 5.0, grant=16)(summed, pm, pf)
    blocks = call(gather_last_kernel, sds((16, 36, PACK + PACK_A), BF16), 6, 2.5, grant=16)(
        *parts, blocks
    )
    rest = lax.all_to_all(after(blocks, grad), OUTER, 0, 0, tiled=True)
    outs = call(
        finish_kernel,
        [
            sds((2, 72), F32),
            sds((36, 2, 72), F32),
            sds((2, 24, 36), F32),
            sds((2, 24, 36), F32),
            sds((36, 2, 72), F32),
            sds((36, 2, 192), F32),
            sds((36, 2, 192), F32),
            sds((2, 72, 96), F32),
        ],
        2,
        2.9,
        grant=16,
    )(first, rest)
    order = (None, layer_second, turned, turned, layer_second, layer_second, layer_second, turned)
    outs = [out if axes is None else out.transpose(axes) for out, axes in zip(outs, order)]
    output = call(keep_kernel, sds((D, ROWS), BF16), 1, 1.0)(output)
    return (output.T[None], grad.astype(F32).T[None], *outs)


def solution(mesh):
    fine = Mesh(np.asarray(mesh.devices).reshape(SIZES), AXES)
    split = P(None, FSDP, CTX)
    rows = P(FSDP, CTX, None)
    return jax.shard_map(
        on_device,
        mesh=fine,
        in_specs=(rows, P(FSDP, None), P(None, FSDP)) + (split,) * 7 + (rows,),
        out_specs=(rows, rows, P(None, FSDP)) + (split,) * 7,
        check_vma=False,
    )
```
